32 devices in a mesh: seq: 8 (over z, x), batch: 4 (over y, core).
Axes of the slice: x: 2, y: 2, z: 4, core: 2. Of those that a mesh axis runs over, the one named last changes fastest.
Arguments:
- queries: bfloat16 [4, 1024, 1024], P('batch', 'seq'), may hold values from -6 to 6
- keys: bfloat16 [4, 1024, 1024], P('batch', 'seq'), may hold values from -6 to 6
- values: bfloat16 [4, 1024, 1024], P('batch', 'seq'), may hold values from -6 to 6
- gates: bfloat16 [4, 1024, 1024], P('batch', 'seq'), may hold values from -6 to 6
- out_grad: bfloat16 [4, 1024, 1024], P('batch', 'seq'), may hold values from -6 to 6
- w_out: bfloat16 [1024, 1024], replicated, may hold values from -0.1875 to 0.1875
- hist_lengths: int32 [4, 4], P('batch'), may hold values from 1 to 682, 1024 in all within a row
Outputs:
- output: bfloat16 [4, 1024, 1024], P('batch', 'seq')
- grad_queries: bfloat16 [4, 1024, 1024], P('batch', 'seq')
- grad_keys: bfloat16 [4, 1024, 1024], P('batch', 'seq')
- grad_values: bfloat16 [4, 1024, 1024], P('batch', 'seq')
- grad_gates: bfloat16 [4, 1024, 1024], P('batch', 'seq')
- grad_weight: float32 [1024, 1024], P('batch')
The draws below stay inside these ranges and needn't reach their ends.
Inputs may be any that keep to these rules, and one draw needn't show every extreme that they name: `hist_lengths`: each group's 4 lengths sum to 1024, and the longest of each group is exactly 682.
All inputs are finite; a program needn't handle non-finite values.
Results may differ from the reference program's by a relative error of at most 0.0058.
Values may be sent and summed in bfloat16 or wider, within the bound.
No kernel may reach another device: no remote copies, remote signals or barrier semaphores. Data moves between devices by JAX's collectives and lax.ppermute only.
A program may use at most 64 MiB of HBM per device.

```python
import math
import jax
import jax.numpy as jnp
import numpy as np
from jax import lax

HEADS = 8
HEAD_DIM = 128
D = 1024
WINDOW = 256
TOK_DEV = 128
REACH = 2
SEQS = 4
TOKENS = 1024
HIST_MAX = 682
GROUPS = 4


def steps_of(key, dims, split, smallest, largest):
    factor_of = 1.0
    for axis_at, blocks in split:
        draws = jax.random.uniform(jax.random.fold_in(jax.random.fold_in(key, 6), axis_at), (blocks,), jnp.float32, smallest / len(split), largest / len(split))
        factor_of = factor_of * jnp.repeat(jnp.exp(draws), dims[axis_at] // blocks).reshape((-1,) + (1,) * (len(dims) - 1 - axis_at))
    return factor_of


def length_profile(count, total, reach, lean):
    portions = [(1 << 20) // math.isqrt(standing ** lean) + 1 for standing in range(2, count + 1)]
    rest, counts = total - reach - (count - 1), [1] * (count - 1)
    while rest > 0:
        free = [i for i in range(count - 1) if counts[i] < reach]
        pool, left = sum([portions[i] for i in free]), rest
        for i in free:
            extra = min(reach - counts[i], max(1, left * portions[i] // pool), rest)
            counts[i] = counts[i] + extra
            rest = rest - extra
    return np.array([reach] + counts)


def uneven(stream_key, count, total, reach, skew):
    if count == 2:
        one = jax.random.randint(stream_key, (), max(1, total - reach), min(reach, total - 1) + 1)
        return jnp.stack([one, total - one])
    tallies = jnp.asarray(length_profile(count, total, reach, skew), jnp.int32)
    pairs = (count - 1) // 2
    donor, sink = tallies[1:1 + 2 * pairs:2], tallies[2:2 + 2 * pairs:2]
    slack = jnp.minimum(donor - 1, reach - sink)
    passed = jax.random.randint(jax.random.fold_in(stream_key, 1), (pairs,), 0, 1 << 20) % (slack + 1)
    tallies = tallies.at[1:1 + 2 * pairs:2].set(donor - passed).at[2:2 + 2 * pairs:2].set(sink + passed)
    return tallies[jax.random.permutation(jax.random.fold_in(stream_key, 2), count)]


def noise(stream_key, shape, deviation, reach, cuts=(), kind=jnp.bfloat16):
    factor_of = steps_of(stream_key, shape, cuts, -0.22, 0.18) if cuts else 1.0
    result = jax.random.normal(stream_key, shape, jnp.float32) * deviation * factor_of
    return jnp.minimum(jnp.maximum(result, -reach), reach).astype(kind)


def setup_inputs(seed: int = 0) -> dict:
    arg_keys = jax.random.split(jax.random.key(seed), 8)
    queries = noise(arg_keys[0], (GROUPS, TOKENS, D), 1.0, 6.0, ((0, 4), (1, 8)))
    keys = noise(arg_keys[1], (GROUPS, TOKENS, D), 1.0, 6.0, ((0, 4), (1, 8)))
    values = noise(arg_keys[2], (GROUPS, TOKENS, D), 1.0, 6.0, ((0, 4), (1, 8)))
    gates = noise(arg_keys[3], (GROUPS, TOKENS, D), 1.0, 6.0, ((0, 4), (1, 8)))
    out_grad = noise(arg_keys[4], (GROUPS, TOKENS, D), 1.0, 6.0, ((0, 4), (1, 8)))
    w_out = noise(arg_keys[5], (D, D), D ** -0.5, 0.1875)
    hist_lengths = jax.vmap(lambda own: uneven(own, SEQS, TOKENS, HIST_MAX, 2))(jax.random.split(arg_keys[6], GROUPS)).reshape((GROUPS, SEQS)).astype(jnp.int32)
    return dict(queries=queries, keys=keys, values=values, gates=gates, out_grad=out_grad, w_out=w_out, hist_lengths=hist_lengths)


def segment_start(positions, lengths):
    seg_ends = jnp.cumsum(lengths).astype(jnp.int32)
    seg_begins = (seg_ends - lengths).astype(jnp.int32)
    inside = (seg_begins[None, :] <= positions[:, None]) & (positions[:, None] < seg_ends[None, :])
    return lax.optimization_barrier(jnp.sum(jnp.where(inside, seg_begins[None, :], 0), axis=1)).astype(jnp.int32)

def silu_slope(scores):
    logistic = jax.nn.sigmoid(scores)
    return logistic * (1.0 + scores * (1.0 - logistic))

def causal_mask(query_pos, query_start, key_pos):
    inside = (key_pos[None, :] >= query_start[:, None]) & (key_pos[None, :] <= query_pos[:, None])
    return inside & (key_pos[None, :] > query_pos[:, None] - WINDOW)

def one_group(query_rows, key_rows, value_rows, gate_rows, grad_rows, w_out, lengths):
    block_rows = TOK_DEV
    span_rows = (REACH + 1) * TOK_DEV
    block_count = TOKENS // TOK_DEV
    score_scale = HEAD_DIM ** (-0.5)
    positions = jnp.arange(TOKENS + REACH * block_rows, dtype=jnp.int32)
    starts = segment_start(positions, lengths)
    zero_rows = jnp.zeros((REACH * block_rows, D), jnp.bfloat16)
    key_front = jnp.concatenate([zero_rows, key_rows], axis=0)
    value_front = jnp.concatenate([zero_rows, value_rows], axis=0)
    indices = jnp.arange(block_count, dtype=jnp.int32)

    def query_side(first):
        query_blk = lax.dynamic_slice_in_dim(query_rows, first, block_rows, 0).astype(jnp.float32).reshape(block_rows, HEADS, HEAD_DIM)
        key_win = lax.dynamic_slice_in_dim(key_front, first, span_rows, 0).astype(jnp.float32).reshape(span_rows, HEADS, HEAD_DIM)
        value_win = lax.dynamic_slice_in_dim(value_front, first, span_rows, 0).astype(jnp.float32).reshape(span_rows, HEADS, HEAD_DIM)
        query_pos = first + jnp.arange(block_rows, dtype=jnp.int32)
        key_pos = first - REACH * block_rows + jnp.arange(span_rows, dtype=jnp.int32)
        query_start = lax.dynamic_slice_in_dim(starts, first, block_rows, 0)
        scores = jnp.einsum('ihe,jhe->hij', query_blk, key_win) * score_scale
        allowed = causal_mask(query_pos, query_start, key_pos)[None]
        return (scores, allowed, key_win, value_win)

    def forward_block(index):
        first = index * block_rows
        scores, allowed, key_win, value_win = query_side(first)
        attention = jnp.where(allowed, jax.nn.silu(scores), 0.0).astype(jnp.bfloat16)
        return jnp.einsum('hij,jhe->ihe', attention.astype(jnp.float32), value_win).reshape(block_rows, D)
    mixed = lax.map(forward_block, indices).reshape(TOKENS, D)
    centered = mixed - lax.optimization_barrier(jnp.mean(mixed, axis=1, keepdims=True))
    inv_std = lax.rsqrt(lax.optimization_barrier(jnp.mean(centered * centered, axis=1, keepdims=True)) + 1e-05)
    normed = centered * inv_std
    hidden = (normed * gate_rows.astype(jnp.float32)).astype(jnp.bfloat16)
    output = jnp.dot(hidden, w_out, preferred_element_type=jnp.float32).astype(jnp.bfloat16)
    grad_hidden = jnp.dot(grad_rows, w_out.T, preferred_element_type=jnp.float32)
    grad_gates = (grad_hidden * normed).astype(jnp.bfloat16)
    grad_norm = grad_hidden * gate_rows.astype(jnp.float32)
    grad_mix = ((grad_norm - lax.optimization_barrier(jnp.mean(grad_norm, axis=1, keepdims=True)) - normed * lax.optimization_barrier(jnp.mean(grad_norm * normed, axis=1, keepdims=True))) * inv_std).astype(jnp.bfloat16)

    def query_grad_block(index):
        first = index * block_rows
        scores, allowed, key_win, value_win = query_side(first)
        mix_blk = lax.dynamic_slice_in_dim(grad_mix, first, block_rows, 0).astype(jnp.float32).reshape(block_rows, HEADS, HEAD_DIM)
        grad_attention = jnp.einsum('ihe,jhe->hij', mix_blk, value_win)
        grad_scores = jnp.where(allowed, grad_attention * silu_slope(scores) * score_scale, 0.0).astype(jnp.bfloat16)
        return jnp.einsum('hij,jhe->ihe', grad_scores.astype(jnp.float32), key_win).reshape(block_rows, D)
    grad_queries = lax.map(query_grad_block, indices).reshape(TOKENS, D).astype(jnp.bfloat16)
    query_back = jnp.concatenate([query_rows, zero_rows], axis=0)
    mix_back = jnp.concatenate([grad_mix, zero_rows], axis=0)

    def key_grad_block(index):
        first = index * block_rows
        key_blk = lax.dynamic_slice_in_dim(key_rows, first, block_rows, 0).astype(jnp.float32).reshape(block_rows, HEADS, HEAD_DIM)
        value_blk = lax.dynamic_slice_in_dim(value_rows, first, block_rows, 0).astype(jnp.float32).reshape(block_rows, HEADS, HEAD_DIM)
        query_win = lax.dynamic_slice_in_dim(query_back, first, span_rows, 0).astype(jnp.float32).reshape(span_rows, HEADS, HEAD_DIM)
        mix_win = lax.dynamic_slice_in_dim(mix_back, first, span_rows, 0).astype(jnp.float32).reshape(span_rows, HEADS, HEAD_DIM)
        query_pos = first + jnp.arange(span_rows, dtype=jnp.int32)
        query_start = lax.dynamic_slice_in_dim(starts, first, span_rows, 0)
        key_pos = first + jnp.arange(block_rows, dtype=jnp.int32)
        scores = jnp.einsum('ihe,jhe->hij', query_win, key_blk) * score_scale
        allowed = causal_mask(query_pos, query_start, key_pos)[None]
        attention = jnp.where(allowed, jax.nn.silu(scores), 0.0).astype(jnp.bfloat16)
        grad_attention = jnp.einsum('ihe,jhe->hij', mix_win, value_blk)
        grad_scores = jnp.where(allowed, grad_attention * silu_slope(scores) * score_scale, 0.0).astype(jnp.bfloat16)
        grad_key_blk = jnp.einsum('hij,ihe->jhe', grad_scores.astype(jnp.float32), query_win).reshape(block_rows, D)
        grad_value_blk = jnp.einsum('hij,ihe->jhe', attention.astype(jnp.float32), mix_win).reshape(block_rows, D)
        return (grad_key_blk, grad_value_blk)
    grad_key_all, grad_value_all = lax.map(key_grad_block, indices)
    grad_keys = grad_key_all.reshape(TOKENS, D).astype(jnp.bfloat16)
    grad_values = grad_value_all.reshape(TOKENS, D).astype(jnp.bfloat16)
    weight_term = lax.dot_general(hidden, grad_rows, (((0,), (0,)), ((), ())), preferred_element_type=jnp.float32)
    return (output, grad_queries, grad_keys, grad_values, grad_gates, weight_term)

def reference(queries, keys, values, gates, out_grad, w_out, hist_lengths):
    results = []
    weight_total = jnp.zeros((D, D), jnp.float32)
    for group in range(GROUPS):
        outcome = one_group(queries[group], keys[group], values[group], gates[group], out_grad[group], w_out, hist_lengths[group])
        results.append(outcome[:5])
        weight_total = weight_total + outcome[5]
    stacked = [jnp.stack([item[place] for item in results]) for place in range(5)]
    grad_weight = weight_total * (GROUPS * TOKENS) ** (-0.5)
    return (stacked[0], stacked[1], stacked[2], stacked[3], stacked[4], grad_weight)
```

```python
import functools

import jax
import jax.numpy as jnp
from jax import lax
from jax.experimental import pallas as pl
from jax.experimental.pallas import tpu as pltpu
from jax.sharding import PartitionSpec as P

HEADS = 8
WINDOW = 256
REACH = 2

VMEM = pl.BlockSpec(memory_space=pltpu.VMEM)
SMEM = pl.BlockSpec(memory_space=pltpu.SMEM)
F32 = jnp.float32
BF16 = jnp.bfloat16
NT = (((1,), (1,)), ((), ()))
TN = (((0,), (0,)), ((), ()))


def dot(a, b):
    return jnp.dot(a, b, preferred_element_type=F32)


def dot_nt(a, b):
    return lax.dot_general(a, b, NT, preferred_element_type=F32)


def dot_tn(a, b):
    return lax.dot_general(a, b, TN, preferred_element_type=F32)


def logistic(scores):
    return 0.5 * jnp.tanh(0.5 * scores) + 0.5


def silu_slope(scores, gate):
    return gate * (1.0 + scores * (1.0 - gate))


def start_of(positions, len_ref):
    total = jnp.zeros_like(positions)
    end = jnp.int32(0)
    for k in range(len_ref.shape[1]):
        length = len_ref[0, k]
        end = end + length
        total = total + jnp.where(positions >= end, length, 0)
    return total


def allowed_block(rows, first_query, first_key, len_ref, query_dim):
    shape = (rows, rows)
    query_pos = first_query + lax.broadcasted_iota(jnp.int32, shape, query_dim)
    key_pos = first_key + lax.broadcasted_iota(jnp.int32, shape, 1 - query_dim)
    start = start_of(query_pos, len_ref)
    return (key_pos >= start) & (key_pos <= query_pos) & (key_pos > query_pos - WINDOW)


def head_slice(h, width):
    return slice(h * width, (h + 1) * width)


def cost(flops, arrays):
    total = sum(a.size * a.dtype.itemsize for a in arrays)
    return pl.CostEstimate(flops=flops, bytes_accessed=total, transcendentals=0)


def call(kernel, outs, scalars, arrays, flops, scratch=()):
    return pl.pallas_call(
        kernel,
        out_shape=outs,
        in_specs=[SMEM] * len(scalars) + [VMEM] * len(arrays),
        out_specs=[VMEM] * len(outs),
        scratch_shapes=list(scratch),
        cost_estimate=cost(flops, list(arrays) + list(outs)),
        compiler_params=pltpu.CompilerParams(vmem_limit_bytes=40 * 1024 * 1024),
    )(*scalars, *arrays)


def own_kernel(len_ref, place_ref, q, k, v, grad, w, mixed_own, grad_hidden):
    rows, width = q.shape
    size = width // HEADS
    scale = size ** (-0.5)
    first = place_ref[0] * rows
    grad_hidden[...] = dot_nt(grad[...], w[...])
    allowed = allowed_block(rows, first, first, len_ref, 0)
    for h in range(HEADS):
        cols = head_slice(h, size)
        scores = dot_nt(q[:, cols], k[:, cols]) * scale
        attention = jnp.where(allowed, scores * logistic(scores), 0.0).astype(BF16)
        mixed_own[:, cols] = dot(attention, v[:, cols])


def forward_kernel(
    groups, len_ref, place_ref, q, k1, k2, v1, v2, mixed_own, grad_hidden, gates, *rest
):
    hidden, grad_gates, grad_mix = rest[:3]
    slices = rest[3 : 3 + groups]
    mixed = rest[3 + groups]
    rows, width = q.shape
    size = width // HEADS
    scale = size ** (-0.5)
    first = place_ref[0] * rows
    masks = [allowed_block(rows, first, first - d * rows, len_ref, 0) for d in (1, 2)]
    for h in range(HEADS):
        cols = head_slice(h, size)
        total = mixed_own[:, cols]
        for mask, kd, vd in zip(masks, (k1, k2), (v1, v2)):
            scores = dot_nt(q[:, cols], kd[:, cols]) * scale
            attention = jnp.where(mask, scores * logistic(scores), 0.0).astype(BF16)
            total = total + dot(attention, vd[:, cols])
        mixed[:, cols] = total
    values = mixed[...]
    centered = values - jnp.mean(values, axis=1, keepdims=True)
    inv_std = lax.rsqrt(jnp.mean(centered * centered, axis=1, keepdims=True) + 1e-05)
    normed = centered * inv_std
    gate = gates[...].astype(F32)
    hidden[...] = (normed * gate).astype(BF16)
    gh = grad_hidden[...]
    grad_gates[...] = (gh * normed).astype(BF16)
    grad_norm = gh * gate
    grad_mix[...] = (
        (
            grad_norm
            - jnp.mean(grad_norm, axis=1, keepdims=True)
            - normed * jnp.mean(grad_norm * normed, axis=1, keepdims=True)
        )
        * inv_std
    ).astype(BF16)
    part = width // groups
    for d, ref in enumerate(slices):
        at = pl.multiple_of((place_ref[1] ^ d) * part, 128)
        ref[...] = hidden[:, pl.ds(at, part)]


def query_kernel(len_ref, place_ref, q, k0, k1, k2, v0, v1, v2, grad_mix, hidden, w, output, grad_queries):
    rows, width = q.shape
    size = width // HEADS
    scale = size ** (-0.5)
    first = place_ref[0] * rows
    output[...] = dot(hidden[...], w[...]).astype(BF16)
    masks = [allowed_block(rows, first, first - d * rows, len_ref, 0) for d in range(REACH + 1)]
    for h in range(HEADS):
        cols = head_slice(h, size)
        total = jnp.zeros((rows, size), F32)
        for mask, kd, vd in zip(masks, (k0, k1, k2), (v0, v1, v2)):
            scores = dot_nt(q[:, cols], kd[:, cols]) * scale
            grad_attention = dot_nt(grad_mix[:, cols], vd[:, cols])
            slope = silu_slope(scores, logistic(scores))
            grad_scores = jnp.where(mask, grad_attention * slope * scale, 0.0).astype(BF16)
            total = total + dot(grad_scores, kd[:, cols])
        grad_queries[:, cols] = total.astype(BF16)


def key_kernel(len_ref, place_ref, k, v, q0, q1, q2, g0, g1, g2, grad_keys, grad_values):
    rows, width = k.shape
    size = width // HEADS
    scale = size ** (-0.5)
    first = place_ref[0] * rows
    masks = [allowed_block(rows, first + d * rows, first, len_ref, 1) for d in range(REACH + 1)]
    for h in range(HEADS):
        cols = head_slice(h, size)
        keys_total = jnp.zeros((rows, size), F32)
        values_total = jnp.zeros((rows, size), F32)
        for mask, qd, gd in zip(masks, (q0, q1, q2), (g0, g1, g2)):
            scores = dot_nt(k[:, cols], qd[:, cols]) * scale
            gate = logistic(scores)
            attention = jnp.where(mask, scores * gate, 0.0).astype(BF16)
            grad_attention = dot_nt(v[:, cols], gd[:, cols])
            slope = silu_slope(scores, gate)
            grad_scores = jnp.where(mask, grad_attention * slope * scale, 0.0).astype(BF16)
            keys_total = keys_total + dot(grad_scores, qd[:, cols])
            values_total = values_total + dot(attention, gd[:, cols])
        grad_keys[:, cols] = keys_total.astype(BF16)
        grad_values[:, cols] = values_total.astype(BF16)


def weight_kernel(groups, place_ref, *refs):
    hidden = refs[:groups]
    grads = refs[groups : 2 * groups]
    own = refs[2 * groups]
    sends = refs[2 * groups + 1 : -1]
    total = refs[-1]
    acc = dot_tn(hidden[0][...], grads[0][...])
    for a, b in zip(hidden[1:], grads[1:]):
        acc = acc + dot_tn(a[...], b[...])
    total[...] = acc
    rows = own.shape[0]
    if not sends:
        own[...] = acc
        return
    own[...] = total[pl.ds(pl.multiple_of(place_ref[0] * rows, rows), rows), :]
    for e, ref in enumerate(sends):
        at = pl.multiple_of((place_ref[0] ^ (e + 1)) * rows, rows)
        ref[...] = total[pl.ds(at, rows), :].astype(BF16)


def sum_kernel(scale, own, *refs):
    total = own[...]
    for ref in refs[:-1]:
        total = total + ref[...].astype(F32)
    refs[-1][...] = (total * scale).astype(BF16)


def place_kernel(place_ref, *refs):
    out = refs[-1]
    rows = refs[0].shape[0]
    for e, ref in enumerate(refs[:-1]):
        at = pl.multiple_of((place_ref[0] ^ e) * rows, rows)
        out[pl.ds(at, rows), :] = ref[...].astype(F32)


def xor_route(size, mask):
    return [(i, i ^ mask) for i in range(size)]


def halo(block, distance, even):
    count = lax.axis_size("seq")
    route = [(i, i + distance) for i in range(count) if 0 <= i + distance < count]
    far = lax.ppermute(block, "seq", route)
    keeps = even if distance > 0 else jnp.logical_not(even)
    passed = jnp.where(keeps, block, far)
    near = lax.ppermute(passed, "seq", xor_route(count, 1))
    return near, far


def on_device(queries, keys, values, gates, out_grad, w_out, hist_lengths):
    q, k, v, gate, grad = queries[0], keys[0], values[0], gates[0], out_grad[0]
    rows, width = q.shape
    seq = lax.axis_size("seq")
    batch = lax.axis_size("batch")
    seq_at = lax.axis_index("seq")
    batch_at = lax.axis_index("batch")
    place = jnp.stack([seq_at, batch_at]).astype(jnp.int32)
    scalars = (hist_lengths, place)
    even = (seq_at & 1) == 0
    full = jax.ShapeDtypeStruct((rows, width), BF16)
    wide = jax.ShapeDtypeStruct((rows, width), F32)
    block_flops = 2 * rows * rows * width
    proj_flops = 2 * rows * width * width

    k1, k2 = halo(k, 2, even)
    v1, v2 = halo(v, 2, even)
    q1, q2 = halo(q, -2, even)
    grads = [grad] + [lax.ppermute(grad, "batch", xor_route(batch, d)) for d in range(1, batch)]

    mixed_own, grad_hidden = call(
        own_kernel, [wide, wide], scalars, (q, k, v, grad, w_out), proj_flops + 2 * block_flops
    )
    part = width // batch
    piece = jax.ShapeDtypeStruct((rows, part), BF16)
    hidden, grad_gates, grad_mix, *slices = call(
        functools.partial(forward_kernel, batch),
        [full, full, full] + [piece] * batch,
        scalars,
        (q, k1, k2, v1, v2, mixed_own, grad_hidden, gate),
        4 * block_flops,
        [pltpu.VMEM((rows, width), F32)],
    )
    hiddens = [slices[0]] + [
        lax.ppermute(slices[d], "batch", xor_route(batch, d)) for d in range(1, batch)
    ]
    g1, g2 = halo(grad_mix, -2, even)

    direct = seq == 8
    rows_w = part // seq if direct else part
    own_shape = jax.ShapeDtypeStruct((rows_w, width), F32)
    send_shape = jax.ShapeDtypeStruct((rows_w, width), BF16)
    scale = (rows * seq * batch) ** (-0.5)
    own, *sends = call(
        functools.partial(weight_kernel, batch),
        [own_shape] + ([send_shape] * (seq - 1) if direct else []),
        (place,),
        (*hiddens, *grads),
        proj_flops,
        [pltpu.VMEM((part, width), F32)],
    )
    if direct:
        got = [lax.ppermute(s, "seq", xor_route(seq, e + 1)) for e, s in enumerate(sends)]
        (mine,) = call(functools.partial(sum_kernel, scale), [send_shape], (), (own, *got), own.size * 8)
        shares = [mine] + [lax.ppermute(mine, "seq", xor_route(seq, e)) for e in range(1, seq)]
        (grad_weight,) = call(
            place_kernel,
            [jax.ShapeDtypeStruct((part, width), F32)],
            (place,),
            tuple(shares),
            part * width,
        )
    else:
        grad_weight = lax.psum(own, "seq") * scale

    output, grad_queries = call(
        query_kernel,
        [full, full],
        scalars,
        (q, k, k1, k2, v, v1, v2, grad_mix, hidden, w_out),
        proj_flops + 9 * block_flops,
    )
    grad_keys, grad_values = call(
        key_kernel, [full, full], scalars, (k, v, q, q1, q2, grad_mix, g1, g2), 12 * block_flops
    )
    return (
        output[None],
        grad_queries[None],
        grad_keys[None],
        grad_values[None],
        grad_gates[None],
        grad_weight,
    )


def solution(mesh):
    token = P("batch", "seq", None)
    return jax.shard_map(
        on_device,
        mesh=mesh,
        in_specs=(token, token, token, token, token, P(), P("batch", None)),
        out_specs=(token, token, token, token, token, P("batch", None)),
        check_vma=False,
    )
```

```python
import functools

import jax
import jax.numpy as jnp
from jax import lax
from jax.experimental import pallas as pl
from jax.experimental.pallas import tpu as pltpu
from jax.sharding import PartitionSpec as P

HEADS = 8
WINDOW = 256
REACH = 2

VMEM = pl.BlockSpec(memory_space=pltpu.VMEM)
SMEM = pl.BlockSpec(memory_space=pltpu.SMEM)
F32 = jnp.float32
BF16 = jnp.bfloat16
NT = (((1,), (1,)), ((), ()))
TN = (((0,), (0,)), ((), ()))


def dot(a, b):
    return jnp.dot(a, b, preferred_element_type=F32)


def dot_nt(a, b):
    return lax.dot_general(a, b, NT, preferred_element_type=F32)


def dot_tn(a, b):
    return lax.dot_general(a, b, TN, preferred_element_type=F32)


def logistic(scores):
    return 0.5 * jnp.tanh(0.5 * scores) + 0.5


def silu_slope(scores, gate):
    return gate * (1.0 + scores * (1.0 - gate))


def start_of(positions, len_ref):
    total = jnp.zeros_like(positions)
    end = jnp.int32(0)
    for k in range(len_ref.shape[1]):
        length = len_ref[0, k]
        end = end + length
        total = total + jnp.where(positions >= end, length, 0)
    return total


def allowed_block(rows, first_query, first_key, len_ref, query_dim):
    shape = (rows, rows)
    query_pos = first_query + lax.broadcasted_iota(jnp.int32, shape, query_dim)
    key_pos = first_key + lax.broadcasted_iota(jnp.int32, shape, 1 - query_dim)
    start = start_of(query_pos, len_ref)
    return (key_pos >= start) & (key_pos <= query_pos) & (key_pos > query_pos - WINDOW)


def head_slice(h, width):
    return slice(h * width, (h + 1) * width)


def cost(flops, arrays):
    total = sum(a.size * a.dtype.itemsize for a in arrays)
    return pl.CostEstimate(flops=flops, bytes_accessed=total, transcendentals=0)


def call(kernel, outs, scalars, arrays, flops, scratch=()):
    return pl.pallas_call(
        kernel,
        out_shape=outs,
        in_specs=[SMEM] * len(scalars) + [VMEM] * len(arrays),
        out_specs=[VMEM] * len(outs),
        scratch_shapes=list(scratch),
        cost_estimate=cost(flops, list(arrays) + list(outs)),
        compiler_params=pltpu.CompilerParams(vmem_limit_bytes=40 * 1024 * 1024),
    )(*scalars, *arrays)


def own_kernel(len_ref, place_ref, q, k, v, grad, w, mixed_own, grad_hidden):
    rows, width = q.shape
    size = width // HEADS
    scale = size ** (-0.5)
    first = place_ref[0] * rows
    grad_hidden[...] = dot_nt(grad[...], w[...])
    allowed = allowed_block(rows, first, first, len_ref, 0)
    for h in range(HEADS):
        cols = head_slice(h, size)
        scores = dot_nt(q[:, cols], k[:, cols]) * scale
        attention = jnp.where(allowed, scores * logistic(scores), 0.0).astype(BF16)
        mixed_own[:, cols] = dot(attention, v[:, cols])


def forward_kernel(
    groups, len_ref, place_ref, q, k1, k2, v1, v2, mixed_own, grad_hidden, gates, *rest
):
    hidden, grad_gates, grad_mix = rest[:3]
    slices, mixed = rest[3:]
    rows, width = q.shape
    size = width // HEADS
    scale = size ** (-0.5)
    first = place_ref[0] * rows
    masks = [allowed_block(rows, first, first - d * rows, len_ref, 0) for d in (1, 2)]
    for h in range(HEADS):
        cols = head_slice(h, size)
        total = mixed_own[:, cols]
        for mask, kd, vd in zip(masks, (k1, k2), (v1, v2)):
            scores = dot_nt(q[:, cols], kd[:, cols]) * scale
            attention = jnp.where(mask, scores * logistic(scores), 0.0).astype(BF16)
            total = total + dot(attention, vd[:, cols])
        mixed[:, cols] = total
    values = mixed[...]
    centered = values - jnp.mean(values, axis=1, keepdims=True)
    inv_std = lax.rsqrt(jnp.mean(centered * centered, axis=1, keepdims=True) + 1e-05)
    normed = centered * inv_std
    gate = gates[...].astype(F32)
    hidden[...] = (normed * gate).astype(BF16)
    gh = grad_hidden[...]
    grad_gates[...] = (gh * normed).astype(BF16)
    grad_norm = gh * gate
    grad_mix[...] = (
        (
            grad_norm
            - jnp.mean(grad_norm, axis=1, keepdims=True)
            - normed * jnp.mean(grad_norm * normed, axis=1, keepdims=True)
        )
        * inv_std
    ).astype(BF16)
    part = width // groups
    for d in range(groups):
        slices[d * rows : (d + 1) * rows, :] = hidden[:, d * part : (d + 1) * part]


def query_kernel(len_ref, place_ref, q, k0, k1, k2, v0, v1, v2, grad_mix, hidden, w, output, grad_queries):
    rows, width = q.shape
    size = width // HEADS
    scale = size ** (-0.5)
    first = place_ref[0] * rows
    output[...] = dot(hidden[...], w[...]).astype(BF16)
    masks = [allowed_block(rows, first, first - d * rows, len_ref, 0) for d in range(REACH + 1)]
    for h in range(HEADS):
        cols = head_slice(h, size)
        total = jnp.zeros((rows, size), F32)
        for mask, kd, vd in zip(masks, (k0, k1, k2), (v0, v1, v2)):
            scores = dot_nt(q[:, cols], kd[:, cols]) * scale
            grad_attention = dot_nt(grad_mix[:, cols], vd[:, cols])
            slope = silu_slope(scores, logistic(scores))
            grad_scores = jnp.where(mask, grad_attention * slope * scale, 0.0).astype(BF16)
            total = total + dot(grad_scores, kd[:, cols])
        grad_queries[:, cols] = total.astype(BF16)


def key_kernel(len_ref, place_ref, k, v, q0, q1, q2, g0, g1, g2, grad_keys, grad_values):
    rows, width = k.shape
    size = width // HEADS
    scale = size ** (-0.5)
    first = place_ref[0] * rows
    masks = [allowed_block(rows, first + d * rows, first, len_ref, 1) for d in range(REACH + 1)]
    for h in range(HEADS):
        cols = head_slice(h, size)
        keys_total = jnp.zeros((rows, size), F32)
        values_total = jnp.zeros((rows, size), F32)
        for mask, qd, gd in zip(masks, (q0, q1, q2), (g0, g1, g2)):
            scores = dot_nt(k[:, cols], qd[:, cols]) * scale
            gate = logistic(scores)
            attention = jnp.where(mask, scores * gate, 0.0).astype(BF16)
            grad_attention = dot_nt(v[:, cols], gd[:, cols])
            slope = silu_slope(scores, gate)
            grad_scores = jnp.where(mask, grad_attention * slope * scale, 0.0).astype(BF16)
            keys_total = keys_total + dot(grad_scores, qd[:, cols])
            values_total = values_total + dot(attention, gd[:, cols])
        grad_keys[:, cols] = keys_total.astype(BF16)
        grad_values[:, cols] = values_total.astype(BF16)


def weight_kernel(place_ref, hidden, *refs):
    grads, total = refs[:-1], refs[-1]
    rows = grads[0].shape[0]
    acc = jnp.zeros(total.shape, F32)
    for d, grad in enumerate(grads):
        at = pl.multiple_of((place_ref[1] ^ d) * rows, rows)
        acc = acc + dot_tn(hidden[pl.ds(at, rows), :], grad[...])
    total[...] = acc.astype(total.dtype)


def sum_kernel(count, scale, parts, out):
    rows = parts.shape[0] // count
    total = parts[:rows, :].astype(F32)
    for e in range(1, parts.shape[0] // rows):
        total = total + parts[e * rows : (e + 1) * rows, :].astype(F32)
    piece = (total * scale).astype(BF16)
    for e in range(parts.shape[0] // rows):
        out[e * rows : (e + 1) * rows, :] = piece


def widen_kernel(parts, out):
    out[...] = parts[...].astype(F32)


def xor_route(size, mask):
    return [(i, i ^ mask) for i in range(size)]


def halo(block, distance, even):
    count = lax.axis_size("seq")
    route = [(i, i + distance) for i in range(count) if 0 <= i + distance < count]
    far = lax.ppermute(block, "seq", route)
    keeps = even if distance > 0 else jnp.logical_not(even)
    passed = jnp.where(keeps, block, far)
    near = lax.ppermute(passed, "seq", xor_route(count, 1))
    return near, far


def on_device(queries, keys, values, gates, out_grad, w_out, hist_lengths):
    q, k, v, gate, grad = queries[0], keys[0], values[0], gates[0], out_grad[0]
    rows, width = q.shape
    seq = lax.axis_size("seq")
    batch = lax.axis_size("batch")
    seq_at = lax.axis_index("seq")
    batch_at = lax.axis_index("batch")
    place = jnp.stack([seq_at, batch_at]).astype(jnp.int32)
    scalars = (hist_lengths, place)
    even = (seq_at & 1) == 0
    full = jax.ShapeDtypeStruct((rows, width), BF16)
    wide = jax.ShapeDtypeStruct((rows, width), F32)
    block_flops = 2 * rows * rows * width
    proj_flops = 2 * rows * width * width

    k1, k2 = halo(k, 2, even)
    v1, v2 = halo(v, 2, even)
    q1, q2 = halo(q, -2, even)
    grads = [grad] + [lax.ppermute(grad, "batch", xor_route(batch, d)) for d in range(1, batch)]

    mixed_own, grad_hidden = call(
        own_kernel, [wide, wide], scalars, (q, k, v, grad, w_out), proj_flops + 2 * block_flops
    )
    part = width // batch
    hidden, grad_gates, grad_mix, slices = call(
        functools.partial(forward_kernel, batch),
        [full, full, full, jax.ShapeDtypeStruct((batch * rows, part), BF16)],
        scalars,
        (q, k1, k2, v1, v2, mixed_own, grad_hidden, gate),
        4 * block_flops,
        [pltpu.VMEM((rows, width), F32)],
    )
    gathered = lax.all_to_all(slices, "batch", 0, 0, tiled=True)
    g1, g2 = halo(grad_mix, -2, even)

    direct = part % (16 * seq) == 0
    scale = (rows * seq * batch) ** (-0.5)
    narrow = jax.ShapeDtypeStruct((part, width), BF16)
    result = jax.ShapeDtypeStruct((part, width), F32)
    (total,) = call(weight_kernel, [narrow if direct else result], (place,), (gathered, *grads), proj_flops)
    if direct:
        parts = lax.all_to_all(total, "seq", 0, 0, tiled=True)
        (mine,) = call(functools.partial(sum_kernel, seq, scale), [narrow], (), (parts,), part * width)
        shares = lax.all_to_all(mine, "seq", 0, 0, tiled=True)
        (grad_weight,) = call(widen_kernel, [result], (), (shares,), part * width)
    else:
        grad_weight = lax.psum(total, "seq") * scale

    output, grad_queries = call(
        query_kernel,
        [full, full],
        scalars,
        (q, k, k1, k2, v, v1, v2, grad_mix, hidden, w_out),
        proj_flops + 9 * block_flops,
    )
    grad_keys, grad_values = call(
        key_kernel, [full, full], scalars, (k, v, q, q1, q2, grad_mix, g1, g2), 12 * block_flops
    )
    return (
        output[None],
        grad_queries[None],
        grad_keys[None],
        grad_values[None],
        grad_gates[None],
        grad_weight,
    )


def solution(mesh):
    token = P("batch", "seq", None)
    return jax.shard_map(
        on_device,
        mesh=mesh,
        in_specs=(token, token, token, token, token, P(), P("batch", None)),
        out_specs=(token, token, token, token, token, P("batch", None)),
        check_vma=False,
    )
```

```python
import functools

import jax
import jax.numpy as jnp
from jax import lax
from jax.experimental import pallas as pl
from jax.experimental.pallas import tpu as pltpu
from jax.sharding import PartitionSpec as P

HEADS = 8
WINDOW = 256
REACH = 2

VMEM = pl.BlockSpec(memory_space=pltpu.VMEM)
SMEM = pl.BlockSpec(memory_space=pltpu.SMEM)
F32 = jnp.float32
BF16 = jnp.bfloat16
NT = (((1,), (1,)), ((), ()))
TN = (((0,), (0,)), ((), ()))


def dot(a, b):
    return jnp.dot(a, b, preferred_element_type=F32)


def dot_nt(a, b):
    return lax.dot_general(a, b, NT, preferred_element_type=F32)


def dot_tn(a, b):
    return lax.dot_general(a, b, TN, preferred_element_type=F32)


def logistic(scores):
    return 0.5 * jnp.tanh(0.5 * scores) + 0.5


def silu_slope(scores, gate):
    return gate * (1.0 + scores * (1.0 - gate))


def start_of(positions, len_ref):
    total = jnp.zeros_like(positions)
    end = jnp.int32(0)
    for k in range(len_ref.shape[1]):
        length = len_ref[0, k]
        end = end + length
        total = total + jnp.where(positions >= end, length, 0)
    return total


def allowed_block(rows, first_query, first_key, len_ref, query_dim):
    shape = (rows, rows)
    query_pos = first_query + lax.broadcasted_iota(jnp.int32, shape, query_dim)
    key_pos = first_key + lax.broadcasted_iota(jnp.int32, shape, 1 - query_dim)
    start = start_of(query_pos, len_ref)
    return (key_pos >= start) & (key_pos <= query_pos) & (key_pos > query_pos - WINDOW)


def head_slice(h, width):
    return slice(h * width, (h + 1) * width)


def cost(flops, arrays):
    total = sum(a.size * a.dtype.itemsize for a in arrays)
    return pl.CostEstimate(flops=flops, bytes_accessed=total, transcendentals=0)


def call(kernel, outs, scalars, arrays, flops, scratch=(), spaces=None):
    spaces = spaces or [VMEM] * len(arrays)
    return pl.pallas_call(
        kernel,
        out_shape=outs,
        in_specs=[SMEM] * len(scalars) + spaces,
        out_specs=[VMEM] * len(outs),
        scratch_shapes=list(scratch),
        cost_estimate=cost(flops, list(arrays) + list(outs)),
        compiler_params=pltpu.CompilerParams(vmem_limit_bytes=40 * 1024 * 1024),
    )(*scalars, *arrays)


def own_kernel(
    len_ref, place_ref, q_in, k_in, v_in, grad_in, w_in, q, k, v, grad, w, mixed, grad_hidden, slope, sems
):
    moves = [
        pltpu.make_async_copy(src, dst, sems.at[i])
        for i, (src, dst) in enumerate(
            ((q_in, q), (k_in, k), (v_in, v), (grad_in, grad), (w_in, w))
        )
    ]
    for move in moves:
        move.start()
    rows, width = q.shape
    size = width // HEADS
    scale = size ** (-0.5)
    first = place_ref[0] * rows
    allowed = allowed_block(rows, first, first, len_ref, 0)
    for move in moves[:3]:
        move.wait()
    for h in range(HEADS):
        cols = head_slice(h, size)
        scores = dot_nt(q[:, cols], k[:, cols]) * scale
        gate = logistic(scores)
        attention = jnp.where(allowed, scores * gate, 0.0).astype(BF16)
        slope[:, cols] = jnp.where(allowed, silu_slope(scores, gate) * scale, 0.0)
        mixed[:, cols] = dot(attention, v[:, cols])
    for move in moves[3:]:
        move.wait()
    grad_hidden[...] = dot_nt(grad[...], w[...])


def far_kernel(len_ref, place_ref, q, k1, k2, attention1, attention2, slope1, slope2):
    rows, width = q.shape
    size = width // HEADS
    scale = size ** (-0.5)
    first = place_ref[0] * rows
    parts = ((k1, attention1, slope1), (k2, attention2, slope2))
    for d, (keys, attention, slope) in enumerate(parts):
        allowed = allowed_block(rows, first, first - (d + 1) * rows, len_ref, 0)
        for h in range(HEADS):
            cols = head_slice(h, size)
            scores = dot_nt(q[:, cols], keys[:, cols]) * scale
            gate = logistic(scores)
            attention[:, cols] = jnp.where(allowed, scores * gate, 0.0).astype(BF16)
            slope[:, cols] = jnp.where(allowed, silu_slope(scores, gate) * scale, 0.0)


def forward_kernel(
    groups, place_ref, attention1, attention2, v1, v2, mixed_own, grad_hidden, gates, *rest
):
    hidden, grad_gates, grad_mix = rest[:3]
    slices = rest[3 : 3 + groups]
    mixed = rest[3 + groups]
    rows, width = v1.shape
    size = width // HEADS
    for h in range(HEADS):
        cols = head_slice(h, size)
        mixed[:, cols] = (
            mixed_own[:, cols]
            + dot(attention1[:, cols], v1[:, cols])
            + dot(attention2[:, cols], v2[:, cols])
        )
    values = mixed[...]
    centered = values - jnp.mean(values, axis=1, keepdims=True)
    inv_std = lax.rsqrt(jnp.mean(centered * centered, axis=1, keepdims=True) + 1e-05)
    normed = centered * inv_std
    gate = gates[...].astype(F32)
    hidden[...] = (normed * gate).astype(BF16)
    part = width // groups
    for d, ref in enumerate(slices):
        at = pl.multiple_of((place_ref[1] ^ d) * part, 128)
        ref[...] = hidden[:, pl.ds(at, part)]
    gh = grad_hidden[...]
    grad_gates[...] = (gh * normed).astype(BF16)
    grad_norm = gh * gate
    grad_mix[...] = (
        (
            grad_norm
            - jnp.mean(grad_norm, axis=1, keepdims=True)
            - normed * jnp.mean(grad_norm * normed, axis=1, keepdims=True)
        )
        * inv_std
    ).astype(BF16)


def query_kernel(k0, k1, k2, v0, v1, v2, slope0, slope1, slope2, grad_mix, hidden, w, output, grad_queries):
    rows, width = k0.shape
    size = width // HEADS
    output[...] = dot(hidden[...], w[...]).astype(BF16)
    parts = ((k0, v0, slope0), (k1, v1, slope1), (k2, v2, slope2))
    for h in range(HEADS):
        cols = head_slice(h, size)
        total = jnp.zeros((rows, size), F32)
        for keys, vals, slope in parts:
            grad_attention = dot_nt(grad_mix[:, cols], vals[:, cols])
            grad_scores = (grad_attention * slope[:, cols]).astype(BF16)
            total = total + dot(grad_scores, keys[:, cols])
        grad_queries[:, cols] = total.astype(BF16)


def key_kernel(len_ref, place_ref, k, v, q0, q1, q2, g0, g1, g2, grad_keys, grad_values):
    rows, width = k.shape
    size = width // HEADS
    scale = size ** (-0.5)
    first = place_ref[0] * rows
    masks = [allowed_block(rows, first + d * rows, first, len_ref, 1) for d in range(REACH + 1)]
    for h in range(HEADS):
        cols = head_slice(h, size)
        keys_total = jnp.zeros((rows, size), F32)
        values_total = jnp.zeros((rows, size), F32)
        for mask, qd, gd in zip(masks, (q0, q1, q2), (g0, g1, g2)):
            scores = dot_nt(k[:, cols], qd[:, cols]) * scale
            gate = logistic(scores)
            attention = jnp.where(mask, scores * gate, 0.0).astype(BF16)
            grad_attention = dot_nt(v[:, cols], gd[:, cols])
            slope = jnp.where(mask, silu_slope(scores, gate) * scale, 0.0)
            grad_scores = (grad_attention * slope).astype(BF16)
            keys_total = keys_total + dot(grad_scores, qd[:, cols])
            values_total = values_total + dot(attention, gd[:, cols])
        grad_keys[:, cols] = keys_total.astype(BF16)
        grad_values[:, cols] = values_total.astype(BF16)


def weight_kernel(groups, place_ref, *refs):
    hidden = jnp.concatenate([ref[...] for ref in refs[:groups]], axis=0)
    grads = jnp.concatenate([ref[...] for ref in refs[groups : 2 * groups]], axis=0)
    own = refs[2 * groups]
    sends = refs[2 * groups + 1 : -1]
    total = refs[-1]
    total[...] = dot_tn(hidden, grads)
    if not sends:
        own[...] = total[...]
        return
    rows = own.shape[0]
    corner = place_ref[0] & len(sends)
    own[...] = total[pl.ds(pl.multiple_of(corner * rows, rows), rows), :]
    for e, ref in enumerate(sends):
        at = pl.multiple_of((corner ^ (e + 1)) * rows, rows)
        ref[...] = total[pl.ds(at, rows), :].astype(BF16)


def corner_kernel(corners, place_ref, own, *refs):
    got, (keep, send, total) = refs[:-3], refs[-3:]
    acc = own[...]
    for ref in got:
        acc = acc + ref[...].astype(F32)
    total[...] = acc
    rows = keep.shape[0]
    side = place_ref[0] // corners
    keep[...] = total[pl.ds(pl.multiple_of(side * rows, rows), rows), :]
    send[...] = total[pl.ds(pl.multiple_of((1 - side) * rows, rows), rows), :].astype(BF16)


def piece_kernel(scale, keep, got, piece):
    piece[...] = ((keep[...] + got[...].astype(F32)) * scale).astype(BF16)


def pair_kernel(corners, place_ref, mine, other, both):
    rows = mine.shape[0]
    side = place_ref[0] // corners
    both[pl.ds(pl.multiple_of(side * rows, rows), rows), :] = mine[...]
    both[pl.ds(pl.multiple_of((1 - side) * rows, rows), rows), :] = other[...]


def place_kernel(corners, place_ref, *refs):
    out = refs[-1]
    rows = refs[0].shape[0]
    corner = place_ref[0] & (corners - 1)
    for e, ref in enumerate(refs[:-1]):
        at = pl.multiple_of((corner ^ e) * rows, rows)
        out[pl.ds(at, rows), :] = ref[...].astype(F32)


def xor_route(size, mask):
    return [(i, i ^ mask) for i in range(size)]


def shifted(block, distance):
    count = lax.axis_size("seq")
    route = [(i, i + distance) for i in range(count) if 0 <= i + distance < count]
    return lax.ppermute(block, "seq", route)


def swapped(block, axis, mask):
    return lax.ppermute(block, axis, xor_route(lax.axis_size(axis), mask))


def after(value, *others):
    return lax.optimization_barrier((value, *others))[0]


def on_device(queries, keys, values, gates, out_grad, w_out, hist_lengths):
    rows, width = queries.shape[1:]
    seq = lax.axis_size("seq")
    batch = lax.axis_size("batch")
    seq_at = lax.axis_index("seq")
    place = jnp.stack([seq_at, lax.axis_index("batch")]).astype(jnp.int32)
    scalars = (hist_lengths, place)
    even = (seq_at & 1) == 0
    full = jax.ShapeDtypeStruct((rows, width), BF16)
    wide = jax.ShapeDtypeStruct((rows, width), F32)
    block_flops = 2 * rows * rows * width
    proj_flops = 2 * rows * width * width

    k2 = shifted(keys[0], 2)
    v2 = shifted(values[0], 2)
    v1 = shifted(values[0], 1)
    q, k, v, grad, w, mixed_own, grad_hidden, slope0 = call(
        own_kernel,
        [full, full, full, full, jax.ShapeDtypeStruct(w_out.shape, BF16), wide, wide, wide],
        scalars,
        (queries[0], keys[0], values[0], out_grad[0], w_out),
        proj_flops + 2 * block_flops,
        [pltpu.SemaphoreType.DMA((5,))],
        [pl.BlockSpec(memory_space=pltpu.HBM)] * 5,
    )
    k1 = swapped(jnp.where(even, k, k2), "seq", 1)
    grads = [grad] + [swapped(grad, "batch", d) for d in range(1, batch)]
    q2 = shifted(q, -2)
    attention1, attention2, slope1, slope2 = call(
        far_kernel, [full, full, wide, wide], scalars, (q, k1, k2), 2 * block_flops
    )
    q1 = swapped(jnp.where(even, q2, q), "seq", 1)
    part = width // batch
    piece = jax.ShapeDtypeStruct((rows, part), BF16)
    hidden, grad_gates, grad_mix, *slices = call(
        functools.partial(forward_kernel, batch),
        [full, full, full] + [piece] * batch,
        (place,),
        (attention1, attention2, v1, v2, mixed_own, grad_hidden, gates[0]),
        2 * block_flops,
        [pltpu.VMEM((rows, width), F32)],
    )
    hiddens = [slices[0]] + [swapped(slices[d], "batch", d) for d in range(1, batch)]
    g2 = shifted(grad_mix, -2)
    g1 = swapped(jnp.where(even, g2, grad_mix), "seq", 1)

    corners = 4
    direct = seq == 2 * corners
    rows_w = part // corners if direct else part
    scale = (rows * seq * batch) ** (-0.5)
    own, *sends = call(
        functools.partial(weight_kernel, batch),
        [jax.ShapeDtypeStruct((rows_w, width), F32)]
        + ([jax.ShapeDtypeStruct((rows_w, width), BF16)] * (corners - 1) if direct else []),
        (place,),
        (*hiddens, *grads),
        proj_flops,
        [pltpu.VMEM((part, width), F32)],
    )
    output, grad_queries = call(
        query_kernel,
        [full, full],
        (),
        (k, k1, k2, v, v1, v2, slope0, slope1, slope2, grad_mix, after(hidden, own), w),
        proj_flops + 6 * block_flops,
    )
    if direct:
        half = jax.ShapeDtypeStruct((rows_w // 2, width), BF16)
        half_wide = jax.ShapeDtypeStruct((rows_w // 2, width), F32)
        got = [swapped(s, "seq", e + 1) for e, s in enumerate(sends)]
        keep, send = call(
            functools.partial(corner_kernel, corners),
            [half_wide, half],
            (place,),
            (own, *got),
            own.size * 4,
            [pltpu.VMEM((rows_w, width), F32)],
        )
        (mine,) = call(
            functools.partial(piece_kernel, scale),
            [half],
            (),
            (keep, swapped(send, "seq", corners)),
            own.size,
        )
        (both,) = call(
            functools.partial(pair_kernel, corners),
            [jax.ShapeDtypeStruct((rows_w, width), BF16)],
            (place,),
            (mine, swapped(mine, "seq", corners)),
            own.size,
        )
        shares = [both] + [swapped(both, "seq", e) for e in range(1, corners)]
        (grad_weight,) = call(
            functools.partial(place_kernel, corners),
            [jax.ShapeDtypeStruct((part, width), F32)],
            (place,),
            tuple(shares),
            part * width,
        )
        v_late = after(v, mine)
    else:
        grad_weight = lax.psum(own, "seq") * scale
        v_late = v
    grad_keys, grad_values = call(
        key_kernel, [full, full], scalars, (k, v_late, q, q1, q2, grad_mix, g1, g2), 12 * block_flops
    )
    return (
        output[None],
        grad_queries[None],
        grad_keys[None],
        grad_values[None],
        grad_gates[None],
        grad_weight,
    )


def solution(mesh):
    token = P("batch", "seq", None)
    return jax.shard_map(
        on_device,
        mesh=mesh,
        in_specs=(token, token, token, token, token, P(), P("batch", None)),
        out_specs=(token, token, token, token, token, P("batch", None)),
        check_vma=False,
    )
```

```python
import functools

import jax
import jax.numpy as jnp
from jax import lax
from jax.experimental import pallas as pl
from jax.experimental.pallas import tpu as pltpu
from jax.sharding import PartitionSpec as P

HEADS = 8
WINDOW = 256
REACH = 2

VMEM = pl.BlockSpec(memory_space=pltpu.VMEM)
SMEM = pl.BlockSpec(memory_space=pltpu.SMEM)
F32 = jnp.float32
BF16 = jnp.bfloat16
NT = (((1,), (1,)), ((), ()))
TN = (((0,), (0,)), ((), ()))


def dot(a, b):
    return jnp.dot(a, b, preferred_element_type=F32)


def dot_nt(a, b):
    return lax.dot_general(a, b, NT, preferred_element_type=F32)


def dot_tn(a, b):
    return lax.dot_general(a, b, TN, preferred_element_type=F32)


def logistic(scores):
    return 0.5 * jnp.tanh(0.5 * scores) + 0.5


def silu_slope(scores, gate):
    return gate * (1.0 + scores * (1.0 - gate))


def start_of(positions, len_ref):
    total = jnp.zeros_like(positions)
    end = jnp.int32(0)
    for k in range(len_ref.shape[1]):
        length = len_ref[0, k]
        end = end + length
        total = total + jnp.where(positions >= end, length, 0)
    return total


def allowed_block(rows, first_query, first_key, len_ref, query_dim):
    shape = (rows, rows)
    query_pos = first_query + lax.broadcasted_iota(jnp.int32, shape, query_dim)
    key_pos = first_key + lax.broadcasted_iota(jnp.int32, shape, 1 - query_dim)
    start = start_of(query_pos, len_ref)
    return (key_pos >= start) & (key_pos <= query_pos) & (key_pos > query_pos - WINDOW)


def head_slice(h, width):
    return slice(h * width, (h + 1) * width)


def cost(flops, arrays):
    total = sum(a.size * a.dtype.itemsize for a in arrays)
    return pl.CostEstimate(flops=flops, bytes_accessed=total, transcendentals=0)


def call(kernel, outs, scalars, arrays, flops, scratch=(), spaces=None, out_space=VMEM):
    spaces = spaces or [VMEM] * len(arrays)
    return pl.pallas_call(
        kernel,
        out_shape=outs,
        in_specs=[SMEM] * len(scalars) + spaces,
        out_specs=[out_space] * len(outs),
        scratch_shapes=list(scratch),
        cost_estimate=cost(flops, list(arrays) + list(outs)),
        compiler_params=pltpu.CompilerParams(vmem_limit_bytes=40 * 1024 * 1024),
    )(*scalars, *arrays)


def own_kernel(
    len_ref, place_ref, q_in, k_in, v_in, grad_in, w_in, gate_in, q, k, v, grad, w, gates, mixed, grad_hidden, slope, sems
):
    moves = [
        pltpu.make_async_copy(src, dst, sems.at[i])
        for i, (src, dst) in enumerate(
            ((q_in, q), (k_in, k), (v_in, v), (grad_in, grad), (w_in, w), (gate_in, gates))
        )
    ]
    for move in moves:
        move.start()
    rows, width = q.shape
    size = width // HEADS
    scale = size ** (-0.5)
    first = place_ref[0] * rows
    allowed = allowed_block(rows, first, first, len_ref, 0)
    for move in moves[:3]:
        move.wait()
    for h in range(HEADS):
        cols = head_slice(h, size)
        scores = dot_nt(q[:, cols], k[:, cols]) * scale
        gate = logistic(scores)
        attention = jnp.where(allowed, scores * gate, 0.0).astype(BF16)
        slope[:, cols] = jnp.where(allowed, silu_slope(scores, gate) * scale, 0.0)
        mixed[:, cols] = dot(attention, v[:, cols])
    for move in moves[3:]:
        move.wait()
    grad_hidden[...] = dot_nt(grad[...], w[...])


def far_scores(h, allowed, q, keys, slope):
    size = q.shape[1] // HEADS
    scale = size ** (-0.5)
    cols = head_slice(h, size)
    scores = dot_nt(q[:, cols], keys[:, cols]) * scale
    gate = logistic(scores)
    slope[:, cols] = jnp.where(allowed, silu_slope(scores, gate) * scale, 0.0)
    return jnp.where(allowed, scores * gate, 0.0).astype(BF16)


def second_kernel(len_ref, place_ref, q, keys, vals, mixed_own, mixed, slope):
    rows, width = q.shape
    size = width // HEADS
    first = place_ref[0] * rows
    allowed = allowed_block(rows, first, first - 2 * rows, len_ref, 0)
    for h in range(HEADS):
        cols = head_slice(h, size)
        attention = far_scores(h, allowed, q, keys, slope)
        mixed[:, cols] = mixed_own[:, cols] + dot(attention, vals[:, cols])


def first_kernel(len_ref, place_ref, q, keys, attention, slope):
    rows, width = q.shape
    size = width // HEADS
    first = place_ref[0] * rows
    allowed = allowed_block(rows, first, first - rows, len_ref, 0)
    for h in range(HEADS):
        attention[:, head_slice(h, size)] = far_scores(h, allowed, q, keys, slope)


def forward_kernel(groups, place_ref, attention, vals, mixed_far, gates, hidden, normed, inv_std, *rest):
    slices, mixed = rest[:-1], rest[-1]
    rows, width = vals.shape
    size = width // HEADS
    for h in range(HEADS):
        cols = head_slice(h, size)
        mixed[:, cols] = mixed_far[:, cols] + dot(attention[:, cols], vals[:, cols])
    values = mixed[...]
    centered = values - jnp.mean(values, axis=1, keepdims=True)
    inverse = lax.rsqrt(jnp.mean(centered * centered, axis=1, keepdims=True) + 1e-05)
    inv_std[...] = jnp.broadcast_to(inverse, inv_std.shape)
    normed[...] = centered * inverse
    hidden[...] = (normed[...] * gates[...].astype(F32)).astype(BF16)
    part = width // groups
    for d, ref in enumerate(slices):
        at = pl.multiple_of((place_ref[1] ^ d) * part, 128)
        ref[...] = hidden[:, pl.ds(at, part)]


def mix_kernel(grad_hidden, gates, normed, inv_std, grad_gates, grad_mix):
    gh = grad_hidden[...]
    norm = normed[...]
    grad_gates[...] = (gh * norm).astype(BF16)
    grad_norm = gh * gates[...].astype(F32)
    grad_mix[...] = (
        (
            grad_norm
            - jnp.mean(grad_norm, axis=1, keepdims=True)
            - norm * jnp.mean(grad_norm * norm, axis=1, keepdims=True)
        )
        * inv_std[:, :1]
    ).astype(BF16)


def query_kernel(k0, k1, k2, v0, v1, v2, slope0, slope1, slope2, grad_mix, hidden, w, output, grad_queries):
    rows, width = k0.shape
    size = width // HEADS
    output[...] = dot(hidden[...], w[...]).astype(BF16)
    parts = ((k0, v0, slope0), (k1, v1, slope1), (k2, v2, slope2))
    for h in range(HEADS):
        cols = head_slice(h, size)
        total = jnp.zeros((rows, size), F32)
        for keys, vals, slope in parts:
            grad_attention = dot_nt(grad_mix[:, cols], vals[:, cols])
            grad_scores = (grad_attention * slope[:, cols]).astype(BF16)
            total = total + dot(grad_scores, keys[:, cols])
        grad_queries[:, cols] = total.astype(BF16)


def key_kernel(len_ref, place_ref, k, v, q0, q1, q2, g0, g1, g2, grad_keys, grad_values):
    rows, width = k.shape
    size = width // HEADS
    scale = size ** (-0.5)
    first = place_ref[0] * rows
    masks = [allowed_block(rows, first + d * rows, first, len_ref, 1) for d in range(REACH + 1)]
    for h in range(HEADS):
        cols = head_slice(h, size)
        keys_total = jnp.zeros((rows, size), F32)
        values_total = jnp.zeros((rows, size), F32)
        for mask, qd, gd in zip(masks, (q0, q1, q2), (g0, g1, g2)):
            scores = dot_nt(k[:, cols], qd[:, cols]) * scale
            gate = logistic(scores)
            attention = jnp.where(mask, scores * gate, 0.0).astype(BF16)
            grad_attention = dot_nt(v[:, cols], gd[:, cols])
            slope = jnp.where(mask, silu_slope(scores, gate) * scale, 0.0)
            grad_scores = (grad_attention * slope).astype(BF16)
            keys_total = keys_total + dot(grad_scores, qd[:, cols])
            values_total = values_total + dot(attention, gd[:, cols])
        grad_keys[:, cols] = keys_total.astype(BF16)
        grad_values[:, cols] = values_total.astype(BF16)


def weight_kernel(groups, place_ref, *refs):
    hidden = jnp.concatenate([ref[...] for ref in refs[:groups]], axis=0)
    grads = jnp.concatenate([ref[...] for ref in refs[groups : 2 * groups]], axis=0)
    own = refs[2 * groups]
    sends = refs[2 * groups + 1 : -1]
    total = refs[-1]
    total[...] = dot_tn(hidden, grads)
    if not sends:
        own[...] = total[...]
        return
    rows = own.shape[0]
    corner = place_ref[0] & len(sends)
    own[...] = total[pl.ds(pl.multiple_of(corner * rows, rows), rows), :]
    for e, ref in enumerate(sends):
        at = pl.multiple_of((corner ^ (e + 1)) * rows, rows)
        ref[...] = total[pl.ds(at, rows), :].astype(BF16)


def corner_kernel(own, *refs):
    got, narrow = refs[:-1], refs[-1]
    acc = own[...]
    for ref in got:
        acc = acc + ref[...].astype(F32)
    narrow[...] = acc.astype(BF16)


def pair_kernel(scale, mine, other, both):
    both[...] = ((mine[...].astype(F32) + other[...].astype(F32)) * scale).astype(BF16)


def place_kernel(corners, place_ref, *refs):
    shares, (out, wide, sems) = refs[:corners], refs[corners:]
    rows = shares[0].shape[0]
    corner = place_ref[0] & (corners - 1)
    moves = []
    for e, ref in enumerate(shares):
        wide[e] = ref[...].astype(F32)
        at = pl.multiple_of((corner ^ e) * rows, rows)
        moves.append(pltpu.make_async_copy(wide.at[e], out.at[pl.ds(at, rows), :], sems.at[e]))
        moves[-1].start()
    for move in moves:
        move.wait()


def xor_route(size, mask):
    return [(i, i ^ mask) for i in range(size)]


def shifted(block, distance):
    count = lax.axis_size("seq")
    route = [(i, i + distance) for i in range(count) if 0 <= i + distance < count]
    return lax.ppermute(block, "seq", route)


def swapped(block, axis, mask):
    return lax.ppermute(block, axis, xor_route(lax.axis_size(axis), mask))


def after(value, *others):
    return lax.optimization_barrier((value, *others))[0]


def on_device(queries, keys, values, gates, out_grad, w_out, hist_lengths):
    rows, width = queries.shape[1:]
    seq = lax.axis_size("seq")
    batch = lax.axis_size("batch")
    seq_at = lax.axis_index("seq")
    place = jnp.stack([seq_at, lax.axis_index("batch")]).astype(jnp.int32)
    scalars = (hist_lengths, place)
    even = (seq_at & 1) == 0
    full = jax.ShapeDtypeStruct((rows, width), BF16)
    wide = jax.ShapeDtypeStruct((rows, width), F32)
    block_flops = 2 * rows * rows * width
    proj_flops = 2 * rows * width * width

    k2 = shifted(keys[0], 2)
    v2 = shifted(values[0], 2)
    v1 = shifted(values[0], 1)
    grads = [out_grad[0]]
    for d in range(1, batch):
        low = d & -d
        grads.append(swapped(grads[d ^ low], "batch", low))
    q, k, v, grad, w, gate, mixed_own, grad_hidden, slope0 = call(
        own_kernel,
        [full, full, full, full, jax.ShapeDtypeStruct(w_out.shape, BF16), full, wide, wide, wide],
        scalars,
        tuple(
            pltpu.with_memory_space_constraint(a, pltpu.HBM)
            for a in (queries[0], keys[0], values[0], out_grad[0], w_out, gates[0])
        ),
        proj_flops + 2 * block_flops,
        [pltpu.SemaphoreType.DMA((6,))],
        [pl.BlockSpec(memory_space=pltpu.HBM)] * 6,
    )
    grads[0] = grad
    k1 = swapped(jnp.where(even, k, k2), "seq", 1)
    q2 = shifted(q, -2)
    mixed_far, slope2 = call(
        second_kernel, [wide, wide], scalars, (q, k2, v2, mixed_own), 2 * block_flops
    )
    q1 = swapped(jnp.where(even, q2, q), "seq", 1)
    attention1, slope1 = call(first_kernel, [full, wide], scalars, (q, k1), block_flops)
    part = width // batch
    piece = jax.ShapeDtypeStruct((rows, part), BF16)
    hidden, normed, inv_std, *slices = call(
        functools.partial(forward_kernel, batch),
        [full, wide, jax.ShapeDtypeStruct((rows, 128), F32)] + [piece] * batch,
        (place,),
        (attention1, v1, mixed_far, gate),
        block_flops,
        [pltpu.VMEM((rows, width), F32)],
    )
    hiddens = [slices[0]] + [swapped(slices[d], "batch", d) for d in range(1, batch)]
    grad_gates, grad_mix = call(
        mix_kernel, [full, full], (), (grad_hidden, gate, normed, inv_std), block_flops // 4
    )
    g2 = shifted(grad_mix, -2)
    g1 = swapped(jnp.where(even, g2, grad_mix), "seq", 1)

    corners = 4
    direct = seq == 2 * corners
    rows_w = part // corners if direct else part
    share = jax.ShapeDtypeStruct((rows_w, width), BF16)
    scale = (rows * seq * batch) ** (-0.5)
    own, *sends = call(
        functools.partial(weight_kernel, batch),
        [jax.ShapeDtypeStruct((rows_w, width), F32)] + [share] * (corners - 1 if direct else 0),
        (place,),
        (*hiddens, *grads),
        proj_flops,
        [pltpu.VMEM((part, width), F32)],
    )
    output, grad_queries = call(
        query_kernel,
        [full, full],
        (),
        (k, k1, k2, v, v1, v2, slope0, slope1, slope2, grad_mix, after(hidden, own), w),
        proj_flops + 6 * block_flops,
    )
    if direct:
        got = [swapped(s, "seq", e + 1) for e, s in enumerate(sends)]
        (mine,) = call(corner_kernel, [share], (), (after(own, output), *got), own.size * 4)
        other = swapped(mine, "seq", corners)
        (both,) = call(
            functools.partial(pair_kernel, scale), [share], (), (mine, other), own.size * 2
        )
        last = after(v, both)
    else:
        last = v
    grad_keys, grad_values = call(
        key_kernel, [full, full], scalars, (k, last, q, q1, q2, grad_mix, g1, g2), 12 * block_flops
    )
    if direct:
        shares = [swapped(both, "seq", e) for e in range(1, corners)]
        (grad_weight,) = call(
            functools.partial(place_kernel, corners),
            [jax.ShapeDtypeStruct((part, width), F32)],
            (place,),
            (after(both, grad_keys), *shares),
            part * width,
            [pltpu.VMEM((corners, rows_w, width), F32), pltpu.SemaphoreType.DMA((corners,))],
            out_space=pl.BlockSpec(memory_space=pltpu.HBM),
        )
    else:
        grad_weight = lax.psum(own, "seq") * scale
    return (
        output[None],
        grad_queries[None],
        grad_keys[None],
        grad_values[None],
        grad_gates[None],
        grad_weight,
    )


def solution(mesh):
    token = P("batch", "seq", None)
    return jax.shard_map(
        on_device,
        mesh=mesh,
        in_specs=(token, token, token, token, token, P(), P("batch", None)),
        out_specs=(token, token, token, token, token, P("batch", None)),
        check_vma=False,
    )
```

```python
import functools
import math

import jax
import jax.numpy as jnp
from jax import lax
from jax.experimental import pallas as pl
from jax.experimental.pallas import tpu as pltpu
from jax.sharding import PartitionSpec as P

HEADS = 8
WINDOW = 256
REACH = 2
CHUNKS = 4

VMEM = pl.BlockSpec(memory_space=pltpu.VMEM)
SMEM = pl.BlockSpec(memory_space=pltpu.SMEM)
F32 = jnp.float32
BF16 = jnp.bfloat16
NT = (((1,), (1,)), ((), ()))
TN = (((0,), (0,)), ((), ()))


def dot(a, b):
    return jnp.dot(a, b, preferred_element_type=F32)


def dot_nt(a, b):
    return lax.dot_general(a, b, NT, preferred_element_type=F32)


def dot_tn(a, b):
    return lax.dot_general(a, b, TN, preferred_element_type=F32)


def logistic(scores):
    return 0.5 * jnp.tanh(0.5 * scores) + 0.5


def silu_slope(scores, gate):
    return gate * (1.0 + scores * (1.0 - gate))


def start_of(positions, len_ref):
    total = jnp.zeros_like(positions)
    end = jnp.int32(0)
    for k in range(len_ref.shape[1]):
        length = len_ref[0, k]
        end = end + length
        total = total + jnp.where(positions >= end, length, 0)
    return total


def allowed_block(rows, first_query, first_key, len_ref, query_dim):
    shape = (rows, rows)
    query_pos = first_query + lax.broadcasted_iota(jnp.int32, shape, query_dim)
    key_pos = first_key + lax.broadcasted_iota(jnp.int32, shape, 1 - query_dim)
    start = start_of(query_pos, len_ref)
    return (key_pos >= start) & (key_pos <= query_pos) & (key_pos > query_pos - WINDOW)


def head_slice(h, width):
    return slice(h * width, (h + 1) * width)


def kept(shape, dtype):
    return pltpu.VMEM(shape, dtype)


def in_hbm(array):
    return pltpu.with_memory_space_constraint(array, pltpu.HBM)


def nbytes(arrays):
    return sum(math.prod(a.shape) * jnp.dtype(a.dtype).itemsize for a in arrays)


def call(kernel, outs, scalars, arrays, flops, scratch=(), spaces=None, out_space=VMEM, aliases={}):
    return pl.pallas_call(
        kernel,
        out_shape=outs,
        in_specs=[SMEM] * len(scalars) + (spaces or [VMEM] * len(arrays)),
        out_specs=[out_space] * len(outs),
        scratch_shapes=list(scratch),
        input_output_aliases=aliases,
        cost_estimate=pl.CostEstimate(
            flops=flops, bytes_accessed=nbytes([*arrays, *outs]), transcendentals=0
        ),
        compiler_params=pltpu.CompilerParams(vmem_limit_bytes=32 * 1024 * 1024),
    )(*scalars, *arrays)


def own_kernel(len_ref, place_ref, q_in, k_in, v_in, q, k, v, mixed, slope, sems):
    moves = [
        pltpu.make_async_copy(src, dst, sems.at[i])
        for i, (src, dst) in enumerate(((q_in, q), (k_in, k), (v_in, v)))
    ]
    for move in moves:
        move.start()
    rows, width = q.shape
    size = width // HEADS
    first = place_ref[0] * rows
    allowed = allowed_block(rows, first, first, len_ref, 0)
    for move in moves:
        move.wait()
    for h in range(HEADS):
        cols = head_slice(h, size)
        attention = block_scores(h, allowed, q, k, slope)
        mixed[:, cols] = dot(attention, v[:, cols])


def project_kernel(grad_in, w_in, gate_in, grad, w, gates, grad_hidden, sems):
    width = w.shape[0]
    part = width // CHUNKS
    moves = [pltpu.make_async_copy(grad_in, grad, sems.at[0])]
    for c in range(CHUNKS):
        here = pl.ds(c * part, part)
        moves.append(pltpu.make_async_copy(w_in.at[here, :], w.at[here, :], sems.at[c + 1]))
    moves.append(pltpu.make_async_copy(gate_in, gates, sems.at[CHUNKS + 1]))
    for move in moves:
        move.start()
    moves[0].wait()
    for c in range(CHUNKS):
        moves[c + 1].wait()
        here = slice(c * part, (c + 1) * part)
        grad_hidden[:, here] = dot_nt(grad[...], w[here, :])
    moves[-1].wait()


def block_scores(h, allowed, q, keys, slope):
    size = q.shape[1] // HEADS
    scale = size ** (-0.5)
    cols = head_slice(h, size)
    scores = dot_nt(q[:, cols], keys[:, cols]) * scale
    gate = logistic(scores)
    slope[:, cols] = jnp.where(allowed, silu_slope(scores, gate) * scale, 0.0)
    return jnp.where(allowed, scores * gate, 0.0).astype(BF16)


def second_kernel(len_ref, place_ref, q, keys, vals, mixed_own, mixed, slope):
    rows, width = q.shape
    size = width // HEADS
    first = place_ref[0] * rows
    allowed = allowed_block(rows, first, first - 2 * rows, len_ref, 0)
    for h in range(HEADS):
        cols = head_slice(h, size)
        attention = block_scores(h, allowed, q, keys, slope)
        mixed[:, cols] = mixed_own[:, cols] + dot(attention, vals[:, cols])


def first_kernel(len_ref, place_ref, q, keys, attention, slope):
    rows, width = q.shape
    size = width // HEADS
    first = place_ref[0] * rows
    allowed = allowed_block(rows, first, first - rows, len_ref, 0)
    for h in range(HEADS):
        attention[:, head_slice(h, size)] = block_scores(h, allowed, q, keys, slope)


def forward_kernel(groups, place_ref, attention, vals, mixed_far, gates, hidden, normed, inv_std, *rest):
    slices, mixed = rest[:-1], rest[-1]
    rows, width = vals.shape
    size = width // HEADS
    for h in range(HEADS):
        cols = head_slice(h, size)
        mixed[:, cols] = mixed_far[:, cols] + dot(attention[:, cols], vals[:, cols])
    values = mixed[...]
    centered = values - jnp.mean(values, axis=1, keepdims=True)
    inverse = lax.rsqrt(jnp.mean(centered * centered, axis=1, keepdims=True) + 1e-05)
    inv_std[...] = jnp.broadcast_to(inverse, inv_std.shape)
    normed[...] = centered * inverse
    hidden[...] = (normed[...] * gates[...].astype(F32)).astype(BF16)
    part = width // groups
    for d, ref in enumerate(slices):
        at = pl.multiple_of((place_ref[1] ^ d) * part, 128)
        ref[...] = hidden[:, pl.ds(at, part)]


def mix_kernel(grad_hidden, gates, normed, inv_std, grad_gates, grad_mix):
    gh = grad_hidden[...]
    norm = normed[...]
    grad_gates[...] = (gh * norm).astype(BF16)
    grad_norm = gh * gates[...].astype(F32)
    grad_mix[...] = (
        (
            grad_norm
            - jnp.mean(grad_norm, axis=1, keepdims=True)
            - norm * jnp.mean(grad_norm * norm, axis=1, keepdims=True)
        )
        * inv_std[:, :1]
    ).astype(BF16)


def query_kernel(k0, k1, k2, v0, v1, v2, slope0, slope1, slope2, grad_mix, hidden, w, output, grad_queries):
    rows, width = k0.shape
    size = width // HEADS
    output[...] = dot(hidden[...], w[...]).astype(BF16)
    parts = ((k0, v0, slope0), (k1, v1, slope1), (k2, v2, slope2))
    for h in range(HEADS):
        cols = head_slice(h, size)
        total = jnp.zeros((rows, size), F32)
        for keys, vals, slope in parts:
            grad_attention = dot_nt(grad_mix[:, cols], vals[:, cols])
            grad_scores = (grad_attention * slope[:, cols]).astype(BF16)
            total = total + dot(grad_scores, keys[:, cols])
        grad_queries[:, cols] = total.astype(BF16)


def key_terms(h, mask, k, v, qd, gd):
    size = k.shape[1] // HEADS
    scale = size ** (-0.5)
    cols = head_slice(h, size)
    scores = dot_nt(k[:, cols], qd[:, cols]) * scale
    gate = logistic(scores)
    attention = jnp.where(mask, scores * gate, 0.0).astype(BF16)
    grad_attention = dot_nt(v[:, cols], gd[:, cols])
    slope = jnp.where(mask, silu_slope(scores, gate) * scale, 0.0)
    grad_scores = (grad_attention * slope).astype(BF16)
    return dot(grad_scores, qd[:, cols]), dot(attention, gd[:, cols])


def key_kernel(len_ref, place_ref, k, v, q0, q2, g0, g2, keys_total, values_total):
    rows, width = k.shape
    first = place_ref[0] * rows
    masks = [allowed_block(rows, first + d * rows, first, len_ref, 1) for d in (0, 2)]
    for h in range(HEADS):
        cols = head_slice(h, width // HEADS)
        own = key_terms(h, masks[0], k, v, q0, g0)
        far = key_terms(h, masks[1], k, v, q2, g2)
        keys_total[:, cols] = own[0] + far[0]
        values_total[:, cols] = own[1] + far[1]


def key_end_kernel(len_ref, place_ref, k, v, q1, g1, keys_part, values_part, grad_keys, grad_values):
    rows, width = k.shape
    first = place_ref[0] * rows
    mask = allowed_block(rows, first + rows, first, len_ref, 1)
    for h in range(HEADS):
        cols = head_slice(h, width // HEADS)
        near = key_terms(h, mask, k, v, q1, g1)
        grad_keys[:, cols] = (keys_part[:, cols] + near[0]).astype(BF16)
        grad_values[:, cols] = (values_part[:, cols] + near[1]).astype(BF16)


def weight_kernel(groups, place_ref, *refs):
    hidden = jnp.concatenate([ref[...] for ref in refs[:groups]], axis=0)
    grads = jnp.concatenate([ref[...] for ref in refs[groups : 2 * groups]], axis=0)
    own = refs[2 * groups]
    sends = refs[2 * groups + 1 : -1]
    total = refs[-1]
    total[...] = dot_tn(hidden, grads)
    if not sends:
        own[...] = total[...]
        return
    rows = own.shape[0]
    corner = place_ref[0] & len(sends)
    own[...] = total[pl.ds(pl.multiple_of(corner * rows, rows), rows), :]
    for e, ref in enumerate(sends):
        at = pl.multiple_of((corner ^ (e + 1)) * rows, rows)
        ref[...] = total[pl.ds(at, rows), :].astype(BF16)


def corner_kernel(own, *refs):
    got, narrow = refs[:-1], refs[-1]
    acc = own[...]
    for ref in got:
        acc = acc + ref[...].astype(F32)
    narrow[...] = acc.astype(BF16)


def pair_kernel(scale, mine, other, both):
    both[...] = ((mine[...].astype(F32) + other[...].astype(F32)) * scale).astype(BF16)


def place_kernel(corners, partner, place_ref, share, *refs):
    out, wide, sem = refs[-3:]
    rows = share.shape[0]
    corner = (place_ref[0] & (corners - 1)) ^ partner
    wide[...] = share[...].astype(F32)
    at = pl.multiple_of(corner * rows, rows)
    move = pltpu.make_async_copy(wide, out.at[pl.ds(at, rows), :], sem)
    move.start()
    move.wait()


def xor_route(size, mask):
    return [(i, i ^ mask) for i in range(size)]


def shifted(block, distance):
    count = lax.axis_size("seq")
    route = [(i, i + distance) for i in range(count) if 0 <= i + distance < count]
    return lax.ppermute(block, "seq", route)


def swapped(block, axis, mask):
    return lax.ppermute(block, axis, xor_route(lax.axis_size(axis), mask))


def after(value, *others):
    return lax.optimization_barrier((value, *others))[0]


def on_device(queries, keys, values, gates, out_grad, w_out, hist_lengths):
    rows, width = queries.shape[1:]
    seq = lax.axis_size("seq")
    batch = lax.axis_size("batch")
    seq_at = lax.axis_index("seq")
    place = jnp.stack([seq_at, lax.axis_index("batch")]).astype(jnp.int32)
    scalars = (hist_lengths, place)
    even = (seq_at & 1) == 0
    full = jax.ShapeDtypeStruct((rows, width), BF16)
    near = kept((rows, width), BF16)
    wide = kept((rows, width), F32)
    block_flops = 2 * rows * rows * width
    proj_flops = 2 * rows * width * width
    part = width // batch
    hbm = pl.BlockSpec(memory_space=pltpu.HBM)

    k2 = shifted(keys[0], 2)
    v2 = shifted(values[0], 2)
    q, k, v, mixed_own, slope0 = call(
        own_kernel,
        [near, near, near, wide, wide],
        scalars,
        (in_hbm(queries[0]), in_hbm(keys[0]), in_hbm(values[0])),
        2 * block_flops,
        [pltpu.SemaphoreType.DMA((3,))],
        [hbm] * 3,
    )
    passed = jnp.where(even, k, k2)
    k1 = swapped(passed, "seq", 1)
    v1 = shifted(v, 1)
    grad, w, gate, grad_hidden = call(
        project_kernel,
        [near, kept(w_out.shape, BF16), near, wide],
        (),
        (in_hbm(after(out_grad[0], passed)), in_hbm(w_out), in_hbm(gates[0])),
        proj_flops,
        [pltpu.SemaphoreType.DMA((CHUNKS + 2,))],
        [hbm] * 3,
    )
    grads = [grad]
    for d in range(1, batch):
        low = d & -d
        source = out_grad[0] if d == low else grads[d ^ low]
        grads.append(swapped(after(source, v2) if d == 1 else source, "batch", low))
    q2 = shifted(q, -2)
    mixed_far, slope2 = call(
        second_kernel, [wide, wide], scalars, (after(q, grads[-2]), k2, v2, mixed_own), 2 * block_flops
    )
    passed_q = jnp.where(even, q2, q)
    q1 = swapped(passed_q, "seq", 1)
    attention1, slope1 = call(first_kernel, [near, wide], scalars, (after(q, passed_q, grads[1], grads[-1]), k1), block_flops)
    hidden, normed, inv_std, *slices = call(
        functools.partial(forward_kernel, batch),
        [near, wide, kept((rows, 128), F32)] + [kept((rows, part), BF16)] * batch,
        (place,),
        (attention1, v1, mixed_far, gate),
        block_flops,
        [pltpu.VMEM((rows, width), F32)],
    )
    hiddens = [slices[0]] + [swapped(slices[d], "batch", d) for d in range(1, batch)]
    grad_gates, grad_mix = call(
        mix_kernel, [full, near], (), (grad_hidden, gate, normed, inv_std), block_flops // 4
    )
    g2 = shifted(grad_mix, -2)
    passed_g = jnp.where(even, g2, grad_mix)

    corners = 4
    direct = seq == 2 * corners
    rows_w = part // corners if direct else part
    share = kept((rows_w, width), BF16)
    scale = (rows * seq * batch) ** (-0.5)
    own, *sends = call(
        functools.partial(weight_kernel, batch),
        [kept((rows_w, width), F32)] + [share] * (corners - 1 if direct else 0),
        (place,),
        (*hiddens, *grads),
        proj_flops,
        [pltpu.VMEM((part, width), F32)],
    )
    keys_part, values_part = call(
        key_kernel,
        [wide, wide],
        scalars,
        (k, after(v, own), q, q2, grad_mix, g2),
        8 * block_flops,
    )
    hidden_late = hidden
    if direct:
        got = [swapped(s, "seq", e + 1) for e, s in enumerate(sends)]
        (mine,) = call(corner_kernel, [share], (), (after(own, keys_part), *got), own.size * 4)
        other = swapped(mine, "seq", corners)
        passed_g = after(passed_g, got[0])
        hidden_late = after(hidden, mine)
    output, grad_queries = call(
        query_kernel,
        [full, full],
        (),
        (k, k1, k2, v, v1, v2, slope0, slope1, slope2, grad_mix, hidden_late, w),
        proj_flops + 6 * block_flops,
    )
    g1 = swapped(passed_g, "seq", 1)
    last = v
    if direct:
        (both,) = call(
            functools.partial(pair_kernel, scale),
            [share],
            (),
            (after(mine, output), other),
            own.size * 2,
        )
        last = after(v, both)
    grad_keys, grad_values = call(
        key_end_kernel,
        [full, full],
        scalars,
        (k, last, q1, g1, keys_part, values_part),
        4 * block_flops,
    )
    if direct:
        result = jax.ShapeDtypeStruct((part, width), F32)
        shares = [after(both, grad_keys)] + [swapped(both, "seq", e) for e in range(1, corners)]
        grad_weight = None
        for e, piece in enumerate(shares):
            (grad_weight,) = call(
                functools.partial(place_kernel, corners, e),
                [result],
                (place,),
                (piece,) if e == 0 else (piece, grad_weight),
                piece.size,
                [pltpu.VMEM((rows_w, width), F32), pltpu.SemaphoreType.DMA(())],
                spaces=[VMEM] if e == 0 else [VMEM, hbm],
                out_space=hbm,
                aliases={} if e == 0 else {2: 0},
            )
    else:
        grad_weight = lax.psum(own, "seq") * scale
    return (
        output[None],
        grad_queries[None],
        grad_keys[None],
        grad_values[None],
        grad_gates[None],
        grad_weight,
    )


def solution(mesh):
    token = P("batch", "seq", None)
    return jax.shard_map(
        on_device,
        mesh=mesh,
        in_specs=(token, token, token, token, token, P(), P("batch", None)),
        out_specs=(token, token, token, token, token, P("batch", None)),
        check_vma=False,
    )
```

```python
import functools
import math

import jax
import jax.numpy as jnp
from jax import lax
from jax.experimental import pallas as pl
from jax.experimental.pallas import tpu as pltpu
from jax.sharding import PartitionSpec as P

HEADS = 8
WINDOW = 256
REACH = 2
CHUNKS = 4

VMEM = pl.BlockSpec(memory_space=pltpu.VMEM)
SMEM = pl.BlockSpec(memory_space=pltpu.SMEM)
F32 = jnp.float32
BF16 = jnp.bfloat16
NT = (((1,), (1,)), ((), ()))
TN = (((0,), (0,)), ((), ()))


def dot(a, b):
    return jnp.dot(a, b, preferred_element_type=F32)


def dot_nt(a, b):
    return lax.dot_general(a, b, NT, preferred_element_type=F32)


def dot_tn(a, b):
    return lax.dot_general(a, b, TN, preferred_element_type=F32)


def logistic(scores):
    return 0.5 * jnp.tanh(0.5 * scores) + 0.5


def silu_slope(scores, gate):
    return gate * (1.0 + scores * (1.0 - gate))


def start_of(positions, len_ref):
    total = jnp.zeros_like(positions)
    end = jnp.int32(0)
    for k in range(len_ref.shape[1]):
        length = len_ref[0, k]
        end = end + length
        total = total + jnp.where(positions >= end, length, 0)
    return total


def allowed_block(rows, first_query, first_key, len_ref, query_dim):
    shape = (rows, rows)
    query_pos = first_query + lax.broadcasted_iota(jnp.int32, shape, query_dim)
    key_pos = first_key + lax.broadcasted_iota(jnp.int32, shape, 1 - query_dim)
    start = start_of(query_pos, len_ref)
    return (key_pos >= start) & (key_pos <= query_pos) & (key_pos > query_pos - WINDOW)


def head_slice(h, width):
    return slice(h * width, (h + 1) * width)


def kept(shape, dtype):
    return pltpu.VMEM(shape, dtype)


def in_hbm(array):
    return pltpu.with_memory_space_constraint(array, pltpu.HBM)


def nbytes(arrays):
    return sum(math.prod(a.shape) * jnp.dtype(a.dtype).itemsize for a in arrays)


def call(kernel, outs, scalars, arrays, flops, scratch=(), spaces=None, out_space=VMEM, aliases={}):
    return pl.pallas_call(
        kernel,
        out_shape=outs,
        in_specs=[SMEM] * len(scalars) + (spaces or [VMEM] * len(arrays)),
        out_specs=[out_space] * len(outs),
        scratch_shapes=list(scratch),
        input_output_aliases=aliases,
        cost_estimate=pl.CostEstimate(
            flops=flops, bytes_accessed=nbytes([*arrays, *outs]), transcendentals=0
        ),
        compiler_params=pltpu.CompilerParams(vmem_limit_bytes=32 * 1024 * 1024),
    )(*scalars, *arrays)


def own_kernel(len_ref, place_ref, q_in, k_in, v_in, q, k, v, mixed, slope, sems):
    moves = [
        pltpu.make_async_copy(src, dst, sems.at[i])
        for i, (src, dst) in enumerate(((q_in, q), (k_in, k), (v_in, v)))
    ]
    for move in moves:
        move.start()
    rows, width = q.shape
    size = width // HEADS
    first = place_ref[0] * rows
    allowed = allowed_block(rows, first, first, len_ref, 0)
    for move in moves:
        move.wait()
    for h in range(HEADS):
        cols = head_slice(h, size)
        attention = block_scores(h, allowed, q, k, slope)
        mixed[:, cols] = dot(attention, v[:, cols])


def project_kernel(grad_in, w_in, gate_in, grad, w, gates, grad_hidden, sems):
    width = w.shape[0]
    part = width // CHUNKS
    moves = [pltpu.make_async_copy(grad_in, grad, sems.at[0])]
    for c in range(CHUNKS):
        here = pl.ds(c * part, part)
        moves.append(pltpu.make_async_copy(w_in.at[here, :], w.at[here, :], sems.at[c + 1]))
    moves.append(pltpu.make_async_copy(gate_in, gates, sems.at[CHUNKS + 1]))
    for move in moves:
        move.start()
    moves[0].wait()
    for c in range(CHUNKS):
        moves[c + 1].wait()
        here = slice(c * part, (c + 1) * part)
        grad_hidden[:, here] = dot_nt(grad[...], w[here, :])
    moves[-1].wait()


def block_scores(h, allowed, q, keys, slope):
    size = q.shape[1] // HEADS
    scale = size ** (-0.5)
    cols = head_slice(h, size)
    scores = dot_nt(q[:, cols], keys[:, cols]) * scale
    gate = logistic(scores)
    slope[:, cols] = jnp.where(allowed, silu_slope(scores, gate) * scale, 0.0)
    return jnp.where(allowed, scores * gate, 0.0).astype(BF16)


def second_kernel(len_ref, place_ref, q, keys, vals, mixed_own, mixed, slope):
    rows, width = q.shape
    size = width // HEADS
    first = place_ref[0] * rows
    allowed = allowed_block(rows, first, first - 2 * rows, len_ref, 0)
    for h in range(HEADS):
        cols = head_slice(h, size)
        attention = block_scores(h, allowed, q, keys, slope)
        mixed[:, cols] = mixed_own[:, cols] + dot(attention, vals[:, cols])


def first_kernel(len_ref, place_ref, q, keys, attention, slope):
    rows, width = q.shape
    size = width // HEADS
    first = place_ref[0] * rows
    allowed = allowed_block(rows, first, first - rows, len_ref, 0)
    for h in range(HEADS):
        attention[:, head_slice(h, size)] = block_scores(h, allowed, q, keys, slope)


def forward_kernel(groups, place_ref, attention, vals, mixed_far, gates, hidden, normed, inv_std, *rest):
    slices, mixed = rest[:-1], rest[-1]
    rows, width = vals.shape
    size = width // HEADS
    for h in range(HEADS):
        cols = head_slice(h, size)
        mixed[:, cols] = mixed_far[:, cols] + dot(attention[:, cols], vals[:, cols])
    values = mixed[...]
    centered = values - jnp.mean(values, axis=1, keepdims=True)
    inverse = lax.rsqrt(jnp.mean(centered * centered, axis=1, keepdims=True) + 1e-05)
    inv_std[...] = jnp.broadcast_to(inverse, inv_std.shape)
    normed[...] = centered * inverse
    hidden[...] = (normed[...] * gates[...].astype(F32)).astype(BF16)
    part = width // groups
    for d, ref in enumerate(slices):
        at = pl.multiple_of((place_ref[1] ^ d) * part, 128)
        ref[...] = hidden[:, pl.ds(at, part)]


def mix_kernel(grad_hidden, gates, normed, inv_std, grad_gates, grad_mix):
    gh = grad_hidden[...]
    norm = normed[...]
    grad_gates[...] = (gh * norm).astype(BF16)
    grad_norm = gh * gates[...].astype(F32)
    grad_mix[...] = (
        (
            grad_norm
            - jnp.mean(grad_norm, axis=1, keepdims=True)
            - norm * jnp.mean(grad_norm * norm, axis=1, keepdims=True)
        )
        * inv_std[:, :1]
    ).astype(BF16)


def query_kernel(k0, k1, k2, v0, v1, v2, slope0, slope1, slope2, grad_mix, hidden, w, output, grad_queries):
    rows, width = k0.shape
    size = width // HEADS
    output[...] = dot(hidden[...], w[...]).astype(BF16)
    parts = ((k0, v0, slope0), (k1, v1, slope1), (k2, v2, slope2))
    for h in range(HEADS):
        cols = head_slice(h, size)
        total = jnp.zeros((rows, size), F32)
        for keys, vals, slope in parts:
            grad_attention = dot_nt(grad_mix[:, cols], vals[:, cols])
            grad_scores = (grad_attention * slope[:, cols]).astype(BF16)
            total = total + dot(grad_scores, keys[:, cols])
        grad_queries[:, cols] = total.astype(BF16)


def key_terms(h, mask, k, v, qd, gd):
    size = k.shape[1] // HEADS
    scale = size ** (-0.5)
    cols = head_slice(h, size)
    scores = dot_nt(k[:, cols], qd[:, cols]) * scale
    gate = logistic(scores)
    attention = jnp.where(mask, scores * gate, 0.0).astype(BF16)
    grad_attention = dot_nt(v[:, cols], gd[:, cols])
    slope = jnp.where(mask, silu_slope(scores, gate) * scale, 0.0)
    grad_scores = (grad_attention * slope).astype(BF16)
    return dot(grad_scores, qd[:, cols]), dot(attention, gd[:, cols])


def key_kernel(len_ref, place_ref, k, v, q0, q2, g0, g2, keys_total, values_total):
    rows, width = k.shape
    first = place_ref[0] * rows
    masks = [allowed_block(rows, first + d * rows, first, len_ref, 1) for d in (0, 2)]
    for h in range(HEADS):
        cols = head_slice(h, width // HEADS)
        own = key_terms(h, masks[0], k, v, q0, g0)
        far = key_terms(h, masks[1], k, v, q2, g2)
        keys_total[:, cols] = own[0] + far[0]
        values_total[:, cols] = own[1] + far[1]


def key_end_kernel(len_ref, place_ref, k, v, q1, g1, keys_part, values_part, grad_keys, grad_values):
    rows, width = k.shape
    first = place_ref[0] * rows
    mask = allowed_block(rows, first + rows, first, len_ref, 1)
    for h in range(HEADS):
        cols = head_slice(h, width // HEADS)
        near = key_terms(h, mask, k, v, q1, g1)
        grad_keys[:, cols] = (keys_part[:, cols] + near[0]).astype(BF16)
        grad_values[:, cols] = (values_part[:, cols] + near[1]).astype(BF16)


def weight_kernel(groups, place_ref, *refs):
    hidden = jnp.concatenate([ref[...] for ref in refs[:groups]], axis=0)
    grads = jnp.concatenate([ref[...] for ref in refs[groups : 2 * groups]], axis=0)
    own = refs[2 * groups]
    sends = refs[2 * groups + 1 : -1]
    total = refs[-1]
    total[...] = dot_tn(hidden, grads)
    if not sends:
        own[...] = total[...]
        return
    rows = own.shape[0]
    corner = place_ref[0] & len(sends)
    own[...] = total[pl.ds(pl.multiple_of(corner * rows, rows), rows), :]
    for e, ref in enumerate(sends):
        at = pl.multiple_of((corner ^ (e + 1)) * rows, rows)
        ref[...] = total[pl.ds(at, rows), :].astype(BF16)


def corner_kernel(own, *refs):
    got, narrow = refs[:-1], refs[-1]
    acc = own[...]
    for ref in got:
        acc = acc + ref[...].astype(F32)
    narrow[...] = acc.astype(BF16)


def pair_kernel(scale, mine, other, both):
    both[...] = ((mine[...].astype(F32) + other[...].astype(F32)) * scale).astype(BF16)


def place_kernel(corners, place_ref, *refs):
    shares, (out, wide, sems) = refs[:corners], refs[corners:]
    rows = shares[0].shape[0]
    corner = place_ref[0] & (corners - 1)
    moves = []
    for e, ref in enumerate(shares):
        wide[e] = ref[...].astype(F32)
        at = pl.multiple_of((corner ^ e) * rows, rows)
        moves.append(pltpu.make_async_copy(wide.at[e], out.at[pl.ds(at, rows), :], sems.at[e]))
        moves[-1].start()
    for move in moves:
        move.wait()


def xor_route(size, mask):
    return [(i, i ^ mask) for i in range(size)]


def shifted(block, distance):
    count = lax.axis_size("seq")
    route = [(i, i + distance) for i in range(count) if 0 <= i + distance < count]
    return lax.ppermute(block, "seq", route)


def swapped(block, axis, mask):
    return lax.ppermute(block, axis, xor_route(lax.axis_size(axis), mask))


def after(value, *others):
    return lax.optimization_barrier((value, *others))[0]


def on_device(queries, keys, values, gates, out_grad, w_out, hist_lengths):
    rows, width = queries.shape[1:]
    seq = lax.axis_size("seq")
    batch = lax.axis_size("batch")
    seq_at = lax.axis_index("seq")
    place = jnp.stack([seq_at, lax.axis_index("batch")]).astype(jnp.int32)
    scalars = (hist_lengths, place)
    even = (seq_at & 1) == 0
    full = jax.ShapeDtypeStruct((rows, width), BF16)
    near = kept((rows, width), BF16)
    wide = kept((rows, width), F32)
    block_flops = 2 * rows * rows * width
    proj_flops = 2 * rows * width * width
    part = width // batch
    hbm = pl.BlockSpec(memory_space=pltpu.HBM)

    k2 = shifted(keys[0], 2)
    v2 = shifted(values[0], 2)
    q, k, v, mixed_own, slope0 = call(
        own_kernel,
        [near, near, near, wide, wide],
        scalars,
        (in_hbm(queries[0]), in_hbm(keys[0]), in_hbm(values[0])),
        2 * block_flops,
        [pltpu.SemaphoreType.DMA((3,))],
        [hbm] * 3,
    )
    passed = jnp.where(even, k, k2)
    k1 = swapped(passed, "seq", 1)
    v1 = shifted(after(v, passed), 1)
    grad, w, gate, grad_hidden = call(
        project_kernel,
        [near, kept(w_out.shape, BF16), near, wide],
        (),
        (in_hbm(after(out_grad[0], passed)), in_hbm(w_out), in_hbm(gates[0])),
        proj_flops,
        [pltpu.SemaphoreType.DMA((CHUNKS + 2,))],
        [hbm] * 3,
    )
    grads = [grad]
    for d in range(1, batch):
        low = d & -d
        source = after(out_grad[0], passed) if d == 1 else out_grad[0] if d == low else grads[d ^ low]
        grads.append(swapped(source, "batch", low))
    mixed_far, slope2 = call(
        second_kernel, [wide, wide], scalars, (q, k2, v2, mixed_own), 2 * block_flops
    )
    q2 = shifted(after(q, mixed_far), -2)
    passed_q = jnp.where(even, q2, q)
    q1 = swapped(passed_q, "seq", 1)
    attention1, slope1 = call(first_kernel, [near, wide], scalars, (after(q, grads[1]), k1), block_flops)
    hidden, normed, inv_std, *slices = call(
        functools.partial(forward_kernel, batch),
        [near, wide, kept((rows, 128), F32)] + [kept((rows, part), BF16)] * batch,
        (place,),
        (attention1, v1, mixed_far, gate),
        block_flops,
        [pltpu.VMEM((rows, width), F32)],
    )
    hiddens = [slices[0]] + [swapped(slices[d], "batch", d) for d in range(1, batch)]
    grad_gates, grad_mix = call(
        mix_kernel, [full, near], (), (grad_hidden, gate, normed, inv_std), block_flops // 4
    )
    g2 = shifted(grad_mix, -2)
    passed_g = jnp.where(even, g2, grad_mix)

    corners = 4
    direct = seq == 2 * corners
    rows_w = part // corners if direct else part
    share = kept((rows_w, width), BF16)
    scale = (rows * seq * batch) ** (-0.5)
    output, grad_queries = call(
        query_kernel,
        [full, full],
        (),
        (k, k1, k2, v, v1, v2, slope0, slope1, slope2, grad_mix, hidden, w),
        proj_flops + 6 * block_flops,
    )
    own, *sends = call(
        functools.partial(weight_kernel, batch),
        [kept((rows_w, width), F32)] + [share] * (corners - 1 if direct else 0),
        (place,),
        (after(hiddens[0], output), *hiddens[1:], *grads),
        proj_flops,
        [pltpu.VMEM((part, width), F32)],
    )
    keys_part, values_part = call(
        key_kernel,
        [wide, wide],
        scalars,
        (k, after(v, own), q, q2, grad_mix, g2),
        8 * block_flops,
    )
    if direct:
        got = [swapped(s, "seq", e + 1) for e, s in enumerate(sends)]
        (mine,) = call(corner_kernel, [share], (), (after(own, keys_part), *got), own.size * 4)
        other = swapped(mine, "seq", corners)
        passed_g = after(passed_g, mine)
    g1 = swapped(passed_g, "seq", 1)
    grad_keys, grad_values = call(
        key_end_kernel,
        [full, full],
        scalars,
        (k, after(v, mine) if direct else v, q1, g1, keys_part, values_part),
        4 * block_flops,
    )
    if direct:
        (both,) = call(
            functools.partial(pair_kernel, scale),
            [share],
            (),
            (after(mine, grad_keys), other),
            own.size * 2,
        )
        shares = [both] + [swapped(both, "seq", e) for e in range(1, corners)]
        (grad_weight,) = call(
            functools.partial(place_kernel, corners),
            [jax.ShapeDtypeStruct((part, width), F32)],
            (place,),
            shares,
            part * width,
            [pltpu.VMEM((corners, rows_w, width), F32), pltpu.SemaphoreType.DMA((corners,))],
            out_space=hbm,
        )
    else:
        grad_weight = lax.psum(own, "seq") * scale
    return (
        output[None],
        grad_queries[None],
        grad_keys[None],
        grad_values[None],
        grad_gates[None],
        grad_weight,
    )


def solution(mesh):
    token = P("batch", "seq", None)
    return jax.shard_map(
        on_device,
        mesh=mesh,
        in_specs=(token, token, token, token, token, P(), P("batch", None)),
        out_specs=(token, token, token, token, token, P("batch", None)),
        check_vma=False,
    )
```

```python
import functools
import math

import jax
import jax.numpy as jnp
from jax import lax
from jax.experimental import pallas as pl
from jax.experimental.pallas import tpu as pltpu
from jax.sharding import PartitionSpec as P

HEADS = 8
WINDOW = 256
REACH = 2
CHUNKS = 4

VMEM = pl.BlockSpec(memory_space=pltpu.VMEM)
SMEM = pl.BlockSpec(memory_space=pltpu.SMEM)
F32 = jnp.float32
BF16 = jnp.bfloat16
NT = (((1,), (1,)), ((), ()))
TN = (((0,), (0,)), ((), ()))


def dot(a, b):
    return jnp.dot(a, b, preferred_element_type=F32)


def dot_nt(a, b):
    return lax.dot_general(a, b, NT, preferred_element_type=F32)


def dot_tn(a, b):
    return lax.dot_general(a, b, TN, preferred_element_type=F32)


def logistic(scores):
    return 0.5 * jnp.tanh(0.5 * scores) + 0.5


def silu_slope(scores, gate):
    return gate * (1.0 + scores * (1.0 - gate))


def start_of(positions, len_ref):
    total = jnp.zeros_like(positions)
    end = jnp.int32(0)
    for k in range(len_ref.shape[1]):
        length = len_ref[0, k]
        end = end + length
        total = total + jnp.where(positions >= end, length, 0)
    return total


def allowed_block(rows, first_query, first_key, len_ref, query_dim):
    shape = (rows, rows)
    query_pos = first_query + lax.broadcasted_iota(jnp.int32, shape, query_dim)
    key_pos = first_key + lax.broadcasted_iota(jnp.int32, shape, 1 - query_dim)
    start = start_of(query_pos, len_ref)
    return (key_pos >= start) & (key_pos <= query_pos) & (key_pos > query_pos - WINDOW)


def head_slice(h, width):
    return slice(h * width, (h + 1) * width)


def kept(shape, dtype):
    return pltpu.VMEM(shape, dtype)


def in_hbm(array):
    return pltpu.with_memory_space_constraint(array, pltpu.HBM)


def nbytes(arrays):
    return sum(math.prod(a.shape) * jnp.dtype(a.dtype).itemsize for a in arrays)


def call(kernel, outs, scalars, arrays, flops, scratch=(), spaces=None, out_space=VMEM, aliases={}):
    return pl.pallas_call(
        kernel,
        out_shape=outs,
        in_specs=[SMEM] * len(scalars) + (spaces or [VMEM] * len(arrays)),
        out_specs=[out_space] * len(outs),
        scratch_shapes=list(scratch),
        input_output_aliases=aliases,
        cost_estimate=pl.CostEstimate(
            flops=flops, bytes_accessed=nbytes([*arrays, *outs]), transcendentals=0
        ),
        compiler_params=pltpu.CompilerParams(vmem_limit_bytes=32 * 1024 * 1024),
    )(*scalars, *arrays)


def own_kernel(len_ref, place_ref, q_in, k_in, v_in, q, k, v, mixed, slope, sems):
    moves = [
        pltpu.make_async_copy(src, dst, sems.at[i])
        for i, (src, dst) in enumerate(((q_in, q), (k_in, k), (v_in, v)))
    ]
    for move in moves:
        move.start()
    rows, width = q.shape
    size = width // HEADS
    first = place_ref[0] * rows
    allowed = allowed_block(rows, first, first, len_ref, 0)
    for move in moves:
        move.wait()
    for h in range(HEADS):
        cols = head_slice(h, size)
        attention = block_scores(h, allowed, q, k, slope)
        mixed[:, cols] = dot(attention, v[:, cols])


def project_kernel(grad_in, w_in, gate_in, grad, w, gates, grad_hidden, sems):
    width = w.shape[0]
    part = width // CHUNKS
    moves = [pltpu.make_async_copy(grad_in, grad, sems.at[0])]
    for c in range(CHUNKS):
        here = pl.ds(c * part, part)
        moves.append(pltpu.make_async_copy(w_in.at[here, :], w.at[here, :], sems.at[c + 1]))
    moves.append(pltpu.make_async_copy(gate_in, gates, sems.at[CHUNKS + 1]))
    for move in moves:
        move.start()
    moves[0].wait()
    for c in range(CHUNKS):
        moves[c + 1].wait()
        here = slice(c * part, (c + 1) * part)
        grad_hidden[:, here] = dot_nt(grad[...], w[here, :])
    moves[-1].wait()


def block_scores(h, allowed, q, keys, slope):
    size = q.shape[1] // HEADS
    scale = size ** (-0.5)
    cols = head_slice(h, size)
    scores = dot_nt(q[:, cols], keys[:, cols]) * scale
    gate = logistic(scores)
    slope[:, cols] = jnp.where(allowed, silu_slope(scores, gate) * scale, 0.0)
    return jnp.where(allowed, scores * gate, 0.0).astype(BF16)


def second_kernel(len_ref, place_ref, q, keys, vals, mixed_own, mixed, slope):
    rows, width = q.shape
    size = width // HEADS
    first = place_ref[0] * rows
    allowed = allowed_block(rows, first, first - 2 * rows, len_ref, 0)
    for h in range(HEADS):
        cols = head_slice(h, size)
        attention = block_scores(h, allowed, q, keys, slope)
        mixed[:, cols] = mixed_own[:, cols] + dot(attention, vals[:, cols])


def first_kernel(len_ref, place_ref, q, keys, attention, slope):
    rows, width = q.shape
    size = width // HEADS
    first = place_ref[0] * rows
    allowed = allowed_block(rows, first, first - rows, len_ref, 0)
    for h in range(HEADS):
        attention[:, head_slice(h, size)] = block_scores(h, allowed, q, keys, slope)


def forward_kernel(groups, place_ref, attention, vals, mixed_far, gates, hidden, normed, inv_std, *rest):
    slices, mixed = rest[:-1], rest[-1]
    rows, width = vals.shape
    size = width // HEADS
    for h in range(HEADS):
        cols = head_slice(h, size)
        mixed[:, cols] = mixed_far[:, cols] + dot(attention[:, cols], vals[:, cols])
    values = mixed[...]
    centered = values - jnp.mean(values, axis=1, keepdims=True)
    inverse = lax.rsqrt(jnp.mean(centered * centered, axis=1, keepdims=True) + 1e-05)
    inv_std[...] = jnp.broadcast_to(inverse, inv_std.shape)
    normed[...] = centered * inverse
    hidden[...] = (normed[...] * gates[...].astype(F32)).astype(BF16)
    part = width // groups
    for d, ref in enumerate(slices):
        at = pl.multiple_of((place_ref[1] ^ d) * part, 128)
        ref[...] = hidden[:, pl.ds(at, part)]


def mix_kernel(grad_hidden, gates, normed, inv_std, grad_gates, grad_mix):
    gh = grad_hidden[...]
    norm = normed[...]
    grad_gates[...] = (gh * norm).astype(BF16)
    grad_norm = gh * gates[...].astype(F32)
    grad_mix[...] = (
        (
            grad_norm
            - jnp.mean(grad_norm, axis=1, keepdims=True)
            - norm * jnp.mean(grad_norm * norm, axis=1, keepdims=True)
        )
        * inv_std[:, :1]
    ).astype(BF16)


def query_kernel(k0, k1, k2, v0, v1, v2, slope0, slope1, slope2, grad_mix, hidden, w, output, grad_queries):
    rows, width = k0.shape
    size = width // HEADS
    output[...] = dot(hidden[...], w[...]).astype(BF16)
    parts = ((k0, v0, slope0), (k1, v1, slope1), (k2, v2, slope2))
    for h in range(HEADS):
        cols = head_slice(h, size)
        total = jnp.zeros((rows, size), F32)
        for keys, vals, slope in parts:
            grad_attention = dot_nt(grad_mix[:, cols], vals[:, cols])
            grad_scores = (grad_attention * slope[:, cols]).astype(BF16)
            total = total + dot(grad_scores, keys[:, cols])
        grad_queries[:, cols] = total.astype(BF16)


def key_terms(h, mask, k, v, qd, gd):
    size = k.shape[1] // HEADS
    scale = size ** (-0.5)
    cols = head_slice(h, size)
    scores = dot_nt(k[:, cols], qd[:, cols]) * scale
    gate = logistic(scores)
    attention = jnp.where(mask, scores * gate, 0.0).astype(BF16)
    grad_attention = dot_nt(v[:, cols], gd[:, cols])
    slope = jnp.where(mask, silu_slope(scores, gate) * scale, 0.0)
    grad_scores = (grad_attention * slope).astype(BF16)
    return dot(grad_scores, qd[:, cols]), dot(attention, gd[:, cols])


def key_kernel(len_ref, place_ref, k, v, q0, q2, g0, g2, keys_total, values_total):
    rows, width = k.shape
    first = place_ref[0] * rows
    masks = [allowed_block(rows, first + d * rows, first, len_ref, 1) for d in (0, 2)]
    for h in range(HEADS):
        cols = head_slice(h, width // HEADS)
        own = key_terms(h, masks[0], k, v, q0, g0)
        far = key_terms(h, masks[1], k, v, q2, g2)
        keys_total[:, cols] = own[0] + far[0]
        values_total[:, cols] = own[1] + far[1]


def key_end_kernel(len_ref, place_ref, k, v, q1, g1, keys_part, values_part, grad_keys, grad_values):
    rows, width = k.shape
    first = place_ref[0] * rows
    mask = allowed_block(rows, first + rows, first, len_ref, 1)
    for h in range(HEADS):
        cols = head_slice(h, width // HEADS)
        near = key_terms(h, mask, k, v, q1, g1)
        grad_keys[:, cols] = (keys_part[:, cols] + near[0]).astype(BF16)
        grad_values[:, cols] = (values_part[:, cols] + near[1]).astype(BF16)


def weight_kernel(groups, place_ref, *refs):
    hidden = jnp.concatenate([ref[...] for ref in refs[:groups]], axis=0)
    grads = jnp.concatenate([ref[...] for ref in refs[groups : 2 * groups]], axis=0)
    own = refs[2 * groups]
    sends = refs[2 * groups + 1 : -1]
    total = refs[-1]
    total[...] = dot_tn(hidden, grads)
    if not sends:
        own[...] = total[...]
        return
    rows = own.shape[0]
    corner = place_ref[0] & len(sends)
    own[...] = total[pl.ds(pl.multiple_of(corner * rows, rows), rows), :]
    for e, ref in enumerate(sends):
        at = pl.multiple_of((corner ^ (e + 1)) * rows, rows)
        ref[...] = total[pl.ds(at, rows), :].astype(BF16)


def corner_kernel(own, *refs):
    got, narrow = refs[:-1], refs[-1]
    acc = own[...]
    for ref in got:
        acc = acc + ref[...].astype(F32)
    narrow[...] = acc.astype(BF16)


def pair_kernel(scale, mine, other, both):
    both[...] = ((mine[...].astype(F32) + other[...].astype(F32)) * scale).astype(BF16)


def place_kernel(corners, place_ref, *refs):
    shares, (out, wide, sems) = refs[:corners], refs[corners:]
    rows = shares[0].shape[0]
    corner = place_ref[0] & (corners - 1)
    moves = []
    for e, ref in enumerate(shares):
        wide[e] = ref[...].astype(F32)
        at = pl.multiple_of((corner ^ e) * rows, rows)
        moves.append(pltpu.make_async_copy(wide.at[e], out.at[pl.ds(at, rows), :], sems.at[e]))
        moves[-1].start()
    for move in moves:
        move.wait()


def xor_route(size, mask):
    return [(i, i ^ mask) for i in range(size)]


def shifted(block, distance):
    count = lax.axis_size("seq")
    route = [(i, i + distance) for i in range(count) if 0 <= i + distance < count]
    return lax.ppermute(block, "seq", route)


def swapped(block, axis, mask):
    return lax.ppermute(block, axis, xor_route(lax.axis_size(axis), mask))


def after(value, *others):
    return lax.optimization_barrier((value, *others))[0]


def on_device(queries, keys, values, gates, out_grad, w_out, hist_lengths):
    rows, width = queries.shape[1:]
    seq = lax.axis_size("seq")
    batch = lax.axis_size("batch")
    seq_at = lax.axis_index("seq")
    place = jnp.stack([seq_at, lax.axis_index("batch")]).astype(jnp.int32)
    scalars = (hist_lengths, place)
    even = (seq_at & 1) == 0
    full = jax.ShapeDtypeStruct((rows, width), BF16)
    near = kept((rows, width), BF16)
    wide = kept((rows, width), F32)
    block_flops = 2 * rows * rows * width
    proj_flops = 2 * rows * width * width
    part = width // batch
    hbm = pl.BlockSpec(memory_space=pltpu.HBM)

    k2 = shifted(keys[0], 2)
    v2 = shifted(values[0], 2)
    q, k, v, mixed_own, slope0 = call(
        own_kernel,
        [near, near, near, wide, wide],
        scalars,
        (in_hbm(queries[0]), in_hbm(keys[0]), in_hbm(values[0])),
        2 * block_flops,
        [pltpu.SemaphoreType.DMA((3,))],
        [hbm] * 3,
    )
    passed = jnp.where(even, k, k2)
    k1 = swapped(passed, "seq", 1)
    v1 = shifted(values[0], 1)
    grad, w, gate, grad_hidden = call(
        project_kernel,
        [near, kept(w_out.shape, BF16), near, wide],
        (),
        (in_hbm(after(out_grad[0], passed)), in_hbm(w_out), in_hbm(gates[0])),
        proj_flops,
        [pltpu.SemaphoreType.DMA((CHUNKS + 2,))],
        [hbm] * 3,
    )
    grads = [grad]
    for d in range(1, batch):
        low = d & -d
        source = after(out_grad[0], passed) if d == 1 else out_grad[0] if d == low else grads[d ^ low]
        grads.append(swapped(source, "batch", low))
    mixed_far, slope2 = call(
        second_kernel, [wide, wide], scalars, (after(q, v1, grad_hidden), k2, v2, mixed_own), 2 * block_flops
    )
    q2 = shifted(after(q, grads[2]), -2)
    passed_q = jnp.where(even, q2, q)
    q1 = swapped(passed_q, "seq", 1)
    attention1, slope1 = call(first_kernel, [near, wide], scalars, (after(q, v1), k1), block_flops)
    hidden, normed, inv_std, *slices = call(
        functools.partial(forward_kernel, batch),
        [near, wide, kept((rows, 128), F32)] + [kept((rows, part), BF16)] * batch,
        (place,),
        (attention1, v1, after(mixed_far, grads[1]), gate),
        block_flops,
        [pltpu.VMEM((rows, width), F32)],
    )
    hiddens = [slices[0]] + [swapped(slices[d], "batch", d) for d in range(1, batch)]
    grad_gates, grad_mix = call(
        mix_kernel, [full, near], (), (grad_hidden, gate, normed, inv_std), block_flops // 4
    )
    g2 = shifted(grad_mix, -2)
    g2_late = g2

    corners = 4
    direct = seq == 2 * corners
    rows_w = part // corners if direct else part
    share = kept((rows_w, width), BF16)
    scale = (rows * seq * batch) ** (-0.5)
    own, *sends = call(
        functools.partial(weight_kernel, batch),
        [kept((rows_w, width), F32)] + [share] * (corners - 1 if direct else 0),
        (place,),
        (*hiddens, *grads),
        proj_flops,
        [pltpu.VMEM((part, width), F32)],
    )
    keys_part, values_part = call(
        key_kernel,
        [wide, wide],
        scalars,
        (k, after(v, own), q, q2, grad_mix, g2),
        8 * block_flops,
    )
    if direct:
        got = [swapped(s, "seq", e + 1) for e, s in enumerate(sends)]
        (mine,) = call(corner_kernel, [share], (), (after(own, keys_part), *got), own.size * 4)
        other = swapped(mine, "seq", corners)
        g2_late = after(g2, mine)
    else:
        mine = own
    output, grad_queries = call(
        query_kernel,
        [full, full],
        (),
        (k, k1, k2, v, v1, v2, slope0, slope1, slope2, grad_mix, after(hidden, mine), w),
        proj_flops + 6 * block_flops,
    )
    g1 = swapped(jnp.where(even, g2_late, grad_mix), "seq", 1)
    if direct:
        (both,) = call(
            functools.partial(pair_kernel, scale),
            [share],
            (),
            (after(mine, output), other),
            own.size * 2,
        )
    else:
        both = own
    grad_keys, grad_values = call(
        key_end_kernel,
        [full, full],
        scalars,
        (k, after(v, both), q1, g1, keys_part, values_part),
        4 * block_flops,
    )
    if direct:
        shares = [after(both, grad_keys)] + [swapped(both, "seq", e) for e in range(1, corners)]
        (grad_weight,) = call(
            functools.partial(place_kernel, corners),
            [jax.ShapeDtypeStruct((part, width), F32)],
            (place,),
            shares,
            part * width,
            [pltpu.VMEM((corners, rows_w, width), F32), pltpu.SemaphoreType.DMA((corners,))],
            out_space=hbm,
        )
    else:
        grad_weight = lax.psum(own, "seq") * scale
    return (
        output[None],
        grad_queries[None],
        grad_keys[None],
        grad_values[None],
        grad_gates[None],
        grad_weight,
    )


def solution(mesh):
    token = P("batch", "seq", None)
    return jax.shard_map(
        on_device,
        mesh=mesh,
        in_specs=(token, token, token, token, token, P(), P("batch", None)),
        out_specs=(token, token, token, token, token, P("batch", None)),
        check_vma=False,
    )
```

```python
import functools
import math

import jax
import jax.numpy as jnp
from jax import lax
from jax.experimental import pallas as pl
from jax.experimental.pallas import tpu as pltpu
from jax.sharding import PartitionSpec as P

HEADS = 8
WINDOW = 256
REACH = 2
CHUNKS = 4

VMEM = pl.BlockSpec(memory_space=pltpu.VMEM)
SMEM = pl.BlockSpec(memory_space=pltpu.SMEM)
F32 = jnp.float32
BF16 = jnp.bfloat16
NT = (((1,), (1,)), ((), ()))
TN = (((0,), (0,)), ((), ()))


def dot(a, b):
    return jnp.dot(a, b, preferred_element_type=F32)


def dot_nt(a, b):
    return lax.dot_general(a, b, NT, preferred_element_type=F32)


def dot_tn(a, b):
    return lax.dot_general(a, b, TN, preferred_element_type=F32)


def logistic(scores):
    return 0.5 * jnp.tanh(0.5 * scores) + 0.5


def silu_slope(scores, gate):
    return gate * (1.0 + scores * (1.0 - gate))


def start_of(positions, len_ref):
    total = jnp.zeros_like(positions)
    end = jnp.int32(0)
    for k in range(len_ref.shape[1]):
        length = len_ref[0, k]
        end = end + length
        total = total + jnp.where(positions >= end, length, 0)
    return total


def allowed_block(rows, first_query, first_key, len_ref, query_dim):
    shape = (rows, rows)
    query_pos = first_query + lax.broadcasted_iota(jnp.int32, shape, query_dim)
    key_pos = first_key + lax.broadcasted_iota(jnp.int32, shape, 1 - query_dim)
    start = start_of(query_pos, len_ref)
    return (key_pos >= start) & (key_pos <= query_pos) & (key_pos > query_pos - WINDOW)


def head_slice(h, width):
    return slice(h * width, (h + 1) * width)


def kept(shape, dtype):
    return pltpu.VMEM(shape, dtype)


def in_hbm(array):
    return pltpu.with_memory_space_constraint(array, pltpu.HBM)


def nbytes(arrays):
    return sum(math.prod(a.shape) * jnp.dtype(a.dtype).itemsize for a in arrays)


def call(kernel, outs, scalars, arrays, flops, scratch=(), spaces=None, out_space=VMEM, aliases={}):
    return pl.pallas_call(
        kernel,
        out_shape=outs,
        in_specs=[SMEM] * len(scalars) + (spaces or [VMEM] * len(arrays)),
        out_specs=[out_space] * len(outs),
        scratch_shapes=list(scratch),
        input_output_aliases=aliases,
        cost_estimate=pl.CostEstimate(
            flops=flops, bytes_accessed=nbytes([*arrays, *outs]), transcendentals=0
        ),
        compiler_params=pltpu.CompilerParams(vmem_limit_bytes=32 * 1024 * 1024),
    )(*scalars, *arrays)


def own_kernel(len_ref, place_ref, q_in, k_in, v_in, q, k, v, mixed, slope, sems):
    moves = [
        pltpu.make_async_copy(src, dst, sems.at[i])
        for i, (src, dst) in enumerate(((q_in, q), (k_in, k), (v_in, v)))
    ]
    for move in moves:
        move.start()
    rows, width = q.shape
    size = width // HEADS
    first = place_ref[0] * rows
    allowed = allowed_block(rows, first, first, len_ref, 0)
    for move in moves:
        move.wait()
    for h in range(HEADS):
        cols = head_slice(h, size)
        attention = block_scores(h, allowed, q, k, slope)
        mixed[:, cols] = dot(attention, v[:, cols])


def project_kernel(grad_in, w_in, gate_in, grad, w, gates, grad_hidden, sems):
    width = w.shape[0]
    part = width // CHUNKS
    moves = [pltpu.make_async_copy(grad_in, grad, sems.at[0])]
    for c in range(CHUNKS):
        here = pl.ds(c * part, part)
        moves.append(pltpu.make_async_copy(w_in.at[here, :], w.at[here, :], sems.at[c + 1]))
    moves.append(pltpu.make_async_copy(gate_in, gates, sems.at[CHUNKS + 1]))
    for move in moves:
        move.start()
    moves[0].wait()
    for c in range(CHUNKS):
        moves[c + 1].wait()
        here = slice(c * part, (c + 1) * part)
        grad_hidden[:, here] = dot_nt(grad[...], w[here, :])
    moves[-1].wait()


def block_scores(h, allowed, q, keys, slope):
    size = q.shape[1] // HEADS
    scale = size ** (-0.5)
    cols = head_slice(h, size)
    scores = dot_nt(q[:, cols], keys[:, cols]) * scale
    gate = logistic(scores)
    slope[:, cols] = jnp.where(allowed, silu_slope(scores, gate) * scale, 0.0)
    return jnp.where(allowed, scores * gate, 0.0).astype(BF16)


def second_kernel(len_ref, place_ref, q, keys, vals, mixed_own, mixed, slope):
    rows, width = q.shape
    size = width // HEADS
    first = place_ref[0] * rows
    allowed = allowed_block(rows, first, first - 2 * rows, len_ref, 0)
    for h in range(HEADS):
        cols = head_slice(h, size)
        attention = block_scores(h, allowed, q, keys, slope)
        mixed[:, cols] = mixed_own[:, cols] + dot(attention, vals[:, cols])


def first_kernel(len_ref, place_ref, q, keys, attention, slope):
    rows, width = q.shape
    size = width // HEADS
    first = place_ref[0] * rows
    allowed = allowed_block(rows, first, first - rows, len_ref, 0)
    for h in range(HEADS):
        attention[:, head_slice(h, size)] = block_scores(h, allowed, q, keys, slope)


def forward_kernel(groups, place_ref, attention, vals, mixed_far, gates, hidden, normed, inv_std, *rest):
    slices, mixed = rest[:-1], rest[-1]
    rows, width = vals.shape
    size = width // HEADS
    for h in range(HEADS):
        cols = head_slice(h, size)
        mixed[:, cols] = mixed_far[:, cols] + dot(attention[:, cols], vals[:, cols])
    values = mixed[...]
    centered = values - jnp.mean(values, axis=1, keepdims=True)
    inverse = lax.rsqrt(jnp.mean(centered * centered, axis=1, keepdims=True) + 1e-05)
    inv_std[...] = jnp.broadcast_to(inverse, inv_std.shape)
    normed[...] = centered * inverse
    hidden[...] = (normed[...] * gates[...].astype(F32)).astype(BF16)
    part = width // groups
    for d, ref in enumerate(slices):
        at = pl.multiple_of((place_ref[1] // 2 ^ d) * part, 128)
        ref[...] = hidden[:, pl.ds(at, part)]


def mix_kernel(grad_hidden, gates, normed, inv_std, grad_gates, grad_mix):
    gh = grad_hidden[...]
    norm = normed[...]
    grad_gates[...] = (gh * norm).astype(BF16)
    grad_norm = gh * gates[...].astype(F32)
    grad_mix[...] = (
        (
            grad_norm
            - jnp.mean(grad_norm, axis=1, keepdims=True)
            - norm * jnp.mean(grad_norm * norm, axis=1, keepdims=True)
        )
        * inv_std[:, :1]
    ).astype(BF16)


def query_kernel(k0, k1, k2, v0, v1, v2, slope0, slope1, slope2, grad_mix, hidden, w, output, grad_queries):
    rows, width = k0.shape
    size = width // HEADS
    output[...] = dot(hidden[...], w[...]).astype(BF16)
    parts = ((k0, v0, slope0), (k1, v1, slope1), (k2, v2, slope2))
    for h in range(HEADS):
        cols = head_slice(h, size)
        total = jnp.zeros((rows, size), F32)
        for keys, vals, slope in parts:
            grad_attention = dot_nt(grad_mix[:, cols], vals[:, cols])
            grad_scores = (grad_attention * slope[:, cols]).astype(BF16)
            total = total + dot(grad_scores, keys[:, cols])
        grad_queries[:, cols] = total.astype(BF16)


def key_terms(h, mask, k, v, qd, gd):
    size = k.shape[1] // HEADS
    scale = size ** (-0.5)
    cols = head_slice(h, size)
    scores = dot_nt(k[:, cols], qd[:, cols]) * scale
    gate = logistic(scores)
    attention = jnp.where(mask, scores * gate, 0.0).astype(BF16)
    grad_attention = dot_nt(v[:, cols], gd[:, cols])
    slope = jnp.where(mask, silu_slope(scores, gate) * scale, 0.0)
    grad_scores = (grad_attention * slope).astype(BF16)
    return dot(grad_scores, qd[:, cols]), dot(attention, gd[:, cols])


def key_kernel(len_ref, place_ref, k, v, q0, q2, g0, g2, keys_total, values_total):
    rows, width = k.shape
    first = place_ref[0] * rows
    masks = [allowed_block(rows, first + d * rows, first, len_ref, 1) for d in (0, 2)]
    for h in range(HEADS):
        cols = head_slice(h, width // HEADS)
        own = key_terms(h, masks[0], k, v, q0, g0)
        far = key_terms(h, masks[1], k, v, q2, g2)
        keys_total[:, cols] = own[0] + far[0]
        values_total[:, cols] = own[1] + far[1]


def key_end_kernel(len_ref, place_ref, k, v, q1, g1, keys_part, values_part, grad_keys, grad_values):
    rows, width = k.shape
    first = place_ref[0] * rows
    mask = allowed_block(rows, first + rows, first, len_ref, 1)
    for h in range(HEADS):
        cols = head_slice(h, width // HEADS)
        near = key_terms(h, mask, k, v, q1, g1)
        grad_keys[:, cols] = (keys_part[:, cols] + near[0]).astype(BF16)
        grad_values[:, cols] = (values_part[:, cols] + near[1]).astype(BF16)


def weight_kernel(groups, place_ref, *refs):
    hidden = jnp.concatenate([ref[...] for ref in refs[:groups]], axis=0)
    grads = jnp.concatenate([ref[...] for ref in refs[groups : 2 * groups]], axis=0)
    own, send, total = refs[2 * groups :]
    rows = own.shape[0]
    side = place_ref[1] & 1
    total[...] = dot_tn(hidden, grads)
    own[...] = total[pl.ds(pl.multiple_of(side * rows, rows), rows), :]
    send[...] = total[pl.ds(pl.multiple_of((1 - side) * rows, rows), rows), :].astype(BF16)


def join_kernel(corners, place_ref, mine, got, own, *rest):
    if not rest:
        own[...] = mine[...] + got[...].astype(F32)
        return
    sends, total = rest[:-1], rest[-1]
    total[...] = mine[...] + got[...].astype(F32)
    rows = own.shape[0]
    corner = place_ref[0] & (corners - 1)
    own[...] = total[pl.ds(pl.multiple_of(corner * rows, rows), rows), :]
    for e, ref in enumerate(sends):
        at = pl.multiple_of((corner ^ (e + 1)) * rows, rows)
        ref[...] = total[pl.ds(at, rows), :].astype(BF16)


def corner_kernel(own, *refs):
    got, narrow = refs[:-1], refs[-1]
    acc = own[...]
    for ref in got:
        acc = acc + ref[...].astype(F32)
    narrow[...] = acc.astype(BF16)


def pair_kernel(scale, mine, other, both):
    both[...] = ((mine[...].astype(F32) + other[...].astype(F32)) * scale).astype(BF16)


def place_kernel(corners, place_ref, *refs):
    shares, (out, wide, sems) = refs[:corners], refs[corners:]
    rows = shares[0].shape[0]
    corner = place_ref[0] & (corners - 1)
    moves = []
    for e, ref in enumerate(shares):
        wide[e] = ref[...].astype(F32)
        at = pl.multiple_of((corner ^ e) * rows, rows)
        moves.append(pltpu.make_async_copy(wide.at[e], out.at[pl.ds(at, rows), :], sems.at[e]))
        moves[-1].start()
    for move in moves:
        move.wait()


def xor_route(size, mask):
    return [(i, i ^ mask) for i in range(size)]


def shifted(block, distance):
    count = lax.axis_size("seq")
    route = [(i, i + distance) for i in range(count) if 0 <= i + distance < count]
    return lax.ppermute(block, "seq", route)


def swapped(block, axis, mask):
    return lax.ppermute(block, axis, xor_route(lax.axis_size(axis), mask))


def after(value, *others):
    return lax.optimization_barrier((value, *others))[0]


def on_device(queries, keys, values, gates, out_grad, w_out, hist_lengths):
    rows, width = queries.shape[1:]
    seq = lax.axis_size("seq")
    batch = lax.axis_size("batch")
    seq_at = lax.axis_index("seq")
    place = jnp.stack([seq_at, lax.axis_index("batch")]).astype(jnp.int32)
    scalars = (hist_lengths, place)
    even = (seq_at & 1) == 0
    full = jax.ShapeDtypeStruct((rows, width), BF16)
    near = kept((rows, width), BF16)
    wide = kept((rows, width), F32)
    block_flops = 2 * rows * rows * width
    proj_flops = 2 * rows * width * width
    part = width // batch
    hbm = pl.BlockSpec(memory_space=pltpu.HBM)

    k2 = shifted(keys[0], 2)
    v2 = shifted(values[0], 2)
    passed = jnp.where(even, keys[0], k2)
    k1 = swapped(passed, "seq", 1)
    q, k, v, mixed_own, slope0 = call(
        own_kernel,
        [near, near, near, wide, wide],
        scalars,
        (in_hbm(after(queries[0], passed)), in_hbm(keys[0]), in_hbm(values[0])),
        2 * block_flops,
        [pltpu.SemaphoreType.DMA((3,))],
        [hbm] * 3,
    )
    v1 = shifted(values[0], 1)
    grad, w, gate, grad_hidden = call(
        project_kernel,
        [near, kept(w_out.shape, BF16), near, wide],
        (),
        (in_hbm(after(out_grad[0], mixed_own)), in_hbm(w_out), in_hbm(gates[0])),
        proj_flops,
        [pltpu.SemaphoreType.DMA((CHUNKS + 2,))],
        [hbm] * 3,
    )
    pairs = batch // 2
    grads = [grad] + [swapped(out_grad[0], "batch", 2 * d) for d in range(1, pairs)]
    mixed_far, slope2 = call(
        second_kernel, [wide, wide], scalars, (after(q, grad_hidden), k2, v2, mixed_own), 2 * block_flops
    )
    q2 = shifted(after(q, grad_hidden), -2)
    passed_q = jnp.where(even, q2, q)
    q1 = swapped(passed_q, "seq", 1)
    attention1, slope1 = call(first_kernel, [near, wide], scalars, (after(q, mixed_far), k1), block_flops)
    hidden, normed, inv_std, *slices = call(
        functools.partial(forward_kernel, pairs),
        [near, wide, kept((rows, 128), F32)] + [kept((rows, 2 * part), BF16)] * pairs,
        (place,),
        (attention1, v1, after(mixed_far, grads[1]), gate),
        block_flops,
        [pltpu.VMEM((rows, width), F32)],
    )
    hiddens = [slices[0]] + [swapped(slices[d], "batch", 2 * d) for d in range(1, pairs)]
    grad_gates, grad_mix = call(
        mix_kernel, [full, near], (), (grad_hidden, gate, normed, inv_std), block_flops // 4
    )
    g2 = shifted(grad_mix, -2)
    g2_late = g2

    corners = 4
    direct = seq == 2 * corners
    rows_w = part // corners if direct else part
    share = kept((rows_w, width), BF16)
    scale = (rows * seq * batch) ** (-0.5)
    mine, send = call(
        functools.partial(weight_kernel, pairs),
        [kept((part, width), F32), kept((part, width), BF16)],
        (place,),
        (after(hiddens[0], passed_q), *hiddens[1:], *grads),
        proj_flops,
        [pltpu.VMEM((2 * part, width), F32)],
    )
    own, *sends = call(
        functools.partial(join_kernel, corners),
        [kept((rows_w, width), F32)] + [share] * (corners - 1 if direct else 0),
        (place,),
        (mine, swapped(send, "batch", 1)),
        part * width,
        [pltpu.VMEM((part, width), F32)] if direct else [],
    )
    keys_part, values_part = call(
        key_kernel,
        [wide, wide],
        scalars,
        (k, after(v, own), q, q2, grad_mix, g2),
        8 * block_flops,
    )
    if direct:
        got = [swapped(s, "seq", e + 1) for e, s in enumerate(sends)]
        (mine,) = call(corner_kernel, [share], (), (after(own, keys_part), *got), own.size * 4)
        other = swapped(mine, "seq", corners)
        g2_late = after(g2, mine)
    else:
        mine = own
    output, grad_queries = call(
        query_kernel,
        [full, full],
        (),
        (k, k1, k2, v, v1, v2, slope0, slope1, slope2, grad_mix, after(hidden, mine), w),
        proj_flops + 6 * block_flops,
    )
    g1 = swapped(jnp.where(even, g2_late, grad_mix), "seq", 1)
    if direct:
        (both,) = call(
            functools.partial(pair_kernel, scale),
            [share],
            (),
            (after(mine, output), other),
            own.size * 2,
        )
    else:
        both = own
    grad_keys, grad_values = call(
        key_end_kernel,
        [full, full],
        scalars,
        (k, after(v, both), q1, g1, keys_part, values_part),
        4 * block_flops,
    )
    if direct:
        shares = [after(both, grad_keys)] + [swapped(both, "seq", e) for e in range(1, corners)]
        (grad_weight,) = call(
            functools.partial(place_kernel, corners),
            [jax.ShapeDtypeStruct((part, width), F32)],
            (place,),
            shares,
            part * width,
            [pltpu.VMEM((corners, rows_w, width), F32), pltpu.SemaphoreType.DMA((corners,))],
            out_space=hbm,
        )
    else:
        grad_weight = lax.psum(own, "seq") * scale
    return (
        output[None],
        grad_queries[None],
        grad_keys[None],
        grad_values[None],
        grad_gates[None],
        grad_weight,
    )


def solution(mesh):
    token = P("batch", "seq", None)
    return jax.shard_map(
        on_device,
        mesh=mesh,
        in_specs=(token, token, token, token, token, P(), P("batch", None)),
        out_specs=(token, token, token, token, token, P("batch", None)),
        check_vma=False,
    )
```

```python
import functools
import math

import jax
import jax.numpy as jnp
from jax import lax
from jax.experimental import pallas as pl
from jax.experimental.pallas import tpu as pltpu
from jax.sharding import PartitionSpec as P

HEADS = 8
WINDOW = 256
REACH = 2
CHUNKS = 4

VMEM = pl.BlockSpec(memory_space=pltpu.VMEM)
SMEM = pl.BlockSpec(memory_space=pltpu.SMEM)
F32 = jnp.float32
BF16 = jnp.bfloat16
NT = (((1,), (1,)), ((), ()))
TN = (((0,), (0,)), ((), ()))


def dot(a, b):
    return jnp.dot(a, b, preferred_element_type=F32)


def dot_nt(a, b):
    return lax.dot_general(a, b, NT, preferred_element_type=F32)


def dot_tn(a, b):
    return lax.dot_general(a, b, TN, preferred_element_type=F32)


def logistic(scores):
    return 0.5 * jnp.tanh(0.5 * scores) + 0.5


def silu_slope(scores, gate):
    return gate * (1.0 + scores * (1.0 - gate))


def start_of(positions, len_ref):
    total = jnp.zeros_like(positions)
    end = jnp.int32(0)
    for k in range(len_ref.shape[1]):
        length = len_ref[0, k]
        end = end + length
        total = total + jnp.where(positions >= end, length, 0)
    return total


def allowed_block(rows, first_query, first_key, len_ref, query_dim):
    shape = (rows, rows)
    query_pos = first_query + lax.broadcasted_iota(jnp.int32, shape, query_dim)
    key_pos = first_key + lax.broadcasted_iota(jnp.int32, shape, 1 - query_dim)
    start = start_of(query_pos, len_ref)
    return (key_pos >= start) & (key_pos <= query_pos) & (key_pos > query_pos - WINDOW)


def head_slice(h, width):
    return slice(h * width, (h + 1) * width)


def kept(shape, dtype):
    return pltpu.VMEM(shape, dtype)


def in_hbm(array):
    return pltpu.with_memory_space_constraint(array, pltpu.HBM)


def nbytes(arrays):
    return sum(math.prod(a.shape) * jnp.dtype(a.dtype).itemsize for a in arrays)


def call(kernel, outs, scalars, arrays, flops, scratch=(), spaces=None, out_space=VMEM, aliases={}):
    return pl.pallas_call(
        kernel,
        out_shape=outs,
        in_specs=[SMEM] * len(scalars) + (spaces or [VMEM] * len(arrays)),
        out_specs=[out_space] * len(outs),
        scratch_shapes=list(scratch),
        input_output_aliases=aliases,
        cost_estimate=pl.CostEstimate(
            flops=flops, bytes_accessed=nbytes([*arrays, *outs]), transcendentals=0
        ),
        compiler_params=pltpu.CompilerParams(vmem_limit_bytes=32 * 1024 * 1024),
    )(*scalars, *arrays)


def own_kernel(
    len_ref, place_ref, q_in, k_in, v_in, grad_in, w_in, gate_in,
    q, k, v, grad, w, gates, mixed, grad_hidden, slope, sems,
):
    pairs = ((q_in, q), (k_in, k), (v_in, v), (grad_in, grad), (gate_in, gates))
    moves = [
        pltpu.make_async_copy(src, dst, sems.at[i]) for i, (src, dst) in enumerate(pairs)
    ]
    rows, width = q.shape
    part = width // CHUNKS
    parts = []
    for c in range(CHUNKS):
        here = pl.ds(c * part, part)
        parts.append(
            pltpu.make_async_copy(w_in.at[here, :], w.at[here, :], sems.at[len(pairs) + c])
        )
    for move in moves[:4] + parts + moves[4:]:
        move.start()
    size = width // HEADS
    first = place_ref[0] * rows
    allowed = allowed_block(rows, first, first, len_ref, 0)
    for move in moves[:3]:
        move.wait()
    for h in range(HEADS):
        cols = head_slice(h, size)
        attention = block_scores(h, allowed, q, k, slope)
        mixed[:, cols] = dot(attention, v[:, cols])
    moves[3].wait()
    for c in range(CHUNKS):
        parts[c].wait()
        here = slice(c * part, (c + 1) * part)
        grad_hidden[:, here] = dot_nt(grad[...], w[here, :])
    moves[4].wait()


def block_scores(h, allowed, q, keys, slope):
    size = q.shape[1] // HEADS
    scale = size ** (-0.5)
    cols = head_slice(h, size)
    scores = dot_nt(q[:, cols], keys[:, cols]) * scale
    gate = logistic(scores)
    slope[:, cols] = jnp.where(allowed, silu_slope(scores, gate) * scale, 0.0)
    return jnp.where(allowed, scores * gate, 0.0).astype(BF16)


def second_kernel(len_ref, place_ref, q, keys, vals, mixed_own, mixed, slope):
    rows, width = q.shape
    size = width // HEADS
    first = place_ref[0] * rows
    allowed = allowed_block(rows, first, first - 2 * rows, len_ref, 0)
    for h in range(HEADS):
        cols = head_slice(h, size)
        attention = block_scores(h, allowed, q, keys, slope)
        mixed[:, cols] = mixed_own[:, cols] + dot(attention, vals[:, cols])


def first_kernel(len_ref, place_ref, q, keys, attention, slope):
    rows, width = q.shape
    size = width // HEADS
    first = place_ref[0] * rows
    allowed = allowed_block(rows, first, first - rows, len_ref, 0)
    for h in range(HEADS):
        attention[:, head_slice(h, size)] = block_scores(h, allowed, q, keys, slope)


def forward_kernel(groups, place_ref, attention, vals, mixed_far, gates, hidden, normed, inv_std, *rest):
    slices, mixed = rest[:-1], rest[-1]
    rows, width = vals.shape
    size = width // HEADS
    for h in range(HEADS):
        cols = head_slice(h, size)
        mixed[:, cols] = mixed_far[:, cols] + dot(attention[:, cols], vals[:, cols])
    values = mixed[...]
    centered = values - jnp.mean(values, axis=1, keepdims=True)
    inverse = lax.rsqrt(jnp.mean(centered * centered, axis=1, keepdims=True) + 1e-05)
    inv_std[...] = jnp.broadcast_to(inverse, inv_std.shape)
    normed[...] = centered * inverse
    hidden[...] = (normed[...] * gates[...].astype(F32)).astype(BF16)
    part = width // groups
    for d, ref in enumerate(slices):
        at = pl.multiple_of((place_ref[1] ^ d) * part, 128)
        ref[...] = hidden[:, pl.ds(at, part)]


def mix_kernel(grad_hidden, gates, normed, inv_std, grad_gates, grad_mix):
    gh = grad_hidden[...]
    norm = normed[...]
    grad_gates[...] = (gh * norm).astype(BF16)
    grad_norm = gh * gates[...].astype(F32)
    grad_mix[...] = (
        (
            grad_norm
            - jnp.mean(grad_norm, axis=1, keepdims=True)
            - norm * jnp.mean(grad_norm * norm, axis=1, keepdims=True)
        )
        * inv_std[:, :1]
    ).astype(BF16)


def query_kernel(k0, k1, k2, v0, v1, v2, slope0, slope1, slope2, grad_mix, hidden, w, output, grad_queries):
    rows, width = k0.shape
    size = width // HEADS
    output[...] = dot(hidden[...], w[...]).astype(BF16)
    parts = ((k0, v0, slope0), (k1, v1, slope1), (k2, v2, slope2))
    for h in range(HEADS):
        cols = head_slice(h, size)
        total = jnp.zeros((rows, size), F32)
        for keys, vals, slope in parts:
            grad_attention = dot_nt(grad_mix[:, cols], vals[:, cols])
            grad_scores = (grad_attention * slope[:, cols]).astype(BF16)
            total = total + dot(grad_scores, keys[:, cols])
        grad_queries[:, cols] = total.astype(BF16)


def key_terms(h, mask, k, v, qd, gd):
    size = k.shape[1] // HEADS
    scale = size ** (-0.5)
    cols = head_slice(h, size)
    scores = dot_nt(k[:, cols], qd[:, cols]) * scale
    gate = logistic(scores)
    attention = jnp.where(mask, scores * gate, 0.0).astype(BF16)
    grad_attention = dot_nt(v[:, cols], gd[:, cols])
    slope = jnp.where(mask, silu_slope(scores, gate) * scale, 0.0)
    grad_scores = (grad_attention * slope).astype(BF16)
    return dot(grad_scores, qd[:, cols]), dot(attention, gd[:, cols])


def key_kernel(len_ref, place_ref, k, v, q0, q2, g0, g2, keys_total, values_total):
    rows, width = k.shape
    first = place_ref[0] * rows
    masks = [allowed_block(rows, first + d * rows, first, len_ref, 1) for d in (0, 2)]
    for h in range(HEADS):
        cols = head_slice(h, width // HEADS)
        own = key_terms(h, masks[0], k, v, q0, g0)
        far = key_terms(h, masks[1], k, v, q2, g2)
        keys_total[:, cols] = own[0] + far[0]
        values_total[:, cols] = own[1] + far[1]


def key_end_kernel(len_ref, place_ref, k, v, q1, g1, keys_part, values_part, grad_keys, grad_values):
    rows, width = k.shape
    first = place_ref[0] * rows
    mask = allowed_block(rows, first + rows, first, len_ref, 1)
    for h in range(HEADS):
        cols = head_slice(h, width // HEADS)
        near = key_terms(h, mask, k, v, q1, g1)
        grad_keys[:, cols] = (keys_part[:, cols] + near[0]).astype(BF16)
        grad_values[:, cols] = (values_part[:, cols] + near[1]).astype(BF16)


def weight_kernel(groups, place_ref, *refs):
    hidden = jnp.concatenate([ref[...] for ref in refs[:groups]], axis=0)
    grads = jnp.concatenate([ref[...] for ref in refs[groups : 2 * groups]], axis=0)
    own = refs[2 * groups]
    sends = refs[2 * groups + 1 : -1]
    total = refs[-1]
    total[...] = dot_tn(hidden, grads)
    if not sends:
        own[...] = total[...]
        return
    rows = own.shape[0]
    corner = place_ref[0] & len(sends)
    own[...] = total[pl.ds(pl.multiple_of(corner * rows, rows), rows), :]
    for e, ref in enumerate(sends):
        at = pl.multiple_of((corner ^ (e + 1)) * rows, rows)
        ref[...] = total[pl.ds(at, rows), :].astype(BF16)


def corner_kernel(own, *refs):
    got, narrow = refs[:-1], refs[-1]
    acc = own[...]
    for ref in got:
        acc = acc + ref[...].astype(F32)
    narrow[...] = acc.astype(BF16)


def pair_kernel(scale, mine, other, both):
    both[...] = ((mine[...].astype(F32) + other[...].astype(F32)) * scale).astype(BF16)


def place_kernel(corners, place_ref, *refs):
    shares, (out, wide, sems) = refs[:corners], refs[corners:]
    rows = shares[0].shape[0]
    corner = place_ref[0] & (corners - 1)
    moves = []
    for e, ref in enumerate(shares):
        wide[e] = ref[...].astype(F32)
        at = pl.multiple_of((corner ^ e) * rows, rows)
        moves.append(pltpu.make_async_copy(wide.at[e], out.at[pl.ds(at, rows), :], sems.at[e]))
        moves[-1].start()
    for move in moves:
        move.wait()


def xor_route(size, mask):
    return [(i, i ^ mask) for i in range(size)]


def shifted(block, distance):
    count = lax.axis_size("seq")
    route = [(i, i + distance) for i in range(count) if 0 <= i + distance < count]
    return lax.ppermute(block, "seq", route)


def swapped(block, axis, mask):
    return lax.ppermute(block, axis, xor_route(lax.axis_size(axis), mask))


def after(value, *others):
    return lax.optimization_barrier((value, *others))[0]


def on_device(queries, keys, values, gates, out_grad, w_out, hist_lengths):
    rows, width = queries.shape[1:]
    seq = lax.axis_size("seq")
    batch = lax.axis_size("batch")
    seq_at = lax.axis_index("seq")
    place = jnp.stack([seq_at, lax.axis_index("batch")]).astype(jnp.int32)
    scalars = (hist_lengths, place)
    even = (seq_at & 1) == 0
    full = jax.ShapeDtypeStruct((rows, width), BF16)
    near = kept((rows, width), BF16)
    wide = kept((rows, width), F32)
    block_flops = 2 * rows * rows * width
    proj_flops = 2 * rows * width * width
    part = width // batch
    hbm = pl.BlockSpec(memory_space=pltpu.HBM)

    k2 = shifted(keys[0], 2)
    v2 = shifted(values[0], 2)
    passed = jnp.where(even, keys[0], k2)
    k1 = swapped(passed, "seq", 1)
    q, k, v, grad, w, gate, mixed_own, grad_hidden, slope0 = call(
        own_kernel,
        [near, near, near, near, kept(w_out.shape, BF16), near, wide, wide, wide],
        scalars,
        tuple(
            in_hbm(a)
            for a in (after(queries[0], passed), keys[0], values[0], out_grad[0], w_out, gates[0])
        ),
        proj_flops + 2 * block_flops,
        [pltpu.SemaphoreType.DMA((5 + CHUNKS,))],
        [hbm] * 6,
    )
    v1 = shifted(values[0], 1)
    grads = [grad]
    for d in range(1, batch):
        low = d & -d
        source = out_grad[0] if d == 1 else out_grad[0] if d == low else after(grads[d ^ low], grad)
        grads.append(swapped(source, "batch", low))
    mixed_far, slope2 = call(
        second_kernel, [wide, wide], scalars, (after(q, passed), k2, v2, mixed_own), 2 * block_flops
    )
    q2 = shifted(after(queries[0], passed), -2)
    passed_q = jnp.where(even, q2, q)
    q1 = swapped(passed_q, "seq", 1)
    attention1, slope1 = call(first_kernel, [near, wide], scalars, (after(q, mixed_far), k1), block_flops)
    hidden, normed, inv_std, *slices = call(
        functools.partial(forward_kernel, batch),
        [near, wide, kept((rows, 128), F32)] + [kept((rows, part), BF16)] * batch,
        (place,),
        (attention1, v1, after(mixed_far, q2, grads[1]), gate),
        block_flops,
        [pltpu.VMEM((rows, width), F32)],
    )
    hiddens = [slices[0]] + [swapped(slices[d], "batch", d) for d in range(1, batch)]
    grad_gates, grad_mix = call(
        mix_kernel, [full, near], (), (grad_hidden, gate, normed, inv_std), block_flops // 4
    )
    g2 = shifted(grad_mix, -2)
    g2_late = g2

    corners = 4
    direct = seq == 2 * corners
    rows_w = part // corners if direct else part
    share = kept((rows_w, width), BF16)
    scale = (rows * seq * batch) ** (-0.5)
    own, *sends = call(
        functools.partial(weight_kernel, batch),
        [kept((rows_w, width), F32)] + [share] * (corners - 1 if direct else 0),
        (place,),
        (*hiddens, *grads),
        proj_flops,
        [pltpu.VMEM((part, width), F32)],
    )
    keys_part, values_part = call(
        key_kernel,
        [wide, wide],
        scalars,
        (k, after(v, own), q, q2, grad_mix, g2),
        8 * block_flops,
    )
    if direct:
        got = [swapped(s, "seq", e + 1) for e, s in enumerate(sends)]
        (mine,) = call(corner_kernel, [share], (), (after(own, keys_part), *got), own.size * 4)
        other = swapped(mine, "seq", corners)
        g2_late = after(g2, mine)
    else:
        mine = own
    output, grad_queries = call(
        query_kernel,
        [full, full],
        (),
        (k, k1, k2, v, v1, v2, slope0, slope1, slope2, grad_mix, after(hidden, mine), w),
        proj_flops + 6 * block_flops,
    )
    g1 = swapped(jnp.where(even, g2_late, grad_mix), "seq", 1)
    if direct:
        (both,) = call(
            functools.partial(pair_kernel, scale),
            [share],
            (),
            (after(mine, output), other),
            own.size * 2,
        )
    else:
        both = own
    grad_keys, grad_values = call(
        key_end_kernel,
        [full, full],
        scalars,
        (k, after(v, both), q1, g1, keys_part, values_part),
        4 * block_flops,
    )
    if direct:
        shares = [after(both, grad_keys)] + [swapped(both, "seq", e) for e in range(1, corners)]
        (grad_weight,) = call(
            functools.partial(place_kernel, corners),
            [jax.ShapeDtypeStruct((part, width), F32)],
            (place,),
            shares,
            part * width,
            [pltpu.VMEM((corners, rows_w, width), F32), pltpu.SemaphoreType.DMA((corners,))],
            out_space=hbm,
        )
    else:
        grad_weight = lax.psum(own, "seq") * scale
    return (
        output[None],
        grad_queries[None],
        grad_keys[None],
        grad_values[None],
        grad_gates[None],
        grad_weight,
    )


def solution(mesh):
    token = P("batch", "seq", None)
    return jax.shard_map(
        on_device,
        mesh=mesh,
        in_specs=(token, token, token, token, token, P(), P("batch", None)),
        out_specs=(token, token, token, token, token, P("batch", None)),
        check_vma=False,
    )
```

```python
import functools
import math

import jax
import jax.numpy as jnp
from jax import lax
from jax.experimental import pallas as pl
from jax.experimental.pallas import tpu as pltpu
from jax.sharding import PartitionSpec as P

HEADS = 8
WINDOW = 256
REACH = 2
CHUNKS = 4

VMEM = pl.BlockSpec(memory_space=pltpu.VMEM)
SMEM = pl.BlockSpec(memory_space=pltpu.SMEM)
F32 = jnp.float32
BF16 = jnp.bfloat16
NT = (((1,), (1,)), ((), ()))
TN = (((0,), (0,)), ((), ()))


def dot(a, b):
    return jnp.dot(a, b, preferred_element_type=F32)


def dot_nt(a, b):
    return lax.dot_general(a, b, NT, preferred_element_type=F32)


def dot_tn(a, b):
    return lax.dot_general(a, b, TN, preferred_element_type=F32)


def logistic(scores):
    return 0.5 * jnp.tanh(0.5 * scores) + 0.5


def silu_slope(scores, gate):
    return gate * (1.0 + scores * (1.0 - gate))


def start_of(positions, len_ref):
    total = jnp.zeros_like(positions)
    end = jnp.int32(0)
    for k in range(len_ref.shape[1]):
        length = len_ref[0, k]
        end = end + length
        total = total + jnp.where(positions >= end, length, 0)
    return total


def allowed_block(rows, first_query, first_key, len_ref, query_dim):
    shape = (rows, rows)
    query_pos = first_query + lax.broadcasted_iota(jnp.int32, shape, query_dim)
    key_pos = first_key + lax.broadcasted_iota(jnp.int32, shape, 1 - query_dim)
    start = start_of(query_pos, len_ref)
    return (key_pos >= start) & (key_pos <= query_pos) & (key_pos > query_pos - WINDOW)


def head_slice(h, width):
    return slice(h * width, (h + 1) * width)


def kept(shape, dtype):
    return pltpu.VMEM(shape, dtype)


def in_hbm(array):
    return pltpu.with_memory_space_constraint(array, pltpu.HBM)


def nbytes(arrays):
    return sum(math.prod(a.shape) * jnp.dtype(a.dtype).itemsize for a in arrays)


def call(kernel, outs, scalars, arrays, flops, scratch=(), spaces=None, out_space=VMEM, aliases={}):
    return pl.pallas_call(
        kernel,
        out_shape=outs,
        in_specs=[SMEM] * len(scalars) + (spaces or [VMEM] * len(arrays)),
        out_specs=[out_space] * len(outs),
        scratch_shapes=list(scratch),
        input_output_aliases=aliases,
        cost_estimate=pl.CostEstimate(
            flops=flops, bytes_accessed=nbytes([*arrays, *outs]), transcendentals=0
        ),
        compiler_params=pltpu.CompilerParams(vmem_limit_bytes=32 * 1024 * 1024),
    )(*scalars, *arrays)


def own_kernel(
    len_ref, place_ref, q_in, k_in, v_in, grad_in, w_in, gate_in,
    q, k, v, grad, w, gates, mixed, grad_hidden, slope, sems,
):
    pairs = ((q_in, q), (k_in, k), (v_in, v), (grad_in, grad), (gate_in, gates))
    moves = [
        pltpu.make_async_copy(src, dst, sems.at[i]) for i, (src, dst) in enumerate(pairs)
    ]
    rows, width = q.shape
    part = width // CHUNKS
    parts = []
    for c in range(CHUNKS):
        here = pl.ds(c * part, part)
        parts.append(
            pltpu.make_async_copy(w_in.at[here, :], w.at[here, :], sems.at[len(pairs) + c])
        )
    for move in moves[:4] + parts + moves[4:]:
        move.start()
    size = width // HEADS
    first = place_ref[0] * rows
    allowed = allowed_block(rows, first, first, len_ref, 0)
    for move in moves[:3]:
        move.wait()
    for h in range(HEADS):
        cols = head_slice(h, size)
        attention = block_scores(h, allowed, q, k, slope)
        mixed[:, cols] = dot(attention, v[:, cols])
    moves[3].wait()
    for c in range(CHUNKS):
        parts[c].wait()
        here = slice(c * part, (c + 1) * part)
        grad_hidden[:, here] = dot_nt(grad[...], w[here, :])
    moves[4].wait()


def block_scores(h, allowed, q, keys, slope):
    size = q.shape[1] // HEADS
    scale = size ** (-0.5)
    cols = head_slice(h, size)
    scores = dot_nt(q[:, cols], keys[:, cols]) * scale
    gate = logistic(scores)
    slope[:, cols] = jnp.where(allowed, silu_slope(scores, gate) * scale, 0.0)
    return jnp.where(allowed, scores * gate, 0.0).astype(BF16)


def far_kernel(distance, len_ref, place_ref, q, keys, attention, slope):
    rows, width = q.shape
    size = width // HEADS
    first = place_ref[0] * rows
    allowed = allowed_block(rows, first, first - distance * rows, len_ref, 0)
    for h in range(HEADS):
        attention[:, head_slice(h, size)] = block_scores(h, allowed, q, keys, slope)


def forward_kernel(groups, place_ref, attention1, attention2, v1, v2, mixed_own, gates, hidden, normed, inv_std, *rest):
    slices, mixed = rest[:-1], rest[-1]
    rows, width = v1.shape
    size = width // HEADS
    for h in range(HEADS):
        cols = head_slice(h, size)
        mixed[:, cols] = (
            mixed_own[:, cols]
            + dot(attention1[:, cols], v1[:, cols])
            + dot(attention2[:, cols], v2[:, cols])
        )
    values = mixed[...]
    centered = values - jnp.mean(values, axis=1, keepdims=True)
    inverse = lax.rsqrt(jnp.mean(centered * centered, axis=1, keepdims=True) + 1e-05)
    inv_std[...] = jnp.broadcast_to(inverse, inv_std.shape)
    normed[...] = centered * inverse
    hidden[...] = (normed[...] * gates[...].astype(F32)).astype(BF16)
    part = width // groups
    for d, ref in enumerate(slices):
        at = pl.multiple_of((place_ref[1] ^ d) * part, 128)
        ref[...] = hidden[:, pl.ds(at, part)]


def mix_kernel(grad_hidden, gates, normed, inv_std, grad_gates, grad_mix):
    gh = grad_hidden[...]
    norm = normed[...]
    grad_gates[...] = (gh * norm).astype(BF16)
    grad_norm = gh * gates[...].astype(F32)
    grad_mix[...] = (
        (
            grad_norm
            - jnp.mean(grad_norm, axis=1, keepdims=True)
            - norm * jnp.mean(grad_norm * norm, axis=1, keepdims=True)
        )
        * inv_std[:, :1]
    ).astype(BF16)


def query_kernel(k0, k1, k2, v0, v1, v2, slope0, slope1, slope2, grad_mix, hidden, w, output, grad_queries):
    rows, width = k0.shape
    size = width // HEADS
    output[...] = dot(hidden[...], w[...]).astype(BF16)
    parts = ((k0, v0, slope0), (k1, v1, slope1), (k2, v2, slope2))
    for h in range(HEADS):
        cols = head_slice(h, size)
        total = jnp.zeros((rows, size), F32)
        for keys, vals, slope in parts:
            grad_attention = dot_nt(grad_mix[:, cols], vals[:, cols])
            grad_scores = (grad_attention * slope[:, cols]).astype(BF16)
            total = total + dot(grad_scores, keys[:, cols])
        grad_queries[:, cols] = total.astype(BF16)


def key_terms(h, mask, k, v, qd, gd):
    size = k.shape[1] // HEADS
    scale = size ** (-0.5)
    cols = head_slice(h, size)
    scores = dot_nt(k[:, cols], qd[:, cols]) * scale
    gate = logistic(scores)
    attention = jnp.where(mask, scores * gate, 0.0).astype(BF16)
    grad_attention = dot_nt(v[:, cols], gd[:, cols])
    slope = jnp.where(mask, silu_slope(scores, gate) * scale, 0.0)
    grad_scores = (grad_attention * slope).astype(BF16)
    return dot(grad_scores, qd[:, cols]), dot(attention, gd[:, cols])


def key_kernel(len_ref, place_ref, k, v, q0, q2, g0, g2, keys_total, values_total):
    rows, width = k.shape
    first = place_ref[0] * rows
    masks = [allowed_block(rows, first + d * rows, first, len_ref, 1) for d in (0, 2)]
    for h in range(HEADS):
        cols = head_slice(h, width // HEADS)
        own = key_terms(h, masks[0], k, v, q0, g0)
        far = key_terms(h, masks[1], k, v, q2, g2)
        keys_total[:, cols] = own[0] + far[0]
        values_total[:, cols] = own[1] + far[1]


def key_end_kernel(len_ref, place_ref, k, v, q1, g1, keys_part, values_part, grad_keys, grad_values):
    rows, width = k.shape
    first = place_ref[0] * rows
    mask = allowed_block(rows, first + rows, first, len_ref, 1)
    for h in range(HEADS):
        cols = head_slice(h, width // HEADS)
        near = key_terms(h, mask, k, v, q1, g1)
        grad_keys[:, cols] = (keys_part[:, cols] + near[0]).astype(BF16)
        grad_values[:, cols] = (values_part[:, cols] + near[1]).astype(BF16)


def weight_kernel(groups, place_ref, *refs):
    hidden = jnp.concatenate([ref[...] for ref in refs[:groups]], axis=0)
    grads = jnp.concatenate([ref[...] for ref in refs[groups : 2 * groups]], axis=0)
    own = refs[2 * groups]
    sends = refs[2 * groups + 1 : -1]
    total = refs[-1]
    total[...] = dot_tn(hidden, grads)
    if not sends:
        own[...] = total[...]
        return
    rows = own.shape[0]
    corner = place_ref[0] & len(sends)
    own[...] = total[pl.ds(pl.multiple_of(corner * rows, rows), rows), :]
    for e, ref in enumerate(sends):
        at = pl.multiple_of((corner ^ (e + 1)) * rows, rows)
        ref[...] = total[pl.ds(at, rows), :].astype(BF16)


def corner_kernel(own, *refs):
    got, narrow = refs[:-1], refs[-1]
    acc = own[...]
    for ref in got:
        acc = acc + ref[...].astype(F32)
    narrow[...] = acc.astype(BF16)


def pair_kernel(scale, mine, other, both):
    both[...] = ((mine[...].astype(F32) + other[...].astype(F32)) * scale).astype(BF16)


def place_kernel(corners, place_ref, *refs):
    shares, (out, wide, sems) = refs[:corners], refs[corners:]
    rows = shares[0].shape[0]
    corner = place_ref[0] & (corners - 1)
    moves = []
    for e, ref in enumerate(shares):
        wide[e] = ref[...].astype(F32)
        at = pl.multiple_of((corner ^ e) * rows, rows)
        moves.append(pltpu.make_async_copy(wide.at[e], out.at[pl.ds(at, rows), :], sems.at[e]))
        moves[-1].start()
    for move in moves:
        move.wait()


def xor_route(size, mask):
    return [(i, i ^ mask) for i in range(size)]


def shifted(block, distance):
    count = lax.axis_size("seq")
    route = [(i, i + distance) for i in range(count) if 0 <= i + distance < count]
    return lax.ppermute(block, "seq", route)


def swapped(block, axis, mask):
    return lax.ppermute(block, axis, xor_route(lax.axis_size(axis), mask))


def after(value, *others):
    return lax.optimization_barrier((value, *others))[0]


def on_device(queries, keys, values, gates, out_grad, w_out, hist_lengths):
    rows, width = queries.shape[1:]
    seq = lax.axis_size("seq")
    batch = lax.axis_size("batch")
    seq_at = lax.axis_index("seq")
    place = jnp.stack([seq_at, lax.axis_index("batch")]).astype(jnp.int32)
    scalars = (hist_lengths, place)
    even = (seq_at & 1) == 0
    full = jax.ShapeDtypeStruct((rows, width), BF16)
    near = kept((rows, width), BF16)
    wide = kept((rows, width), F32)
    block_flops = 2 * rows * rows * width
    proj_flops = 2 * rows * width * width
    part = width // batch
    hbm = pl.BlockSpec(memory_space=pltpu.HBM)

    k2 = shifted(keys[0], 2)
    v2 = shifted(values[0], 2)
    passed = jnp.where(even, keys[0], k2)
    k1 = swapped(passed, "seq", 1)
    q, k, v, grad, w, gate, mixed_own, grad_hidden, slope0 = call(
        own_kernel,
        [near, near, near, near, kept(w_out.shape, BF16), near, wide, wide, wide],
        scalars,
        tuple(
            in_hbm(a)
            for a in (after(queries[0], passed), keys[0], values[0], out_grad[0], w_out, gates[0])
        ),
        proj_flops + 2 * block_flops,
        [pltpu.SemaphoreType.DMA((5 + CHUNKS,))],
        [hbm] * 6,
    )
    v1 = shifted(values[0], 1)
    grads = [grad]
    for d in range(1, batch):
        low = d & -d
        source = out_grad[0] if d == 1 else out_grad[0] if d == low else grads[d ^ low]
        grads.append(swapped(source, "batch", low))
    attention2, slope2 = call(
        functools.partial(far_kernel, 2), [near, wide], scalars, (after(q, passed), k2), block_flops
    )
    q2 = shifted(after(q, attention2), -2)
    passed_q = jnp.where(even, q2, q)
    q1 = swapped(passed_q, "seq", 1)
    attention1, slope1 = call(
        functools.partial(far_kernel, 1), [near, wide], scalars, (after(q, v1), k1), block_flops
    )
    hidden, normed, inv_std, *slices = call(
        functools.partial(forward_kernel, batch),
        [near, wide, kept((rows, 128), F32)] + [kept((rows, part), BF16)] * batch,
        (place,),
        (attention1, attention2, v1, v2, after(mixed_own, grads[1], grads[3]), gate),
        block_flops,
        [pltpu.VMEM((rows, width), F32)],
    )
    hiddens = [slices[0]] + [swapped(slices[d], "batch", d) for d in range(1, batch)]
    grad_gates, grad_mix = call(
        mix_kernel, [full, near], (), (grad_hidden, gate, normed, inv_std), block_flops // 4
    )
    g2 = shifted(grad_mix, -2)
    g2_late = g2

    corners = 4
    direct = seq == 2 * corners
    rows_w = part // corners if direct else part
    share = kept((rows_w, width), BF16)
    scale = (rows * seq * batch) ** (-0.5)
    own, *sends = call(
        functools.partial(weight_kernel, batch),
        [kept((rows_w, width), F32)] + [share] * (corners - 1 if direct else 0),
        (place,),
        (*hiddens, *grads),
        proj_flops,
        [pltpu.VMEM((part, width), F32)],
    )
    output, grad_queries = call(
        query_kernel,
        [full, full],
        (),
        (k, k1, k2, v, v1, v2, slope0, slope1, slope2, grad_mix, after(hidden, own), w),
        proj_flops + 6 * block_flops,
    )
    if direct:
        got = [swapped(s, "seq", e + 1) for e, s in enumerate(sends)]
        (mine,) = call(corner_kernel, [share], (), (after(own, output), *got), own.size * 4)
        other = swapped(mine, "seq", corners)
        g2_late = after(g2, mine)
    else:
        mine = own
    keys_part, values_part = call(
        key_kernel,
        [wide, wide],
        scalars,
        (k, after(v, mine), q, q2, grad_mix, g2),
        8 * block_flops,
    )
    g1 = swapped(jnp.where(even, g2_late, grad_mix), "seq", 1)
    if direct:
        (both,) = call(
            functools.partial(pair_kernel, scale),
            [share],
            (),
            (after(mine, keys_part), other),
            own.size * 2,
        )
    else:
        both = own
    grad_keys, grad_values = call(
        key_end_kernel,
        [full, full],
        scalars,
        (k, after(v, both), q1, g1, keys_part, values_part),
        4 * block_flops,
    )
    if direct:
        shares = [after(both, grad_keys)] + [swapped(both, "seq", e) for e in range(1, corners)]
        (grad_weight,) = call(
            functools.partial(place_kernel, corners),
            [jax.ShapeDtypeStruct((part, width), F32)],
            (place,),
            shares,
            part * width,
            [pltpu.VMEM((corners, rows_w, width), F32), pltpu.SemaphoreType.DMA((corners,))],
            out_space=hbm,
        )
    else:
        grad_weight = lax.psum(own, "seq") * scale
    return (
        output[None],
        grad_queries[None],
        grad_keys[None],
        grad_values[None],
        grad_gates[None],
        grad_weight,
    )


def solution(mesh):
    token = P("batch", "seq", None)
    return jax.shard_map(
        on_device,
        mesh=mesh,
        in_specs=(token, token, token, token, token, P(), P("batch", None)),
        out_specs=(token, token, token, token, token, P("batch", None)),
        check_vma=False,
    )
```

```python
import functools
import math

import jax
import jax.numpy as jnp
from jax import lax
from jax.experimental import pallas as pl
from jax.experimental.pallas import tpu as pltpu
from jax.sharding import PartitionSpec as P

HEADS = 8
WINDOW = 256
REACH = 2
CHUNKS = 4

VMEM = pl.BlockSpec(memory_space=pltpu.VMEM)
SMEM = pl.BlockSpec(memory_space=pltpu.SMEM)
F32 = jnp.float32
BF16 = jnp.bfloat16
NT = (((1,), (1,)), ((), ()))
TN = (((0,), (0,)), ((), ()))


def dot(a, b):
    return jnp.dot(a, b, preferred_element_type=F32)


def dot_nt(a, b):
    return lax.dot_general(a, b, NT, preferred_element_type=F32)


def dot_tn(a, b):
    return lax.dot_general(a, b, TN, preferred_element_type=F32)


def logistic(scores):
    return 0.5 * jnp.tanh(0.5 * scores) + 0.5


def silu_slope(scores, gate):
    return gate * (1.0 + scores * (1.0 - gate))


def start_of(positions, len_ref):
    total = jnp.zeros_like(positions)
    end = jnp.int32(0)
    for k in range(len_ref.shape[1]):
        length = len_ref[0, k]
        end = end + length
        total = total + jnp.where(positions >= end, length, 0)
    return total


def allowed_block(rows, first_query, first_key, len_ref, query_dim):
    shape = (rows, rows)
    query_pos = first_query + lax.broadcasted_iota(jnp.int32, shape, query_dim)
    key_pos = first_key + lax.broadcasted_iota(jnp.int32, shape, 1 - query_dim)
    start = start_of(query_pos, len_ref)
    return (key_pos >= start) & (key_pos <= query_pos) & (key_pos > query_pos - WINDOW)


def head_slice(h, width):
    return slice(h * width, (h + 1) * width)


def kept(shape, dtype):
    return pltpu.VMEM(shape, dtype)


def in_hbm(array):
    return pltpu.with_memory_space_constraint(array, pltpu.HBM)


def nbytes(arrays):
    return sum(math.prod(a.shape) * jnp.dtype(a.dtype).itemsize for a in arrays)


def call(kernel, outs, scalars, arrays, flops, scratch=(), spaces=None, out_space=VMEM, aliases={}):
    return pl.pallas_call(
        kernel,
        out_shape=outs,
        in_specs=[SMEM] * len(scalars) + (spaces or [VMEM] * len(arrays)),
        out_specs=[out_space] * len(outs),
        scratch_shapes=list(scratch),
        input_output_aliases=aliases,
        cost_estimate=pl.CostEstimate(
            flops=flops, bytes_accessed=nbytes([*arrays, *outs]), transcendentals=0
        ),
        compiler_params=pltpu.CompilerParams(vmem_limit_bytes=32 * 1024 * 1024),
    )(*scalars, *arrays)


def own_kernel(
    len_ref, place_ref, q_in, k_in, v_in, grad_in, w_in, gate_in,
    q, k, v, grad, w, gates, mixed, grad_hidden, slope, sems,
):
    pairs = ((q_in, q), (k_in, k), (v_in, v), (grad_in, grad), (gate_in, gates))
    moves = [
        pltpu.make_async_copy(src, dst, sems.at[i]) for i, (src, dst) in enumerate(pairs)
    ]
    rows, width = q.shape
    part = width // CHUNKS
    parts = []
    for c in range(CHUNKS):
        here = pl.ds(c * part, part)
        parts.append(
            pltpu.make_async_copy(w_in.at[here, :], w.at[here, :], sems.at[len(pairs) + c])
        )
    for move in moves[:4] + parts + moves[4:]:
        move.start()
    size = width // HEADS
    first = place_ref[0] * rows
    allowed = allowed_block(rows, first, first, len_ref, 0)
    for move in moves[:3]:
        move.wait()
    for h in range(HEADS):
        cols = head_slice(h, size)
        attention = block_scores(h, allowed, q, k, slope)
        mixed[:, cols] = dot(attention, v[:, cols])
    moves[3].wait()
    for c in range(CHUNKS):
        parts[c].wait()
        here = slice(c * part, (c + 1) * part)
        grad_hidden[:, here] = dot_nt(grad[...], w[here, :])
    moves[4].wait()


def block_scores(h, allowed, q, keys, slope):
    size = q.shape[1] // HEADS
    scale = size ** (-0.5)
    cols = head_slice(h, size)
    scores = dot_nt(q[:, cols], keys[:, cols]) * scale
    gate = logistic(scores)
    slope[:, cols] = jnp.where(allowed, silu_slope(scores, gate) * scale, 0.0)
    return jnp.where(allowed, scores * gate, 0.0).astype(BF16)


def far_kernel(distance, len_ref, place_ref, q, keys, attention, slope):
    rows, width = q.shape
    size = width // HEADS
    first = place_ref[0] * rows
    allowed = allowed_block(rows, first, first - distance * rows, len_ref, 0)
    for h in range(HEADS):
        attention[:, head_slice(h, size)] = block_scores(h, allowed, q, keys, slope)


def forward_kernel(groups, place_ref, attention1, attention2, v1, v2, mixed_own, gates, hidden, normed, inv_std, *rest):
    slices, mixed = rest[:-1], rest[-1]
    rows, width = v1.shape
    size = width // HEADS
    for h in range(HEADS):
        cols = head_slice(h, size)
        mixed[:, cols] = (
            mixed_own[:, cols]
            + dot(attention1[:, cols], v1[:, cols])
            + dot(attention2[:, cols], v2[:, cols])
        )
    values = mixed[...]
    centered = values - jnp.mean(values, axis=1, keepdims=True)
    inverse = lax.rsqrt(jnp.mean(centered * centered, axis=1, keepdims=True) + 1e-05)
    inv_std[...] = jnp.broadcast_to(inverse, inv_std.shape)
    normed[...] = centered * inverse
    hidden[...] = (normed[...] * gates[...].astype(F32)).astype(BF16)
    part = width // groups
    for d, ref in enumerate(slices):
        at = pl.multiple_of((place_ref[1] ^ d) * part, 128)
        ref[...] = hidden[:, pl.ds(at, part)]


def mix_kernel(grad_hidden, gates, normed, inv_std, grad_gates, grad_mix):
    gh = grad_hidden[...]
    norm = normed[...]
    grad_gates[...] = (gh * norm).astype(BF16)
    grad_norm = gh * gates[...].astype(F32)
    grad_mix[...] = (
        (
            grad_norm
            - jnp.mean(grad_norm, axis=1, keepdims=True)
            - norm * jnp.mean(grad_norm * norm, axis=1, keepdims=True)
        )
        * inv_std[:, :1]
    ).astype(BF16)


def query_kernel(k0, k1, k2, v0, v1, v2, slope0, slope1, slope2, grad_mix, hidden, w, output, grad_queries):
    rows, width = k0.shape
    size = width // HEADS
    output[...] = dot(hidden[...], w[...]).astype(BF16)
    parts = ((k0, v0, slope0), (k1, v1, slope1), (k2, v2, slope2))
    for h in range(HEADS):
        cols = head_slice(h, size)
        total = jnp.zeros((rows, size), F32)
        for keys, vals, slope in parts:
            grad_attention = dot_nt(grad_mix[:, cols], vals[:, cols])
            grad_scores = (grad_attention * slope[:, cols]).astype(BF16)
            total = total + dot(grad_scores, keys[:, cols])
        grad_queries[:, cols] = total.astype(BF16)


def key_terms(h, mask, k, v, qd, gd):
    size = k.shape[1] // HEADS
    scale = size ** (-0.5)
    cols = head_slice(h, size)
    scores = dot_nt(k[:, cols], qd[:, cols]) * scale
    gate = logistic(scores)
    attention = jnp.where(mask, scores * gate, 0.0).astype(BF16)
    grad_attention = dot_nt(v[:, cols], gd[:, cols])
    slope = jnp.where(mask, silu_slope(scores, gate) * scale, 0.0)
    grad_scores = (grad_attention * slope).astype(BF16)
    return dot(grad_scores, qd[:, cols]), dot(attention, gd[:, cols])


def key_kernel(len_ref, place_ref, k, v, q0, q2, g0, g2, keys_total, values_total):
    rows, width = k.shape
    first = place_ref[0] * rows
    masks = [allowed_block(rows, first + d * rows, first, len_ref, 1) for d in (0, 2)]
    for h in range(HEADS):
        cols = head_slice(h, width // HEADS)
        own = key_terms(h, masks[0], k, v, q0, g0)
        far = key_terms(h, masks[1], k, v, q2, g2)
        keys_total[:, cols] = own[0] + far[0]
        values_total[:, cols] = own[1] + far[1]


def key_end_kernel(len_ref, place_ref, k, v, q1, g1, keys_part, values_part, grad_keys, grad_values):
    rows, width = k.shape
    first = place_ref[0] * rows
    mask = allowed_block(rows, first + rows, first, len_ref, 1)
    for h in range(HEADS):
        cols = head_slice(h, width // HEADS)
        near = key_terms(h, mask, k, v, q1, g1)
        grad_keys[:, cols] = (keys_part[:, cols] + near[0]).astype(BF16)
        grad_values[:, cols] = (values_part[:, cols] + near[1]).astype(BF16)


def weight_kernel(groups, place_ref, *refs):
    hidden = jnp.concatenate([ref[...] for ref in refs[:groups]], axis=0)
    grads = jnp.concatenate([ref[...] for ref in refs[groups : 2 * groups]], axis=0)
    own = refs[2 * groups]
    sends = refs[2 * groups + 1 : -1]
    total = refs[-1]
    total[...] = dot_tn(hidden, grads)
    if not sends:
        own[...] = total[...]
        return
    rows = own.shape[0]
    corner = place_ref[0] & len(sends)
    own[...] = total[pl.ds(pl.multiple_of(corner * rows, rows), rows), :]
    for e, ref in enumerate(sends):
        at = pl.multiple_of((corner ^ (e + 1)) * rows, rows)
        ref[...] = total[pl.ds(at, rows), :].astype(BF16)


def corner_kernel(own, *refs):
    got, narrow = refs[:-1], refs[-1]
    acc = own[...]
    for ref in got:
        acc = acc + ref[...].astype(F32)
    narrow[...] = acc.astype(BF16)


def pair_kernel(scale, mine, other, both):
    both[...] = ((mine[...].astype(F32) + other[...].astype(F32)) * scale).astype(BF16)


def place_kernel(corners, place_ref, *refs):
    shares, (out, wide, sems) = refs[:corners], refs[corners:]
    rows = shares[0].shape[0]
    corner = place_ref[0] & (corners - 1)
    moves = []
    for e, ref in enumerate(shares):
        wide[e] = ref[...].astype(F32)
        at = pl.multiple_of((corner ^ e) * rows, rows)
        moves.append(pltpu.make_async_copy(wide.at[e], out.at[pl.ds(at, rows), :], sems.at[e]))
        moves[-1].start()
    for move in moves:
        move.wait()


def xor_route(size, mask):
    return [(i, i ^ mask) for i in range(size)]


def shifted(block, distance):
    count = lax.axis_size("seq")
    route = [(i, (i + distance) % count) for i in range(count)]
    return lax.ppermute(block, "seq", route)


def swapped(block, axis, mask):
    return lax.ppermute(block, axis, xor_route(lax.axis_size(axis), mask))


def after(value, *others):
    return lax.optimization_barrier((value, *others))[0]


def on_device(queries, keys, values, gates, out_grad, w_out, hist_lengths):
    rows, width = queries.shape[1:]
    seq = lax.axis_size("seq")
    batch = lax.axis_size("batch")
    seq_at = lax.axis_index("seq")
    place = jnp.stack([seq_at, lax.axis_index("batch")]).astype(jnp.int32)
    scalars = (hist_lengths, place)
    even = (seq_at & 1) == 0
    full = jax.ShapeDtypeStruct((rows, width), BF16)
    near = kept((rows, width), BF16)
    wide = kept((rows, width), F32)
    block_flops = 2 * rows * rows * width
    proj_flops = 2 * rows * width * width
    part = width // batch
    hbm = pl.BlockSpec(memory_space=pltpu.HBM)

    k2 = shifted(keys[0], 2)
    v2 = shifted(values[0], 2)
    passed = jnp.where(even, keys[0], k2)
    k1 = swapped(passed, "seq", 1)
    q, k, v, grad, w, gate, mixed_own, grad_hidden, slope0 = call(
        own_kernel,
        [near, near, near, near, kept(w_out.shape, BF16), near, wide, wide, wide],
        scalars,
        tuple(
            in_hbm(a)
            for a in (after(queries[0], passed), keys[0], values[0], out_grad[0], w_out, gates[0])
        ),
        proj_flops + 2 * block_flops,
        [pltpu.SemaphoreType.DMA((5 + CHUNKS,))],
        [hbm] * 6,
    )
    v1 = shifted(values[0], 1)
    grads = [grad]
    for d in range(1, batch):
        low = d & -d
        source = out_grad[0] if d == 1 else out_grad[0] if d == low else grads[d ^ low]
        grads.append(swapped(source, "batch", low))
    attention2, slope2 = call(
        functools.partial(far_kernel, 2), [near, wide], scalars, (after(q, passed), k2), block_flops
    )
    q2 = shifted(after(q, attention2), -2)
    passed_q = jnp.where(even, q2, q)
    q1 = swapped(passed_q, "seq", 1)
    attention1, slope1 = call(
        functools.partial(far_kernel, 1), [near, wide], scalars, (after(q, v1), k1), block_flops
    )
    hidden, normed, inv_std, *slices = call(
        functools.partial(forward_kernel, batch),
        [near, wide, kept((rows, 128), F32)] + [kept((rows, part), BF16)] * batch,
        (place,),
        (attention1, attention2, v1, v2, after(mixed_own, grads[1], grads[3]), gate),
        block_flops,
        [pltpu.VMEM((rows, width), F32)],
    )
    hiddens = [slices[0]] + [swapped(slices[d], "batch", d) for d in range(1, batch)]
    grad_gates, grad_mix = call(
        mix_kernel, [full, near], (), (grad_hidden, gate, normed, inv_std), block_flops // 4
    )
    g2 = shifted(grad_mix, -2)
    g2_late = g2

    corners = 4
    direct = seq == 2 * corners
    rows_w = part // corners if direct else part
    share = kept((rows_w, width), BF16)
    scale = (rows * seq * batch) ** (-0.5)
    own, *sends = call(
        functools.partial(weight_kernel, batch),
        [kept((rows_w, width), F32)] + [share] * (corners - 1 if direct else 0),
        (place,),
        (*hiddens, *grads),
        proj_flops,
        [pltpu.VMEM((part, width), F32)],
    )
    output, grad_queries = call(
        query_kernel,
        [full, full],
        (),
        (k, k1, k2, v, v1, v2, slope0, slope1, slope2, grad_mix, after(hidden, own), w),
        proj_flops + 6 * block_flops,
    )
    if direct:
        got = [swapped(s, "seq", e + 1) for e, s in enumerate(sends)]
        (mine,) = call(corner_kernel, [share], (), (after(own, output), *got), own.size * 4)
        other = swapped(mine, "seq", corners)
        g2_late = after(g2, mine)
    else:
        mine = own
    keys_part, values_part = call(
        key_kernel,
        [wide, wide],
        scalars,
        (k, after(v, mine), q, q2, grad_mix, g2),
        8 * block_flops,
    )
    g1 = swapped(jnp.where(even, g2_late, grad_mix), "seq", 1)
    if direct:
        (both,) = call(
            functools.partial(pair_kernel, scale),
            [share],
            (),
            (after(mine, keys_part), other),
            own.size * 2,
        )
    else:
        both = own
    grad_keys, grad_values = call(
        key_end_kernel,
        [full, full],
        scalars,
        (k, after(v, both), q1, g1, keys_part, values_part),
        4 * block_flops,
    )
    if direct:
        shares = [after(both, grad_keys)] + [swapped(both, "seq", e) for e in range(1, corners)]
        (grad_weight,) = call(
            functools.partial(place_kernel, corners),
            [jax.ShapeDtypeStruct((part, width), F32)],
            (place,),
            shares,
            part * width,
            [pltpu.VMEM((corners, rows_w, width), F32), pltpu.SemaphoreType.DMA((corners,))],
            out_space=hbm,
        )
    else:
        grad_weight = lax.psum(own, "seq") * scale
    return (
        output[None],
        grad_queries[None],
        grad_keys[None],
        grad_values[None],
        grad_gates[None],
        grad_weight,
    )


def solution(mesh):
    token = P("batch", "seq", None)
    return jax.shard_map(
        on_device,
        mesh=mesh,
        in_specs=(token, token, token, token, token, P(), P("batch", None)),
        out_specs=(token, token, token, token, token, P("batch", None)),
        check_vma=False,
    )
```

```python
import functools
import math

import jax
import jax.numpy as jnp
from jax import lax
from jax.experimental import pallas as pl
from jax.experimental.pallas import tpu as pltpu
from jax.sharding import PartitionSpec as P

HEADS = 8
WINDOW = 256
REACH = 2
CHUNKS = 4

VMEM = pl.BlockSpec(memory_space=pltpu.VMEM)
SMEM = pl.BlockSpec(memory_space=pltpu.SMEM)
F32 = jnp.float32
BF16 = jnp.bfloat16
NT = (((1,), (1,)), ((), ()))
TN = (((0,), (0,)), ((), ()))


def dot(a, b):
    return jnp.dot(a, b, preferred_element_type=F32)


def dot_nt(a, b):
    return lax.dot_general(a, b, NT, preferred_element_type=F32)


def dot_tn(a, b):
    return lax.dot_general(a, b, TN, preferred_element_type=F32)


def logistic(scores):
    return 0.5 * jnp.tanh(0.5 * scores) + 0.5


def silu_slope(scores, gate):
    return gate * (1.0 + scores * (1.0 - gate))


def start_of(positions, len_ref):
    total = jnp.zeros_like(positions)
    end = jnp.int32(0)
    for k in range(len_ref.shape[1]):
        length = len_ref[0, k]
        end = end + length
        total = total + jnp.where(positions >= end, length, 0)
    return total


def allowed_block(rows, first_query, first_key, len_ref, query_dim):
    shape = (rows, rows)
    query_pos = first_query + lax.broadcasted_iota(jnp.int32, shape, query_dim)
    key_pos = first_key + lax.broadcasted_iota(jnp.int32, shape, 1 - query_dim)
    start = start_of(query_pos, len_ref)
    return (key_pos >= start) & (key_pos <= query_pos) & (key_pos > query_pos - WINDOW)


def head_slice(h, width):
    return slice(h * width, (h + 1) * width)


def kept(shape, dtype):
    return pltpu.VMEM(shape, dtype)


def in_hbm(array):
    return pltpu.with_memory_space_constraint(array, pltpu.HBM)


def nbytes(arrays):
    return sum(math.prod(a.shape) * jnp.dtype(a.dtype).itemsize for a in arrays)


def call(kernel, outs, scalars, arrays, flops, scratch=(), spaces=None, out_space=VMEM, aliases={}):
    return pl.pallas_call(
        kernel,
        out_shape=outs,
        in_specs=[SMEM] * len(scalars) + (spaces or [VMEM] * len(arrays)),
        out_specs=[out_space] * len(outs),
        scratch_shapes=list(scratch),
        input_output_aliases=aliases,
        cost_estimate=pl.CostEstimate(
            flops=flops, bytes_accessed=nbytes([*arrays, *outs]), transcendentals=0
        ),
        compiler_params=pltpu.CompilerParams(vmem_limit_bytes=32 * 1024 * 1024),
    )(*scalars, *arrays)


def own_kernel(
    len_ref, place_ref, q_in, k_in, v_in, grad_in, w_in, gate_in,
    q, k, v, grad, w, gates, mixed, grad_hidden, slope, sems,
):
    pairs = ((q_in, q), (k_in, k), (v_in, v), (grad_in, grad), (gate_in, gates))
    moves = [
        pltpu.make_async_copy(src, dst, sems.at[i]) for i, (src, dst) in enumerate(pairs)
    ]
    rows, width = q.shape
    part = width // CHUNKS
    parts = []
    for c in range(CHUNKS):
        here = pl.ds(c * part, part)
        parts.append(
            pltpu.make_async_copy(w_in.at[here, :], w.at[here, :], sems.at[len(pairs) + c])
        )
    for move in moves[:4] + parts + moves[4:]:
        move.start()
    size = width // HEADS
    first = place_ref[0] * rows
    allowed = allowed_block(rows, first, first, len_ref, 0)
    for move in moves[:3]:
        move.wait()
    for h in range(HEADS):
        cols = head_slice(h, size)
        attention = block_scores(h, allowed, q, k, slope)
        mixed[:, cols] = dot(attention, v[:, cols])
    moves[3].wait()
    for c in range(CHUNKS):
        parts[c].wait()
        here = slice(c * part, (c + 1) * part)
        grad_hidden[:, here] = dot_nt(grad[...], w[here, :])
    moves[4].wait()


def block_scores(h, allowed, q, keys, slope):
    size = q.shape[1] // HEADS
    scale = size ** (-0.5)
    cols = head_slice(h, size)
    scores = dot_nt(q[:, cols], keys[:, cols]) * scale
    gate = logistic(scores)
    slope[:, cols] = jnp.where(allowed, silu_slope(scores, gate) * scale, 0.0)
    return jnp.where(allowed, scores * gate, 0.0).astype(BF16)


def far_kernel(distance, len_ref, place_ref, q, keys, attention, slope):
    rows, width = q.shape
    size = width // HEADS
    first = place_ref[0] * rows
    allowed = allowed_block(rows, first, first - distance * rows, len_ref, 0)
    for h in range(HEADS):
        attention[:, head_slice(h, size)] = block_scores(h, allowed, q, keys, slope)


def forward_kernel(groups, place_ref, attention1, attention2, v1, v2, mixed_own, gates, hidden, normed, inv_std, *rest):
    slices, mixed = rest[:-1], rest[-1]
    rows, width = v1.shape
    size = width // HEADS
    for h in range(HEADS):
        cols = head_slice(h, size)
        mixed[:, cols] = (
            mixed_own[:, cols]
            + dot(attention1[:, cols], v1[:, cols])
            + dot(attention2[:, cols], v2[:, cols])
        )
    values = mixed[...]
    centered = values - jnp.mean(values, axis=1, keepdims=True)
    inverse = lax.rsqrt(jnp.mean(centered * centered, axis=1, keepdims=True) + 1e-05)
    inv_std[...] = jnp.broadcast_to(inverse, inv_std.shape)
    normed[...] = centered * inverse
    hidden[...] = (normed[...] * gates[...].astype(F32)).astype(BF16)
    part = width // groups
    for d, ref in enumerate(slices):
        at = pl.multiple_of((place_ref[1] ^ d) * part, 128)
        ref[...] = hidden[:, pl.ds(at, part)]


def mix_kernel(grad_hidden, gates, normed, inv_std, grad_gates, grad_mix):
    gh = grad_hidden[...]
    norm = normed[...]
    grad_gates[...] = (gh * norm).astype(BF16)
    grad_norm = gh * gates[...].astype(F32)
    grad_mix[...] = (
        (
            grad_norm
            - jnp.mean(grad_norm, axis=1, keepdims=True)
            - norm * jnp.mean(grad_norm * norm, axis=1, keepdims=True)
        )
        * inv_std[:, :1]
    ).astype(BF16)


def query_kernel(k0, k1, k2, v0, v1, v2, slope0, slope1, slope2, grad_mix, hidden, w, output, grad_queries):
    rows, width = k0.shape
    size = width // HEADS
    output[...] = dot(hidden[...], w[...]).astype(BF16)
    parts = ((k0, v0, slope0), (k1, v1, slope1), (k2, v2, slope2))
    for h in range(HEADS):
        cols = head_slice(h, size)
        total = jnp.zeros((rows, size), F32)
        for keys, vals, slope in parts:
            grad_attention = dot_nt(grad_mix[:, cols], vals[:, cols])
            grad_scores = (grad_attention * slope[:, cols]).astype(BF16)
            total = total + dot(grad_scores, keys[:, cols])
        grad_queries[:, cols] = total.astype(BF16)


def key_terms(h, mask, k, v, qd, gd):
    size = k.shape[1] // HEADS
    scale = size ** (-0.5)
    cols = head_slice(h, size)
    scores = dot_nt(k[:, cols], qd[:, cols]) * scale
    gate = logistic(scores)
    attention = jnp.where(mask, scores * gate, 0.0).astype(BF16)
    grad_attention = dot_nt(v[:, cols], gd[:, cols])
    slope = jnp.where(mask, silu_slope(scores, gate) * scale, 0.0)
    grad_scores = (grad_attention * slope).astype(BF16)
    return dot(grad_scores, qd[:, cols]), dot(attention, gd[:, cols])


def key_kernel(len_ref, place_ref, k, v, q0, q2, g0, g2, keys_total, values_total):
    rows, width = k.shape
    first = place_ref[0] * rows
    masks = [allowed_block(rows, first + d * rows, first, len_ref, 1) for d in (0, 2)]
    for h in range(HEADS):
        cols = head_slice(h, width // HEADS)
        own = key_terms(h, masks[0], k, v, q0, g0)
        far = key_terms(h, masks[1], k, v, q2, g2)
        keys_total[:, cols] = own[0] + far[0]
        values_total[:, cols] = own[1] + far[1]


def key_end_kernel(len_ref, place_ref, k, v, q1, g1, keys_part, values_part, grad_keys, grad_values):
    rows, width = k.shape
    first = place_ref[0] * rows
    mask = allowed_block(rows, first + rows, first, len_ref, 1)
    for h in range(HEADS):
        cols = head_slice(h, width // HEADS)
        near = key_terms(h, mask, k, v, q1, g1)
        grad_keys[:, cols] = (keys_part[:, cols] + near[0]).astype(BF16)
        grad_values[:, cols] = (values_part[:, cols] + near[1]).astype(BF16)


def weight_kernel(groups, place_ref, *refs):
    hidden = jnp.concatenate([ref[...] for ref in refs[:groups]], axis=0)
    grads = jnp.concatenate([ref[...] for ref in refs[groups : 2 * groups]], axis=0)
    own = refs[2 * groups]
    sends = refs[2 * groups + 1 : -1]
    total = refs[-1]
    total[...] = dot_tn(hidden, grads)
    if not sends:
        own[...] = total[...]
        return
    rows = own.shape[0]
    corner = place_ref[0] & len(sends)
    own[...] = total[pl.ds(pl.multiple_of(corner * rows, rows), rows), :]
    for e, ref in enumerate(sends):
        at = pl.multiple_of((corner ^ (e + 1)) * rows, rows)
        ref[...] = total[pl.ds(at, rows), :].astype(BF16)


def corner_kernel(own, *refs):
    got, narrow = refs[:-1], refs[-1]
    acc = own[...]
    for ref in got:
        acc = acc + ref[...].astype(F32)
    narrow[...] = acc.astype(BF16)


def pair_kernel(scale, mine, other, both):
    both[...] = ((mine[...].astype(F32) + other[...].astype(F32)) * scale).astype(BF16)


def place_kernel(corners, place_ref, *refs):
    shares, (out, wide, sems) = refs[:corners], refs[corners:]
    rows = shares[0].shape[0]
    corner = place_ref[0] & (corners - 1)
    moves = []
    for e, ref in enumerate(shares):
        wide[e] = ref[...].astype(F32)
        at = pl.multiple_of((corner ^ e) * rows, rows)
        moves.append(pltpu.make_async_copy(wide.at[e], out.at[pl.ds(at, rows), :], sems.at[e]))
        moves[-1].start()
    for move in moves:
        move.wait()


def xor_route(size, mask):
    return [(i, i ^ mask) for i in range(size)]


def shifted(block, distance):
    count = lax.axis_size("seq")
    route = [(i, (i + distance) % count) for i in range(count)]
    return lax.ppermute(block, "seq", route)


def swapped(block, axis, mask):
    return lax.ppermute(block, axis, xor_route(lax.axis_size(axis), mask))


def after(value, *others):
    return lax.optimization_barrier((value, *others))[0]


def on_device(queries, keys, values, gates, out_grad, w_out, hist_lengths):
    rows, width = queries.shape[1:]
    seq = lax.axis_size("seq")
    batch = lax.axis_size("batch")
    seq_at = lax.axis_index("seq")
    place = jnp.stack([seq_at, lax.axis_index("batch")]).astype(jnp.int32)
    scalars = (hist_lengths, place)
    even = (seq_at & 1) == 0
    full = jax.ShapeDtypeStruct((rows, width), BF16)
    near = kept((rows, width), BF16)
    wide = kept((rows, width), F32)
    block_flops = 2 * rows * rows * width
    proj_flops = 2 * rows * width * width
    part = width // batch
    hbm = pl.BlockSpec(memory_space=pltpu.HBM)

    k2 = shifted(keys[0], 2)
    v2 = shifted(values[0], 2)
    q, k, v, grad, w, gate, mixed_own, grad_hidden, slope0 = call(
        own_kernel,
        [near, near, near, near, kept(w_out.shape, BF16), near, wide, wide, wide],
        scalars,
        tuple(
            in_hbm(a)
            for a in (queries[0], keys[0], values[0], out_grad[0], w_out, gates[0])
        ),
        proj_flops + 2 * block_flops,
        [pltpu.SemaphoreType.DMA((5 + CHUNKS,))],
        [hbm] * 6,
    )
    passed = jnp.where(even, k, k2)
    k1 = swapped(passed, "seq", 1)
    v1 = shifted(values[0], 1)
    grads = [grad]
    for d in range(1, batch):
        low = d & -d
        source = out_grad[0] if d == 1 else out_grad[0] if d == low else grads[d ^ low]
        grads.append(swapped(source, "batch", low))
    attention2, slope2 = call(
        functools.partial(far_kernel, 2), [near, wide], scalars, (after(q, grads[2]), k2), block_flops
    )
    q2 = shifted(after(q, grads[2]), -2)
    passed_q = jnp.where(even, q2, q)
    q1 = swapped(passed_q, "seq", 1)
    attention1, slope1 = call(
        functools.partial(far_kernel, 1), [near, wide], scalars, (after(q, v1), k1), block_flops
    )
    hidden, normed, inv_std, *slices = call(
        functools.partial(forward_kernel, batch),
        [near, wide, kept((rows, 128), F32)] + [kept((rows, part), BF16)] * batch,
        (place,),
        (attention1, attention2, v1, v2, after(mixed_own, grads[1]), gate),
        block_flops,
        [pltpu.VMEM((rows, width), F32)],
    )
    hiddens = [slices[0]] + [swapped(slices[d], "batch", d) for d in range(1, batch)]
    grad_gates, grad_mix = call(
        mix_kernel, [full, near], (), (grad_hidden, gate, normed, inv_std), block_flops // 4
    )
    g2 = shifted(grad_mix, -2)
    g2_late = g2

    corners = 4
    direct = seq == 2 * corners
    rows_w = part // corners if direct else part
    share = kept((rows_w, width), BF16)
    scale = (rows * seq * batch) ** (-0.5)
    own, *sends = call(
        functools.partial(weight_kernel, batch),
        [kept((rows_w, width), F32)] + [share] * (corners - 1 if direct else 0),
        (place,),
        (*hiddens, *grads),
        proj_flops,
        [pltpu.VMEM((part, width), F32)],
    )
    output, grad_queries = call(
        query_kernel,
        [full, full],
        (),
        (k, k1, k2, v, v1, v2, slope0, slope1, slope2, grad_mix, after(hidden, own), w),
        proj_flops + 6 * block_flops,
    )
    if direct:
        got = [swapped(s, "seq", e + 1) for e, s in enumerate(sends)]
        (mine,) = call(corner_kernel, [share], (), (after(own, output), *got), own.size * 4)
        other = swapped(mine, "seq", corners)
        g2_late = after(g2, mine)
    else:
        mine = own
    keys_part, values_part = call(
        key_kernel,
        [wide, wide],
        scalars,
        (k, after(v, mine), q, q2, grad_mix, g2),
        8 * block_flops,
    )
    g1 = swapped(jnp.where(even, g2_late, grad_mix), "seq", 1)
    if direct:
        (both,) = call(
            functools.partial(pair_kernel, scale),
            [share],
            (),
            (after(mine, keys_part), other),
            own.size * 2,
        )
    else:
        both = own
    grad_keys, grad_values = call(
        key_end_kernel,
        [full, full],
        scalars,
        (k, after(v, both), q1, g1, keys_part, values_part),
        4 * block_flops,
    )
    if direct:
        shares = [after(both, grad_keys)] + [swapped(both, "seq", e) for e in range(1, corners)]
        (grad_weight,) = call(
            functools.partial(place_kernel, corners),
            [jax.ShapeDtypeStruct((part, width), F32)],
            (place,),
            shares,
            part * width,
            [pltpu.VMEM((corners, rows_w, width), F32), pltpu.SemaphoreType.DMA((corners,))],
            out_space=hbm,
        )
    else:
        grad_weight = lax.psum(own, "seq") * scale
    return (
        output[None],
        grad_queries[None],
        grad_keys[None],
        grad_values[None],
        grad_gates[None],
        grad_weight,
    )


def solution(mesh):
    token = P("batch", "seq", None)
    return jax.shard_map(
        on_device,
        mesh=mesh,
        in_specs=(token, token, token, token, token, P(), P("batch", None)),
        out_specs=(token, token, token, token, token, P("batch", None)),
        check_vma=False,
    )
```
